32 devices in a mesh: grp: 2 (over x), row: 16 (over z, y, core).
Axes of the slice: x: 2, y: 2, z: 4, core: 2. Of those that a mesh axis runs over, the one named last changes fastest.
Arguments:
- object_slices: float32 [2, 2, 2048, 2048], P(None, None, ('grp', 'row')), parts along dimension 2
- probe_modes: float32 [8, 2, 128, 128], P('grp'), parts along dimension 0, may hold values from -2.1 to 2.1
- propagator_phase: float32 [128, 128], replicated, may hold values from -3.140625 to 3.140625
- measured: float32 [256, 128, 128], P(('grp', 'row')), parts along dimension 0, may hold values from 0.25 to 4
- offsets: int32 [256, 2], P(('grp', 'row')), parts along dimension 0, may hold values from 0 to 1920, as said below
- counts: int32 [32], P(('grp', 'row')), parts along dimension 0, may hold values from 1 to 8, 72 in all
Outputs:
- object_grad: float32 [2, 2, 2048, 2048], P(None, None, ('grp', 'row')), parts along dimension 2
- probe_step: float32 [8, 2, 128, 128], P('grp'), parts along dimension 0
The draws below stay inside these ranges and needn't reach their ends.
There are 2 independent parts, one for each index of `grp`. The reference program is written for one: setup_inputs(seed, part) draws one part's arguments, and reference() takes and returns one part's arrays. A program takes and returns all parts, laid end to end along the dimension named above; an argument that names none is the same for every part. Nothing has to cross between parts.
Inputs may be any that keep to these rules, and one draw needn't show every extreme that they name: The slots of device d (slots d * 8 to d * 8 + 7) have row offsets d * 64 to d * 64 + 63 and column offsets 0 to 1920. `counts`: counts sum to 72; some device holds 8.
All inputs are finite; a program needn't handle non-finite values.
Results may differ from the reference program's by a relative error of at most 0.0003.
Values sent between devices are 32-bit elements; how exact they have to be, the bound alone decides.
No kernel may reach another device: no remote copies, remote signals or barrier semaphores. Data moves between devices by JAX's collectives and lax.ppermute only.
A program may use at most 64 MiB of HBM per device.

```python
import math
import jax
import jax.numpy as jnp
import numpy as np
from jax import lax

PW = 128
MODES = 4
SLICES = 2
P_CAP = 8
NXO = 2048
TR = 64
NY = 1024
SLOTS = 128
LIVE = 72
N_ROW = 16


def draw_object_slices(key, part):
    key = jax.random.fold_in(key, 5)
    base_key, row_key, col_key = jax.random.split(key, 3)
    values_drawn = jax.random.normal(base_key, (SLICES, 2, NY, NXO), jnp.float32) * 0.7
    spread = 0.35
    row_scale = jnp.exp(jax.random.uniform(row_key, (SLICES, 1, NY, 1), jnp.float32, -spread, spread))
    col_scale = jnp.exp(jax.random.uniform(col_key, (SLICES, 1, 1, NXO), jnp.float32, -spread, spread))
    return values_drawn * row_scale * col_scale


def draw_offsets(key, part):
    key = jax.random.fold_in(key, 11)
    row_key, col_key = jax.random.split(key)
    slot_index = jnp.arange(SLOTS, dtype=jnp.int32)
    inner_row = jax.random.randint(row_key, (SLOTS,), 0, TR, dtype=jnp.int32)
    column = jax.random.randint(col_key, (SLOTS,), 0, NXO - PW + 1, dtype=jnp.int32)
    first_slot = slot_index % P_CAP == 0
    second = slot_index % P_CAP == 1
    inner_row = jnp.where(first_slot, TR - 1, inner_row)
    column = jnp.where(first_slot, NXO - PW, jnp.where(second, 0, column))
    return jnp.stack([slot_index // P_CAP * TR + inner_row, column], axis=1).astype(jnp.int32)


def block_levels(key, shape, pieces, low, largest):
    def one(axis_at, shards_of):
        heights = jax.random.uniform(jax.random.fold_in(jax.random.fold_in(key, 6), axis_at), (shards_of,), jnp.float32, low / len(pieces), largest / len(pieces))
        return jnp.repeat(jnp.exp(heights), shape[axis_at] // shards_of).reshape((-1,) + (1,) * (len(shape) - axis_at - 1))

    level = one(*pieces[0])
    for cut in pieces[1:]:
        level = level * one(*cut)
    return level


def split_up(amount, total, bound, slope):
    portions = [(1 << 20) // math.isqrt(rank ** slope) + 1 for rank in range(2, amount + 1)]
    rest, holding = total - bound - (amount - 1), [1] * (amount - 1)
    while rest > 0:
        movable = [i for i in range(amount - 1) if holding[i] < bound]
        mass, left = sum([portions[i] for i in movable]), rest
        for i in movable:
            more = min(bound - holding[i], max(1, left * portions[i] // mass), rest)
            holding[i] = holding[i] + more
            rest = rest - more
    return np.array([bound] + holding)


def uneven(rng, number_of, total, bound, slope):
    if number_of == 2:
        one = jax.random.randint(rng, (), max(1, total - bound), min(bound, total - 1) + 1)
        return jnp.stack([one, total - one])
    lengths = jnp.asarray(split_up(number_of, total, bound, slope), jnp.int32)
    pairs = (number_of - 1) // 2
    giver, receiver = lengths[1:1 + 2 * pairs:2], lengths[2:2 + 2 * pairs:2]
    room = jnp.minimum(giver - 1, bound - receiver)
    shifted = jax.random.randint(jax.random.fold_in(rng, 1), (pairs,), 0, 1 << 20) % (room + 1)
    lengths = lengths.at[1:1 + 2 * pairs:2].set(giver - shifted).at[2:2 + 2 * pairs:2].set(receiver + shifted)
    return lengths[jax.random.permutation(jax.random.fold_in(rng, 2), number_of)]


def normal_values(own_key, extent, scale, bound, held_as=jnp.bfloat16):
    array = scale * jax.random.normal(own_key, extent, jnp.float32)
    return jnp.clip(array, min=-bound, max=bound).astype(held_as)


def setup_inputs(seed: int = 0, part: int = 0) -> dict:
    key_of = jax.random.split(jax.random.key(seed), 7)
    part_splits = jax.random.split(jax.random.fold_in(key_of[6], part), 7)
    object_slices = draw_object_slices(jax.random.fold_in(jax.random.fold_in(key_of[6], part), 71), part)
    probe_modes = normal_values(part_splits[1], (MODES, 2, PW, PW), 0.35, 2.1, jnp.float32)
    propagator_phase = jnp.clip(jax.random.uniform(key_of[2], (PW, PW), jnp.float32, -3.140625, 3.140625), -3.140625, 3.140625)
    measured = jnp.clip(jnp.exp(math.log(4.0) - 2.7725887 * jax.random.uniform(part_splits[3], (SLOTS, PW, PW), jnp.float32) ** block_levels(part_splits[3], (SLOTS, PW, PW), ((0, 16),), -0.2, 0.2)), 0.25, 4.0)
    offsets = draw_offsets(jax.random.fold_in(jax.random.fold_in(key_of[6], part), 71), part)
    counts = uneven(part_splits[5], N_ROW, LIVE, P_CAP, 2).astype(jnp.int32)
    return dict(object_slices=object_slices, probe_modes=probe_modes, propagator_phase=propagator_phase, measured=measured, offsets=offsets, counts=counts)


def contract(form, first, second):
    return jnp.einsum(form, first, second, precision=lax.Precision.HIGHEST)

def fourier_tables(pixels):
    indices = jnp.arange(pixels, dtype=jnp.int32)
    phases = indices[:, None] * indices[None, :] % pixels
    angles = phases.astype(jnp.float32) * (2.0 * math.pi / pixels)
    scale_factor = 1.0 / math.sqrt(pixels)
    return (jnp.cos(angles) * scale_factor, -jnp.sin(angles) * scale_factor)

def transform(table_re, table_im, real_part, imag_part):
    left_re = contract('ij,mjk->mik', table_re, real_part) - contract('ij,mjk->mik', table_im, imag_part)
    left_im = contract('ij,mjk->mik', table_re, imag_part) + contract('ij,mjk->mik', table_im, real_part)
    right_re = contract('mij,jk->mik', left_re, table_re) - contract('mij,jk->mik', left_im, table_im)
    right_im = contract('mij,jk->mik', left_re, table_im) + contract('mij,jk->mik', left_im, table_re)
    return (right_re, right_im)

def propagate(table_re, table_im, wave_re, wave_im, prop_re, prop_im):
    far_re, far_im = transform(table_re, table_im, wave_re, wave_im)
    turned_re = far_re * prop_re - far_im * prop_im
    turned_im = far_re * prop_im + far_im * prop_re
    return transform(table_re, -table_im, turned_re, turned_im)

def patch_loss(patches, probe_modes, target, table_re, table_im, prop_re, prop_im):
    wave_re = probe_modes[:, 0]
    wave_im = probe_modes[:, 1]
    for layer_index in range(patches.shape[0]):
        if layer_index > 0:
            wave_re, wave_im = propagate(table_re, table_im, wave_re, wave_im, prop_re, prop_im)
        trans_re = patches[layer_index, 0]
        trans_im = patches[layer_index, 1]
        wave_re, wave_im = (wave_re * trans_re - wave_im * trans_im, wave_re * trans_im + wave_im * trans_re)
    far_re, far_im = transform(table_re, table_im, wave_re, wave_im)
    intensity = lax.optimization_barrier(jnp.sum(far_re * far_re + far_im * far_im, axis=0))
    misfit = intensity - target
    return 0.5 * jnp.sum(misfit * misfit)

def reference(object_slices, probe_modes, propagator_phase, measured, offsets, counts):
    table_re, table_im = fourier_tables(PW)
    prop_re = jnp.cos(propagator_phase)
    prop_im = jnp.sin(propagator_phase)
    padded = jnp.concatenate([object_slices, object_slices[:, :, :PW]], axis=2)
    slot_index = jnp.arange(offsets.shape[0], dtype=jnp.int32)
    live = (slot_index % P_CAP < counts[slot_index // P_CAP]).astype(jnp.float32)
    anchor = jnp.zeros((), jnp.int32)

    def visit_slot(running, record):
        grad_field, probe_grad, illumination = running
        row_start, col_start, live_weight, target = record
        corner = (anchor, anchor, row_start.astype(jnp.int32), col_start.astype(jnp.int32))
        patches = lax.dynamic_slice(padded, corner, (SLICES, 2, PW, PW))

        def local_loss(patch_part, probe_part):
            return patch_loss(patch_part, probe_part, target, table_re, table_im, prop_re, prop_im)
        misfit_sum, pullback = jax.vjp(local_loss, patches, probe_modes)
        patch_grad, probe_part = pullback(live_weight)
        current = lax.dynamic_slice(grad_field, corner, (SLICES, 2, PW, PW))
        grad_field = lax.dynamic_update_slice(grad_field, current + patch_grad, corner)
        illumination = illumination + live_weight * (patches[0, 0] * patches[0, 0] + patches[0, 1] * patches[0, 1])
        return ((grad_field, probe_grad + probe_part, illumination), None)
    start = (jnp.zeros(padded.shape, jnp.float32), jnp.zeros(probe_modes.shape, jnp.float32), jnp.zeros((PW, PW), jnp.float32))
    records = (offsets[:, 0], offsets[:, 1], live, measured)
    (grad_field, probe_grad, illumination), _ = lax.scan(visit_slot, start, records)
    object_grad = grad_field[:, :, :NY]
    object_grad = object_grad.at[:, :, :PW].add(grad_field[:, :, NY:])
    probe_step = probe_grad / (illumination + 1.0)
    return (object_grad, probe_step)
```

```python
import functools

import jax
import jax.numpy as jnp
import numpy as np
from jax import lax
from jax.experimental import pallas as pl
from jax.experimental.pallas import tpu as pltpu
from jax.sharding import PartitionSpec as P

CHUNKS = (2, 4, 2)
VMEM_LIMIT = 48 * 1024 * 1024
F32 = jnp.float32
BF16 = jnp.bfloat16


def shifted(array, axis, by):
    peers = lax.axis_size(axis)
    return lax.ppermute(array, axis, [(i, (i + by) % peers) for i in range(peers)])


def fourier_blocks(pixels):
    indices = np.arange(pixels)
    angles = 2.0 * np.pi * (indices[:, None] * indices[None, :] % pixels) / pixels
    re = np.cos(angles) / np.sqrt(pixels)
    im = -np.sin(angles) / np.sqrt(pixels)
    left = np.block([[re, -im], [im, re]]).astype(np.float32)
    high = left.astype(BF16)
    low = (left - high.astype(np.float32)).astype(BF16)
    from_left = np.concatenate([high, low, high], axis=1)
    from_right = np.concatenate([high.T, high.T, low.T], axis=0)
    conj_left = np.concatenate([high.T, low.T, high.T], axis=1)
    conj_right = np.concatenate([high, high, low], axis=0)
    return from_left, from_right, conj_left, conj_right


def pieces(array):
    high = array.astype(BF16)
    return high, (array - high.astype(F32)).astype(BF16)


def transform(left, right, waves):
    stacked = jnp.concatenate([jnp.concatenate(wave, axis=0) for wave in waves], axis=1)
    high, low = pieces(stacked)
    half = jnp.dot(left[...], jnp.concatenate([high, high, low], axis=0), preferred_element_type=F32)
    pixels = half.shape[0] // 2
    turned = jnp.concatenate(
        [
            jnp.concatenate([half[:pixels, at : at + pixels], half[pixels:, at : at + pixels]], axis=1)
            for at in (0, pixels)
        ],
        axis=0,
    )
    high, low = pieces(turned)
    whole = jnp.dot(jnp.concatenate([high, low, high], axis=1), right[...], preferred_element_type=F32)
    return [
        (whole[at : at + pixels, :pixels], whole[at : at + pixels, pixels:]) for at in (0, pixels)
    ]


def times(one, two):
    return one[0] * two[0] - one[1] * two[1], one[0] * two[1] + one[1] * two[0]


def conj_times(one, two):
    return one[0] * two[0] + one[1] * two[1], one[0] * two[1] - one[1] * two[0]


def place(column, columns, pixels):
    base = jnp.minimum(column // pixels * pixels, columns - 2 * pixels)
    return pl.multiple_of(base, pixels), column - base


def cut(tile, column, pixels):
    base, shift = place(column, tile.shape[-1], pixels)
    rows = tile.shape[1]
    wide = tile[:, :, pl.ds(base, 2 * pixels)].reshape(-1, 2 * pixels)
    turned = pltpu.roll(wide, 2 * pixels - shift, 1)
    return turned[:, :pixels].reshape(-1, rows, pixels)


def cut_kernel(pixels, meta, tile, *outs):
    slot = 0
    for out in outs:
        for at in range(out.shape[0]):
            out[at] = cut(tile, meta[slot, 1], pixels)
            slot += 1


def add_kernel(pixels, metas, meta_own, meta_mid, meta_far, *refs):
    refs = list(refs)
    out = refs.pop()
    out[...] = jnp.zeros_like(out)
    count = len(refs) // 3
    for meta, group in (
        (meta_mid, refs[:count]),
        (meta_own, refs[count : 2 * count]),
        (meta_far, refs[2 * count :]),
    ):
        first = 0
        for parts in group:
            size = parts.shape[0]

            def add(at, carry, parts=parts, first=first, meta=meta):
                base, shift = place(meta[first + at, 1], out.shape[-1], pixels)
                part = parts[at]
                wide = jnp.concatenate([part, jnp.zeros_like(part)], axis=2)
                turned = pltpu.roll(wide.reshape(-1, 2 * pixels), shift, 1).reshape(wide.shape)
                out[:, :, pl.ds(base, 2 * pixels)] += turned
                return carry

            lax.fori_loop(0, jnp.clip(meta[0, 2] - first, 0, size), add, 0)
            first += size


def slot_kernel(
    first, meta, tile, above, below, target, probe, prop, left, right, conj_left, conj_right, so_far,
    out_above, out_mid, out_below, total, window, patch, grads, exit_wave, far,
):
    size = above.shape[0]
    modes, _, pixels, _ = probe.shape
    rows = above.shape[2]
    total[...] = so_far[...]

    def visit(at, carry):
        row = lax.rem(meta[first + at, 0], rows)
        window[:, :rows] = above[at]
        window[:, rows : 2 * rows] = cut(tile, meta[first + at, 1], pixels)
        window[:, 2 * rows :] = below[at]
        patch[...] = window[:, pl.ds(row, pixels), :]
        total[2 * modes] += patch[0] * patch[0] + patch[1] * patch[1]
        intensity = jnp.zeros((pixels, pixels), F32)
        for pair in range(0, modes, 2):
            both = (pair, pair + 1)
            waves = [times((probe[m, 0], probe[m, 1]), (patch[0], patch[1])) for m in both]
            waves = transform(left, right, waves)
            waves = [times((prop[0], prop[1]), wave) for wave in waves]
            waves = transform(conj_left, conj_right, waves)
            for m, wave in zip(both, waves):
                exit_wave[m, 0], exit_wave[m, 1] = wave
            waves = [times(wave, (patch[2], patch[3])) for wave in waves]
            waves = transform(left, right, waves)
            for m, wave in zip(both, waves):
                far[m, 0], far[m, 1] = wave
                intensity = intensity + wave[0] * wave[0] + wave[1] * wave[1]
        misfit = 2.0 * (intensity - target[at])
        grads[...] = jnp.zeros_like(grads)
        for pair in range(0, modes, 2):
            both = (pair, pair + 1)
            waves = [(misfit * far[m, 0], misfit * far[m, 1]) for m in both]
            waves = transform(conj_left, conj_right, waves)
            for m, wave in zip(both, waves):
                re, im = conj_times((exit_wave[m, 0], exit_wave[m, 1]), wave)
                grads[2] += re
                grads[3] += im
            waves = [conj_times((patch[2], patch[3]), wave) for wave in waves]
            waves = transform(left, right, waves)
            waves = [conj_times((prop[0], prop[1]), wave) for wave in waves]
            waves = transform(conj_left, conj_right, waves)
            for m, wave in zip(both, waves):
                re, im = conj_times((patch[0], patch[1]), wave)
                total[2 * m] += re
                total[2 * m + 1] += im
                re, im = conj_times((probe[m, 0], probe[m, 1]), wave)
                grads[0] += re
                grads[1] += im
        window[...] = jnp.zeros_like(window)
        window[:, pl.ds(row, pixels), :] = grads[...]
        out_above[at] = window[:, :rows]
        out_mid[at] = window[:, rows : 2 * rows]
        out_below[at] = window[:, 2 * rows :]
        return carry

    lax.fori_loop(0, jnp.clip(meta[0, 2] - first, 0, size), visit, 0)


def in_smem():
    return pl.BlockSpec(memory_space=pltpu.SMEM)


def in_vmem():
    return pl.BlockSpec(memory_space=pltpu.VMEM)


def local(object_slices, probe_modes, propagator_phase, measured, offsets, counts):
    slices, _, tile_rows, columns = object_slices.shape
    modes, _, pixels, _ = probe_modes.shape
    slots = measured.shape[0]
    planes = 2 * slices
    peers = lax.axis_size("row")
    params = pltpu.CompilerParams(vmem_limit_bytes=VMEM_LIMIT)
    tile = object_slices.reshape(planes, tile_rows, columns)
    starts = [sum(CHUNKS[:i]) for i in range(len(CHUNKS))]

    meta_own = jnp.concatenate([offsets, jnp.broadcast_to(counts, (slots, 1))], axis=1)
    meta_mid = shifted(meta_own, "row", 1)
    meta_far = shifted(meta_own, "row", 2)

    def strips(meta):
        return pl.pallas_call(
            functools.partial(cut_kernel, pixels),
            out_shape=[jax.ShapeDtypeStruct((size, planes, tile_rows, pixels), F32) for size in CHUNKS],
            in_specs=[in_smem(), in_vmem()],
            out_specs=[in_vmem()] * len(CHUNKS),
            compiler_params=params,
            cost_estimate=pl.CostEstimate(flops=0, bytes_accessed=4 << 20, transcendentals=0),
        )(meta, tile)

    above = [shifted(part, "row", 1) for part in strips(meta_own)]
    below = [shifted(part, "row", -1) for part in strips(meta_far)]
    targets = [
        shifted(measured[at : at + size], "row", 1) for at, size in zip(starts, CHUNKS)
    ]
    prop = jnp.stack([jnp.cos(propagator_phase), jnp.sin(propagator_phase)])
    tables = [jnp.asarray(table) for table in fourier_blocks(pixels)]

    total = jnp.zeros((2 * modes + 1, pixels, pixels), F32)
    mid, back_own, back_far = [], [], []
    for index, (first, size) in enumerate(zip(starts, CHUNKS)):
        strip = jax.ShapeDtypeStruct((size, planes, tile_rows, pixels), F32)
        field = pltpu.VMEM((planes, pixels, pixels), F32)
        to_above, to_mid, to_below, total = pl.pallas_call(
            functools.partial(slot_kernel, first),
            out_shape=[strip, strip, strip, jax.ShapeDtypeStruct(total.shape, F32)],
            in_specs=[in_smem()] + [in_vmem()] * 11,
            out_specs=[in_vmem()] * 4,
            scratch_shapes=[
                pltpu.VMEM((planes, 3 * tile_rows, pixels), F32),
                field,
                field,
                pltpu.VMEM((modes, 2, pixels, pixels), F32),
                pltpu.VMEM((modes, 2, pixels, pixels), F32),
            ],
            compiler_params=params,
            cost_estimate=pl.CostEstimate(
                flops=size * 6 * modes * 3 * 16 * pixels**3, bytes_accessed=8 << 20, transcendentals=0
            ),
        )(meta_mid, tile, above[index], below[index], targets[index], probe_modes, prop, *tables, total)
        mid.append(to_mid)
        back_own.append(shifted(to_above, "row", -1))
        back_far.append(shifted(to_below, "row", 1))

    object_grad = pl.pallas_call(
        functools.partial(add_kernel, pixels, 3),
        out_shape=jax.ShapeDtypeStruct(tile.shape, F32),
        in_specs=[in_smem()] * 3 + [in_vmem()] * (3 * len(CHUNKS)),
        out_specs=in_vmem(),
        compiler_params=params,
        cost_estimate=pl.CostEstimate(flops=0, bytes_accessed=5 << 20, transcendentals=0),
    )(meta_own, meta_mid, meta_far, *mid, *back_own, *back_far).reshape(object_slices.shape)

    share = pixels // peers
    sent = total.reshape(2 * modes + 1, peers, share, pixels).swapaxes(0, 1)
    summed = lax.all_to_all(sent, "row", 0, 0).sum(axis=0)
    step = summed[: 2 * modes] / (summed[2 * modes :] + 1.0)
    spread = lax.all_to_all(jnp.broadcast_to(step, (peers,) + step.shape), "row", 0, 0)
    probe_step = spread.swapaxes(0, 1).reshape(probe_modes.shape)
    return (object_grad, probe_step)


def solution(mesh):
    in_specs = (
        P(None, None, ("grp", "row"), None),
        P("grp", None, None, None),
        P(),
        P(("grp", "row"), None, None),
        P(("grp", "row"), None),
        P(("grp", "row")),
    )
    out_specs = (P(None, None, ("grp", "row"), None), P("grp", None, None, None))
    return jax.shard_map(local, mesh=mesh, in_specs=in_specs, out_specs=out_specs, check_vma=False)
```

```python
import functools

import jax
import jax.numpy as jnp
import numpy as np
from jax import lax
from jax.experimental import pallas as pl
from jax.experimental.pallas import tpu as pltpu
from jax.sharding import PartitionSpec as P

CHUNKS = (2, 4, 2)
BATCH = 2
VMEM_LIMIT = 48 * 1024 * 1024
F32 = jnp.float32
BF16 = jnp.bfloat16


def shifted(array, axis, by):
    peers = lax.axis_size(axis)
    return lax.ppermute(array, axis, [(i, (i + by) % peers) for i in range(peers)])


def fourier_blocks(pixels):
    indices = np.arange(pixels)
    angles = 2.0 * np.pi * (indices[:, None] * indices[None, :] % pixels) / pixels
    re = np.cos(angles) / np.sqrt(pixels)
    im = -np.sin(angles) / np.sqrt(pixels)
    left = np.block([[re, -im], [im, re]]).astype(np.float32)
    high = left.astype(BF16)
    low = (left - high.astype(np.float32)).astype(BF16)
    from_left = np.concatenate([high, low, high], axis=1)
    from_right = np.concatenate([high.T, high.T, low.T], axis=0)
    conj_left = np.concatenate([high.T, low.T, high.T], axis=1)
    conj_right = np.concatenate([high, high, low], axis=0)
    return from_left, from_right, conj_left, conj_right


def pieces(array):
    high = array.astype(BF16)
    return high, (array - high.astype(F32)).astype(BF16)


def transform(left, right, waves):
    stacked = jnp.concatenate([jnp.concatenate(wave, axis=0) for wave in waves], axis=1)
    high, low = pieces(stacked)
    half = jnp.dot(left[...], jnp.concatenate([high, high, low], axis=0), preferred_element_type=F32)
    pixels = half.shape[0] // 2
    places = [i * pixels for i in range(len(waves))]
    turned = jnp.concatenate(
        [
            jnp.concatenate([half[:pixels, at : at + pixels], half[pixels:, at : at + pixels]], axis=1)
            for at in places
        ],
        axis=0,
    )
    high, low = pieces(turned)
    whole = jnp.dot(jnp.concatenate([high, low, high], axis=1), right[...], preferred_element_type=F32)
    return [(whole[at : at + pixels, :pixels], whole[at : at + pixels, pixels:]) for at in places]


def times(one, two):
    return one[0] * two[0] - one[1] * two[1], one[0] * two[1] + one[1] * two[0]


def conj_times(one, two):
    return one[0] * two[0] + one[1] * two[1], one[0] * two[1] - one[1] * two[0]


def place(column, columns, pixels):
    base = jnp.minimum(column // pixels * pixels, columns - 2 * pixels)
    return pl.multiple_of(base, pixels), column - base


def cut(tile, column, pixels):
    base, shift = place(column, tile.shape[-1], pixels)
    rows = tile.shape[1]
    wide = tile[:, :, pl.ds(base, 2 * pixels)].reshape(-1, 2 * pixels)
    turned = pltpu.roll(wide, 2 * pixels - shift, 1)
    return turned[:, :pixels].reshape(-1, rows, pixels)


def cut_kernel(pixels, meta, tile, *outs):
    slot = 0
    for out in outs:
        for at in range(out.shape[0]):
            out[at] = cut(tile, meta[slot, 1], pixels)
            slot += 1


def add_kernel(pixels, metas, meta_own, meta_mid, meta_far, *refs):
    refs = list(refs)
    out = refs.pop()
    out[...] = jnp.zeros_like(out)
    count = len(refs) // 3
    for meta, group in (
        (meta_mid, refs[:count]),
        (meta_own, refs[count : 2 * count]),
        (meta_far, refs[2 * count :]),
    ):
        first = 0
        for parts in group:
            size = parts.shape[0]

            def add(at, carry, parts=parts, first=first, meta=meta):
                base, shift = place(meta[first + at, 1], out.shape[-1], pixels)
                part = parts[at]
                wide = jnp.concatenate([part, jnp.zeros_like(part)], axis=2)
                turned = pltpu.roll(wide.reshape(-1, 2 * pixels), shift, 1).reshape(wide.shape)
                out[:, :, pl.ds(base, 2 * pixels)] += turned
                return carry

            lax.fori_loop(0, jnp.clip(meta[0, 2] - first, 0, size), add, 0)
            first += size


def slot_kernel(
    first, meta, tile, above, below, target, probe, prop, left, right, conj_left, conj_right, so_far,
    out_above, out_mid, out_below, total, window, patch, grads, exit_wave, far,
):
    size = above.shape[0]
    modes, _, pixels, _ = probe.shape
    rows = above.shape[2]
    total[...] = so_far[...]
    held = [(s, m) for s in range(BATCH) for m in range(modes)]
    live_slots = jnp.clip(meta[0, 2] - first, 0, size)

    def visit(step, carry):
        slots = [step * BATCH + s for s in range(BATCH)]
        starts = [lax.rem(meta[first + at, 0], rows) for at in slots]
        live = [jnp.where(at < live_slots, 1.0, 0.0).astype(F32) for at in slots]
        for s, at in enumerate(slots):
            window[:, :rows] = above[at]
            window[:, rows : 2 * rows] = cut(tile, meta[first + at, 1], pixels)
            window[:, 2 * rows :] = below[at]
            patch[s] = window[:, pl.ds(starts[s], pixels), :]
            total[2 * modes] += live[s] * (patch[s, 0] * patch[s, 0] + patch[s, 1] * patch[s, 1])
        waves = [times((probe[m, 0], probe[m, 1]), (patch[s, 0], patch[s, 1])) for s, m in held]
        waves = transform(left, right, waves)
        waves = [times((prop[0], prop[1]), wave) for wave in waves]
        waves = transform(conj_left, conj_right, waves)
        for (s, m), wave in zip(held, waves):
            exit_wave[s, m, 0], exit_wave[s, m, 1] = wave
        waves = [times(wave, (patch[s, 2], patch[s, 3])) for (s, m), wave in zip(held, waves)]
        waves = transform(left, right, waves)
        intensity = [jnp.zeros((pixels, pixels), F32)] * BATCH
        for (s, m), wave in zip(held, waves):
            far[s, m, 0], far[s, m, 1] = wave
            intensity[s] = intensity[s] + wave[0] * wave[0] + wave[1] * wave[1]
        misfit = [2.0 * live[s] * (intensity[s] - target[at]) for s, at in enumerate(slots)]
        waves = [(misfit[s] * far[s, m, 0], misfit[s] * far[s, m, 1]) for s, m in held]
        waves = transform(conj_left, conj_right, waves)
        grads[...] = jnp.zeros_like(grads)
        for (s, m), wave in zip(held, waves):
            re, im = conj_times((exit_wave[s, m, 0], exit_wave[s, m, 1]), wave)
            grads[s, 2] += re
            grads[s, 3] += im
        waves = [conj_times((patch[s, 2], patch[s, 3]), wave) for (s, m), wave in zip(held, waves)]
        waves = transform(left, right, waves)
        waves = [conj_times((prop[0], prop[1]), wave) for wave in waves]
        waves = transform(conj_left, conj_right, waves)
        for (s, m), wave in zip(held, waves):
            re, im = conj_times((patch[s, 0], patch[s, 1]), wave)
            total[2 * m] += re
            total[2 * m + 1] += im
            re, im = conj_times((probe[m, 0], probe[m, 1]), wave)
            grads[s, 0] += re
            grads[s, 1] += im
        for s, at in enumerate(slots):
            window[...] = jnp.zeros_like(window)
            window[:, pl.ds(starts[s], pixels), :] = grads[s]
            out_above[at] = window[:, :rows]
            out_mid[at] = window[:, rows : 2 * rows]
            out_below[at] = window[:, 2 * rows :]
        return carry

    lax.fori_loop(0, (live_slots + BATCH - 1) // BATCH, visit, 0)


def in_smem():
    return pl.BlockSpec(memory_space=pltpu.SMEM)


def in_vmem():
    return pl.BlockSpec(memory_space=pltpu.VMEM)


def local(object_slices, probe_modes, propagator_phase, measured, offsets, counts):
    slices, _, tile_rows, columns = object_slices.shape
    modes, _, pixels, _ = probe_modes.shape
    slots = measured.shape[0]
    planes = 2 * slices
    peers = lax.axis_size("row")
    params = pltpu.CompilerParams(vmem_limit_bytes=VMEM_LIMIT)
    tile = object_slices.reshape(planes, tile_rows, columns)
    starts = [sum(CHUNKS[:i]) for i in range(len(CHUNKS))]

    meta_own = jnp.concatenate([offsets, jnp.broadcast_to(counts, (slots, 1))], axis=1)
    meta_mid = shifted(meta_own, "row", 1)
    meta_far = shifted(meta_own, "row", 2)

    def strips(meta):
        return pl.pallas_call(
            functools.partial(cut_kernel, pixels),
            out_shape=[jax.ShapeDtypeStruct((size, planes, tile_rows, pixels), F32) for size in CHUNKS],
            in_specs=[in_smem(), in_vmem()],
            out_specs=[in_vmem()] * len(CHUNKS),
            compiler_params=params,
            cost_estimate=pl.CostEstimate(flops=0, bytes_accessed=4 << 20, transcendentals=0),
        )(meta, tile)

    above = [shifted(part, "row", 1) for part in strips(meta_own)]
    below = [shifted(part, "row", -1) for part in strips(meta_far)]
    targets = [
        shifted(measured[at : at + size], "row", 1) for at, size in zip(starts, CHUNKS)
    ]
    prop = jnp.stack([jnp.cos(propagator_phase), jnp.sin(propagator_phase)])
    tables = [jnp.asarray(table) for table in fourier_blocks(pixels)]

    total = jnp.zeros((2 * modes + 1, pixels, pixels), F32)
    mid, back_own, back_far = [], [], []
    for index, (first, size) in enumerate(zip(starts, CHUNKS)):
        strip = jax.ShapeDtypeStruct((size, planes, tile_rows, pixels), F32)
        field = pltpu.VMEM((BATCH, planes, pixels, pixels), F32)
        kept = pltpu.VMEM((BATCH, modes, 2, pixels, pixels), F32)
        to_above, to_mid, to_below, total = pl.pallas_call(
            functools.partial(slot_kernel, first),
            out_shape=[strip, strip, strip, jax.ShapeDtypeStruct(total.shape, F32)],
            in_specs=[in_smem()] + [in_vmem()] * 11,
            out_specs=[in_vmem()] * 4,
            scratch_shapes=[
                pltpu.VMEM((planes, 3 * tile_rows, pixels), F32),
                field,
                field,
                kept,
                kept,
            ],
            compiler_params=params,
            cost_estimate=pl.CostEstimate(
                flops=size * 6 * modes * 3 * 16 * pixels**3, bytes_accessed=8 << 20, transcendentals=0
            ),
        )(meta_mid, tile, above[index], below[index], targets[index], probe_modes, prop, *tables, total)
        mid.append(to_mid)
        back_own.append(shifted(to_above, "row", -1))
        back_far.append(shifted(to_below, "row", 1))

    object_grad = pl.pallas_call(
        functools.partial(add_kernel, pixels, 3),
        out_shape=jax.ShapeDtypeStruct(tile.shape, F32),
        in_specs=[in_smem()] * 3 + [in_vmem()] * (3 * len(CHUNKS)),
        out_specs=in_vmem(),
        compiler_params=params,
        cost_estimate=pl.CostEstimate(flops=0, bytes_accessed=5 << 20, transcendentals=0),
    )(meta_own, meta_mid, meta_far, *mid, *back_own, *back_far).reshape(object_slices.shape)

    share = pixels // peers
    sent = total.reshape(2 * modes + 1, peers, share, pixels).swapaxes(0, 1)
    summed = lax.all_to_all(sent, "row", 0, 0).sum(axis=0)
    step = summed[: 2 * modes] / (summed[2 * modes :] + 1.0)
    spread = lax.all_to_all(jnp.broadcast_to(step, (peers,) + step.shape), "row", 0, 0)
    probe_step = spread.swapaxes(0, 1).reshape(probe_modes.shape)
    return (object_grad, probe_step)


def solution(mesh):
    in_specs = (
        P(None, None, ("grp", "row"), None),
        P("grp", None, None, None),
        P(),
        P(("grp", "row"), None, None),
        P(("grp", "row"), None),
        P(("grp", "row")),
    )
    out_specs = (P(None, None, ("grp", "row"), None), P("grp", None, None, None))
    return jax.shard_map(local, mesh=mesh, in_specs=in_specs, out_specs=out_specs, check_vma=False)
```

```python
import functools

import jax
import jax.numpy as jnp
import numpy as np
from jax import lax
from jax.experimental import pallas as pl
from jax.experimental.pallas import tpu as pltpu
from jax.sharding import PartitionSpec as P

CHUNKS = (2, 4, 2)
BATCH = 2
VMEM_LIMIT = 48 * 1024 * 1024
F32 = jnp.float32
BF16 = jnp.bfloat16


def shifted(array, axis, by):
    peers = lax.axis_size(axis)
    return lax.ppermute(array, axis, [(i, (i + by) % peers) for i in range(peers)])


def fourier_tables(pixels):
    indices = np.arange(pixels)
    angles = 2.0 * np.pi * (indices[:, None] * indices[None, :] % pixels) / pixels
    re = np.cos(angles) / np.sqrt(pixels)
    im = -np.sin(angles) / np.sqrt(pixels)
    left = np.block([[re, -im], [im, re]]).astype(np.float32)
    high = left.astype(BF16)
    low = (left - high.astype(np.float32)).astype(BF16)
    return np.stack([high, low, high.T, low.T])


def pieces(array):
    high = array.astype(BF16)
    return high, (array - high.astype(F32)).astype(BF16)


def transform(tables, conj, waves):
    at_left, at_right = (2, 0) if conj else (0, 2)
    left = jnp.concatenate([tables[at_left], tables[at_left + 1], tables[at_left]], axis=1)
    right = jnp.concatenate([tables[at_right], tables[at_right], tables[at_right + 1]], axis=0)
    stacked = jnp.concatenate([jnp.concatenate(wave, axis=0) for wave in waves], axis=1)
    high, low = pieces(stacked)
    half = jnp.dot(left, jnp.concatenate([high, high, low], axis=0), preferred_element_type=F32)
    pixels = half.shape[0] // 2
    places = [i * pixels for i in range(len(waves))]
    turned = jnp.concatenate(
        [
            jnp.concatenate([half[:pixels, at : at + pixels], half[pixels:, at : at + pixels]], axis=1)
            for at in places
        ],
        axis=0,
    )
    high, low = pieces(turned)
    whole = jnp.dot(jnp.concatenate([high, low, high], axis=1), right, preferred_element_type=F32)
    return [(whole[at : at + pixels, :pixels], whole[at : at + pixels, pixels:]) for at in places]


def times(one, two):
    return one[0] * two[0] - one[1] * two[1], one[0] * two[1] + one[1] * two[0]


def conj_times(one, two):
    return one[0] * two[0] + one[1] * two[1], one[0] * two[1] - one[1] * two[0]


def place(column, columns, pixels):
    base = jnp.minimum(column // pixels * pixels, columns - 2 * pixels)
    return pl.multiple_of(base, pixels), column - base


def cut(tile, column, pixels):
    base, shift = place(column, tile.shape[-1], pixels)
    rows = tile.shape[1]
    wide = tile[:, :, pl.ds(base, 2 * pixels)].reshape(-1, 2 * pixels)
    turned = pltpu.roll(wide, 2 * pixels - shift, 1)
    return turned[:, :pixels].reshape(-1, rows, pixels)


def cut_kernel(pixels, extra, meta, tile, *refs):
    if extra:
        measured, *outs = refs
    else:
        outs = refs
    planes, rows, _ = tile.shape
    slot = 0
    for out in outs:
        for at in range(out.shape[0]):
            out[at, :planes] = cut(tile, meta[slot, 1], pixels)
            if extra:
                out[at, planes:] = measured[slot].reshape(-1, rows, pixels)
            slot += 1


def add_kernel(pixels, meta_own, meta_mid, meta_far, *refs):
    refs = list(refs)
    out = refs.pop()
    out[...] = jnp.zeros_like(out)
    count = len(refs) // 3
    for meta, group in (
        (meta_mid, refs[:count]),
        (meta_own, refs[count : 2 * count]),
        (meta_far, refs[2 * count :]),
    ):
        first = 0
        for parts in group:
            size = parts.shape[0]

            def add(at, carry, parts=parts, first=first, meta=meta):
                base, shift = place(meta[first + at, 1], out.shape[-1], pixels)
                part = parts[at]
                wide = jnp.concatenate([part, jnp.zeros_like(part)], axis=2)
                turned = pltpu.roll(wide.reshape(-1, 2 * pixels), shift, 1).reshape(wide.shape)
                out[:, :, pl.ds(base, 2 * pixels)] += turned
                return carry

            lax.fori_loop(0, jnp.clip(meta[0, 2] - first, 0, size), add, 0)
            first += size


def slot_kernel(
    first, meta, tile, above, below, probe, prop, tables, so_far,
    out_above, out_mid, out_below, total, *refs,
):
    shares, (window, patch, grads, exit_wave, far) = refs[:-5], refs[-5:]
    size = above.shape[0]
    planes = tile.shape[0]
    modes, _, pixels, _ = probe.shape
    rows = above.shape[2]
    total[...] = so_far[...]
    held = [(s, m) for s in range(BATCH) for m in range(modes)]
    live_slots = jnp.clip(meta[0, 2] - first, 0, size)

    def visit(step, carry):
        slots = [step * BATCH + s for s in range(BATCH)]
        starts = [lax.rem(meta[first + at, 0], rows) for at in slots]
        live = [jnp.where(at < live_slots, 1.0, 0.0).astype(F32) for at in slots]
        for s, at in enumerate(slots):
            window[:, :rows] = above[at, :planes]
            window[:, rows : 2 * rows] = cut(tile, meta[first + at, 1], pixels)
            window[:, 2 * rows :] = below[at]
            patch[s] = window[:, pl.ds(starts[s], pixels), :]
            total[2 * modes] += live[s] * (patch[s, 0] * patch[s, 0] + patch[s, 1] * patch[s, 1])
        waves = [times((probe[m, 0], probe[m, 1]), (patch[s, 0], patch[s, 1])) for s, m in held]
        waves = transform(tables, False, waves)
        waves = [times((prop[0], prop[1]), wave) for wave in waves]
        waves = transform(tables, True, waves)
        for (s, m), wave in zip(held, waves):
            exit_wave[s, m, 0], exit_wave[s, m, 1] = wave
        waves = [times(wave, (patch[s, 2], patch[s, 3])) for (s, m), wave in zip(held, waves)]
        waves = transform(tables, False, waves)
        intensity = [jnp.zeros((pixels, pixels), F32)] * BATCH
        for (s, m), wave in zip(held, waves):
            far[s, m, 0], far[s, m, 1] = wave
            intensity[s] = intensity[s] + wave[0] * wave[0] + wave[1] * wave[1]
        misfit = [2.0 * live[s] * (intensity[s] - above[at, planes:].reshape(pixels, pixels)) for s, at in enumerate(slots)]
        waves = [(misfit[s] * far[s, m, 0], misfit[s] * far[s, m, 1]) for s, m in held]
        waves = transform(tables, True, waves)
        grads[...] = jnp.zeros_like(grads)
        for (s, m), wave in zip(held, waves):
            re, im = conj_times((exit_wave[s, m, 0], exit_wave[s, m, 1]), wave)
            grads[s, 2] += re
            grads[s, 3] += im
        waves = [conj_times((patch[s, 2], patch[s, 3]), wave) for (s, m), wave in zip(held, waves)]
        waves = transform(tables, False, waves)
        waves = [conj_times((prop[0], prop[1]), wave) for wave in waves]
        waves = transform(tables, True, waves)
        for (s, m), wave in zip(held, waves):
            re, im = conj_times((patch[s, 0], patch[s, 1]), wave)
            total[2 * m] += re
            total[2 * m + 1] += im
            re, im = conj_times((probe[m, 0], probe[m, 1]), wave)
            grads[s, 0] += re
            grads[s, 1] += im
        for s, at in enumerate(slots):
            window[...] = jnp.zeros_like(window)
            window[:, pl.ds(starts[s], pixels), :] = grads[s]
            out_above[at] = window[:, :rows]
            out_mid[at] = window[:, rows : 2 * rows]
            out_below[at] = window[:, 2 * rows :]
        return carry

    lax.fori_loop(0, (live_slots + BATCH - 1) // BATCH, visit, 0)

    if shares:
        own, other = shares
        chips, _, share, _ = own.shape
        core = lax.rem(meta[0, 0] // rows + 1, 2)
        for chip in range(chips):
            for plane in range(2 * modes + 1):
                own[chip, plane] = total[plane, pl.ds((2 * chip + core) * share, share)]
                other[chip, plane] = total[plane, pl.ds((2 * chip + 1 - core) * share, share)]


def step_kernel(parts, out):
    summed = parts[0]
    for at in range(1, parts.shape[0]):
        summed = summed + parts[at]
    step = summed[:-1] / (summed[-1:] + 1.0)
    for at in range(out.shape[0]):
        out[at] = step


def order_kernel(parts, out):
    share = parts.shape[2]
    for at in range(parts.shape[0]):
        out[:, at * share : (at + 1) * share] = parts[at]


def in_smem():
    return pl.BlockSpec(memory_space=pltpu.SMEM)


def in_vmem():
    return pl.BlockSpec(memory_space=pltpu.VMEM)


def local(object_slices, probe_modes, propagator_phase, measured, offsets, counts):
    slices, _, tile_rows, columns = object_slices.shape
    modes, _, pixels, _ = probe_modes.shape
    slots = measured.shape[0]
    planes = 2 * slices
    peers = lax.axis_size("row")
    params = pltpu.CompilerParams(vmem_limit_bytes=VMEM_LIMIT)
    tile = object_slices.reshape(planes, tile_rows, columns)
    starts = [sum(CHUNKS[:i]) for i in range(len(CHUNKS))]

    meta_own = jnp.concatenate([offsets, jnp.broadcast_to(counts, (slots, 1))], axis=1)
    meta_far = shifted(meta_own, "row", 2)

    def strips(meta, *extra):
        rest = sum(part.size // (slots * tile_rows * pixels) for part in extra)
        return pl.pallas_call(
            functools.partial(cut_kernel, pixels, bool(extra)),
            out_shape=[
                jax.ShapeDtypeStruct((size, planes + rest, tile_rows, pixels), F32) for size in CHUNKS
            ],
            in_specs=[in_smem()] + [in_vmem()] * (1 + len(extra)),
            out_specs=[in_vmem()] * len(CHUNKS),
            compiler_params=params,
            cost_estimate=pl.CostEstimate(flops=0, bytes_accessed=4 << 20, transcendentals=0),
        )(meta, tile, *extra)

    up_strips = strips(meta_own, measured)
    meta_mid = shifted(lax.optimization_barrier((meta_own, up_strips[0]))[0], "row", 1)
    down_strips = strips(meta_far)
    above, below = [], []
    for up, down in zip(up_strips, down_strips):
        if above:
            up, down, _, _ = lax.optimization_barrier((up, down, above[-1], below[-1]))
        above.append(shifted(up, "row", 1))
        below.append(shifted(down, "row", -1))
    prop = jnp.stack([jnp.cos(propagator_phase), jnp.sin(propagator_phase)])
    tables = jnp.asarray(fourier_tables(pixels))

    share = pixels // peers
    total = jnp.zeros((2 * modes + 1, pixels, pixels), F32)
    mid, back_own, back_far = [], [], []
    for index, (first, size) in enumerate(zip(starts, CHUNKS)):
        strip = jax.ShapeDtypeStruct((size, planes, tile_rows, pixels), F32)
        part = jax.ShapeDtypeStruct((peers // 2, 2 * modes + 1, share, pixels), F32)
        shares = [part, part] if index == len(CHUNKS) - 1 else []
        field = pltpu.VMEM((BATCH, planes, pixels, pixels), F32)
        kept = pltpu.VMEM((BATCH, modes, 2, pixels, pixels), F32)
        to_above, to_mid, to_below, total, *shares = pl.pallas_call(
            functools.partial(slot_kernel, first),
            out_shape=[strip, strip, strip, jax.ShapeDtypeStruct(total.shape, F32)] + shares,
            in_specs=[in_smem()] + [in_vmem()] * 7,
            out_specs=[in_vmem()] * (4 + len(shares)),
            scratch_shapes=[pltpu.VMEM((planes, 3 * tile_rows, pixels), F32), field, field, kept, kept],
            compiler_params=params,
            cost_estimate=pl.CostEstimate(
                flops=size * 6 * modes * 3 * 16 * pixels**3, bytes_accessed=8 << 20, transcendentals=0
            ),
        )(meta_mid, tile, above[index], below[index], probe_modes, prop, tables, total)
        mid.append(to_mid)
        back_own.append(shifted(to_above, "row", -1))
        back_far.append(shifted(to_below, "row", 1))

    own, other = shares
    own, other, back_own[:-1], back_far[:-1] = lax.optimization_barrier(
        (own, other, back_own[:-1], back_far[:-1])
    )
    both = own + lax.ppermute(other, "row", [(i, i ^ 1) for i in range(peers)])
    parts = lax.all_to_all(
        both, "row", 0, 0, axis_index_groups=[list(range(core, peers, 2)) for core in range(2)]
    )
    spread = pl.pallas_call(
        step_kernel,
        out_shape=jax.ShapeDtypeStruct((peers, 2 * modes, share, pixels), F32),
        in_specs=[in_vmem()],
        out_specs=in_vmem(),
        compiler_params=params,
    )(parts)
    gathered = lax.all_to_all(spread, "row", 0, 0)

    object_grad = pl.pallas_call(
        functools.partial(add_kernel, pixels),
        out_shape=jax.ShapeDtypeStruct(tile.shape, F32),
        in_specs=[in_smem()] * 3 + [in_vmem()] * (3 * len(CHUNKS)),
        out_specs=in_vmem(),
        compiler_params=params,
        cost_estimate=pl.CostEstimate(flops=0, bytes_accessed=5 << 20, transcendentals=0),
    )(meta_own, meta_mid, meta_far, *mid, *back_own, *back_far).reshape(object_slices.shape)

    probe_step = pl.pallas_call(
        order_kernel,
        out_shape=jax.ShapeDtypeStruct((2 * modes, pixels, pixels), F32),
        in_specs=[in_vmem()],
        out_specs=in_vmem(),
        compiler_params=params,
    )(gathered).reshape(probe_modes.shape)
    return (object_grad, probe_step)


def solution(mesh):
    in_specs = (
        P(None, None, ("grp", "row"), None),
        P("grp", None, None, None),
        P(),
        P(("grp", "row"), None, None),
        P(("grp", "row"), None),
        P(("grp", "row")),
    )
    out_specs = (P(None, None, ("grp", "row"), None), P("grp", None, None, None))
    return jax.shard_map(local, mesh=mesh, in_specs=in_specs, out_specs=out_specs, check_vma=False)
```

```python
import functools

import jax
import jax.numpy as jnp
import numpy as np
from jax import lax
from jax.experimental import pallas as pl
from jax.experimental.pallas import tpu as pltpu
from jax.sharding import PartitionSpec as P

CHUNKS = (2, 4, 2)
BATCH = 2
VMEM_LIMIT = 48 * 1024 * 1024
F32 = jnp.float32
BF16 = jnp.bfloat16


def shifted(array, axis, by):
    peers = lax.axis_size(axis)
    return lax.ppermute(array, axis, [(i, (i + by) % peers) for i in range(peers)])


def fourier_tables(pixels):
    indices = np.arange(pixels)
    angles = 2.0 * np.pi * (indices[:, None] * indices[None, :] % pixels) / pixels
    re = np.cos(angles) / np.sqrt(pixels)
    im = -np.sin(angles) / np.sqrt(pixels)
    left = np.block([[re, -im], [im, re]]).astype(np.float32)
    high = left.astype(BF16)
    low = (left - high.astype(np.float32)).astype(BF16)
    return np.stack([high, low, high.T, low.T])


def pieces(array):
    high = array.astype(BF16)
    return high, (array - high.astype(F32)).astype(BF16)


def transform(tables, conj, waves):
    at_left, at_right = (2, 0) if conj else (0, 2)
    left = jnp.concatenate([tables[at_left], tables[at_left + 1], tables[at_left]], axis=1)
    right = jnp.concatenate([tables[at_right], tables[at_right], tables[at_right + 1]], axis=0)
    stacked = jnp.concatenate([jnp.concatenate(wave, axis=0) for wave in waves], axis=1)
    high, low = pieces(stacked)
    half = jnp.dot(left, jnp.concatenate([high, high, low], axis=0), preferred_element_type=F32)
    pixels = half.shape[0] // 2
    places = [i * pixels for i in range(len(waves))]
    turned = jnp.concatenate(
        [
            jnp.concatenate([half[:pixels, at : at + pixels], half[pixels:, at : at + pixels]], axis=1)
            for at in places
        ],
        axis=0,
    )
    high, low = pieces(turned)
    whole = jnp.dot(jnp.concatenate([high, low, high], axis=1), right, preferred_element_type=F32)
    return [(whole[at : at + pixels, :pixels], whole[at : at + pixels, pixels:]) for at in places]


def times(one, two):
    return one[0] * two[0] - one[1] * two[1], one[0] * two[1] + one[1] * two[0]


def conj_times(one, two):
    return one[0] * two[0] + one[1] * two[1], one[0] * two[1] - one[1] * two[0]


def place(column, columns, pixels):
    base = jnp.minimum(column // pixels * pixels, columns - 2 * pixels)
    return pl.multiple_of(base, pixels), column - base


def cut(tile, column, pixels):
    base, shift = place(column, tile.shape[-1], pixels)
    rows = tile.shape[1]
    wide = tile[:, :, pl.ds(base, 2 * pixels)].reshape(-1, 2 * pixels)
    turned = pltpu.roll(wide, 2 * pixels - shift, 1)
    return turned[:, :pixels].reshape(-1, rows, pixels)


def cut_kernel(pixels, chunks, own, far, counts, tile, measured, *outs):
    planes, rows, _ = tile.shape
    for (first, size), up, down in zip(chunks, outs[::2], outs[1::2]):
        for at in range(size):
            slot = first + at
            up[at, :planes] = cut(tile, own[slot, 1], pixels)
            live = jnp.where(slot < counts[0], 1.0, 0.0).astype(F32)
            up[at, planes:] = (measured[slot] * live).reshape(-1, rows, pixels)
            down[at] = cut(tile, far[slot, 1], pixels)


def add_kernel(pixels, own, mid, far, *refs):
    *refs, out = refs
    out[...] = jnp.zeros_like(out)
    count = len(refs) // 3
    lane = lax.broadcasted_iota(jnp.int32, (1, 1, pixels), 2)
    for offsets, group in ((mid, refs[:count]), (own, refs[count : 2 * count]), (far, refs[2 * count :])):
        first = 0
        for parts in group:

            def add(at, carry, parts=parts, first=first, offsets=offsets):
                base, shift = place(offsets[first + at, 1], out.shape[-1], pixels)
                part = parts[at]
                turned = pltpu.roll(part.reshape(-1, pixels), lax.rem(shift, pixels), 1).reshape(part.shape)
                out[:, :, pl.ds(base, pixels)] += jnp.where(lane >= shift, turned, 0.0)
                out[:, :, pl.ds(pl.multiple_of(base + pixels, pixels), pixels)] += jnp.where(
                    lane < shift, turned, 0.0
                )
                return carry

            lax.fori_loop(0, parts.shape[0], add, 0)
            first += parts.shape[0]


def slot_kernel(
    first, offsets, tile, above, below, probe, prop, tables, so_far,
    out_above, out_mid, out_below, total, *refs,
):
    shares, (window, patch, grads, exit_wave, far) = refs[:-5], refs[-5:]
    size = above.shape[0]
    planes = tile.shape[0]
    modes, _, pixels, _ = probe.shape
    rows = above.shape[2]
    total[...] = so_far[...]
    held = [(s, m) for s in range(BATCH) for m in range(modes)]

    def is_live(at):
        return jnp.max(above[at, planes, :8]) > 0.0

    def leave(slots):
        for at in slots:
            for out in (out_above, out_mid, out_below):
                out[at] = jnp.zeros(out.shape[1:], F32)

    def visit(slots):
        starts = [lax.rem(offsets[first + at, 0], rows) for at in slots]
        live = [jnp.where(is_live(at), 1.0, 0.0).astype(F32) for at in slots]
        for s, at in enumerate(slots):
            window[:, :rows] = above[at, :planes]
            window[:, rows : 2 * rows] = cut(tile, offsets[first + at, 1], pixels)
            window[:, 2 * rows :] = below[at]
            patch[s] = window[:, pl.ds(starts[s], pixels), :]
            total[2 * modes] += live[s] * (patch[s, 0] * patch[s, 0] + patch[s, 1] * patch[s, 1])
        waves = [times((probe[m, 0], probe[m, 1]), (patch[s, 0], patch[s, 1])) for s, m in held]
        waves = transform(tables, False, waves)
        waves = [times((prop[0], prop[1]), wave) for wave in waves]
        waves = transform(tables, True, waves)
        for (s, m), wave in zip(held, waves):
            exit_wave[s, m, 0], exit_wave[s, m, 1] = wave
        waves = [times(wave, (patch[s, 2], patch[s, 3])) for (s, m), wave in zip(held, waves)]
        waves = transform(tables, False, waves)
        intensity = [jnp.zeros((pixels, pixels), F32)] * BATCH
        for (s, m), wave in zip(held, waves):
            far[s, m, 0], far[s, m, 1] = wave
            intensity[s] = intensity[s] + wave[0] * wave[0] + wave[1] * wave[1]
        misfit = [2.0 * live[s] * (intensity[s] - above[at, planes:].reshape(pixels, pixels)) for s, at in enumerate(slots)]
        waves = [(misfit[s] * far[s, m, 0], misfit[s] * far[s, m, 1]) for s, m in held]
        waves = transform(tables, True, waves)
        grads[...] = jnp.zeros_like(grads)
        for (s, m), wave in zip(held, waves):
            re, im = conj_times((exit_wave[s, m, 0], exit_wave[s, m, 1]), wave)
            grads[s, 2] += re
            grads[s, 3] += im
        waves = [conj_times((patch[s, 2], patch[s, 3]), wave) for (s, m), wave in zip(held, waves)]
        waves = transform(tables, False, waves)
        waves = [conj_times((prop[0], prop[1]), wave) for wave in waves]
        waves = transform(tables, True, waves)
        for (s, m), wave in zip(held, waves):
            re, im = conj_times((patch[s, 0], patch[s, 1]), wave)
            total[2 * m] += re
            total[2 * m + 1] += im
            re, im = conj_times((probe[m, 0], probe[m, 1]), wave)
            grads[s, 0] += re
            grads[s, 1] += im
        for s, at in enumerate(slots):
            window[...] = jnp.zeros_like(window)
            window[:, pl.ds(starts[s], pixels), :] = grads[s]
            out_above[at] = window[:, :rows]
            out_mid[at] = window[:, rows : 2 * rows]
            out_below[at] = window[:, 2 * rows :]

    def step(index, carry):
        slots = [index * BATCH + s for s in range(BATCH)]
        some = is_live(slots[0])
        pl.when(some)(lambda: visit(slots))
        pl.when(jnp.logical_not(some))(lambda: leave(slots))
        return carry

    lax.fori_loop(0, size // BATCH, step, 0)

    if shares:
        own, other = shares
        chips, _, share, _ = own.shape
        core = lax.rem(offsets[0, 0] // rows + 1, 2)
        for chip in range(chips):
            for plane in range(2 * modes + 1):
                own[chip, plane] = total[plane, pl.ds((2 * chip + core) * share, share)]
                other[chip, plane] = total[plane, pl.ds((2 * chip + 1 - core) * share, share)]


def step_kernel(parts, out):
    summed = parts[0]
    for at in range(1, parts.shape[0]):
        summed = summed + parts[at]
    step = summed[:-1] / (summed[-1:] + 1.0)
    for at in range(out.shape[0]):
        out[at] = step


def order_kernel(parts, out):
    share = parts.shape[2]
    for at in range(parts.shape[0]):
        out[:, at * share : (at + 1) * share] = parts[at]


def in_smem():
    return pl.BlockSpec(memory_space=pltpu.SMEM)


def in_vmem():
    return pl.BlockSpec(memory_space=pltpu.VMEM)


def local(object_slices, probe_modes, propagator_phase, measured, offsets, counts):
    slices, _, tile_rows, columns = object_slices.shape
    modes, _, pixels, _ = probe_modes.shape
    planes = 2 * slices
    peers = lax.axis_size("row")
    params = pltpu.CompilerParams(vmem_limit_bytes=VMEM_LIMIT)
    tile = object_slices.reshape(planes, tile_rows, columns)
    starts = [sum(CHUNKS[:i]) for i in range(len(CHUNKS))]

    far = shifted(offsets, "row", 2)
    middle = shifted(offsets, "row", 1)

    def strips(chunks):
        shapes = []
        for _, size in chunks:
            for count in (planes + pixels // tile_rows, planes):
                shapes.append(jax.ShapeDtypeStruct((size, count, tile_rows, pixels), F32))
        outs = pl.pallas_call(
            functools.partial(cut_kernel, pixels, chunks),
            out_shape=shapes,
            in_specs=[in_smem()] * 3 + [in_vmem()] * 2,
            out_specs=[in_vmem()] * len(shapes),
            compiler_params=params,
            cost_estimate=pl.CostEstimate(flops=0, bytes_accessed=4 << 20, transcendentals=0),
        )(offsets, far, counts, tile, measured)
        return list(zip(outs[::2], outs[1::2]))

    chunks = list(zip(starts, CHUNKS))
    above, below = [], []
    for up, down in strips(chunks[:1]) + strips(chunks[1:]):
        if above:
            up, down, _, _ = lax.optimization_barrier((up, down, above[-1], below[-1]))
        above.append(shifted(up, "row", 1))
        below.append(shifted(down, "row", -1))
    prop = jnp.stack([jnp.cos(propagator_phase), jnp.sin(propagator_phase)])
    tables = jnp.asarray(fourier_tables(pixels))

    share = pixels // peers
    total = jnp.zeros((2 * modes + 1, pixels, pixels), F32)
    mid, back_own, back_far = [], [], []
    for index, (first, size) in enumerate(zip(starts, CHUNKS)):
        strip = jax.ShapeDtypeStruct((size, planes, tile_rows, pixels), F32)
        part = jax.ShapeDtypeStruct((peers // 2, 2 * modes + 1, share, pixels), F32)
        shares = [part, part] if index == len(CHUNKS) - 1 else []
        field = pltpu.VMEM((BATCH, planes, pixels, pixels), F32)
        kept = pltpu.VMEM((BATCH, modes, 2, pixels, pixels), F32)
        to_above, to_mid, to_below, total, *shares = pl.pallas_call(
            functools.partial(slot_kernel, first),
            out_shape=[strip, strip, strip, jax.ShapeDtypeStruct(total.shape, F32)] + shares,
            in_specs=[in_smem()] + [in_vmem()] * 7,
            out_specs=[in_vmem()] * (4 + len(shares)),
            scratch_shapes=[pltpu.VMEM((planes, 3 * tile_rows, pixels), F32), field, field, kept, kept],
            compiler_params=params,
            cost_estimate=pl.CostEstimate(
                flops=size * 6 * modes * 3 * 16 * pixels**3, bytes_accessed=8 << 20, transcendentals=0
            ),
        )(middle, tile, above[index], below[index], probe_modes, prop, tables, total)
        mid.append(to_mid)
        back_own.append(shifted(to_above, "row", -1))
        back_far.append(shifted(to_below, "row", 1))

    own, other = shares
    own, other, back_own[:-1], back_far[:-1] = lax.optimization_barrier(
        (own, other, back_own[:-1], back_far[:-1])
    )
    both = own + lax.ppermute(other, "row", [(i, i ^ 1) for i in range(peers)])
    both, back_own, back_far = lax.optimization_barrier((both, back_own, back_far))
    parts = lax.all_to_all(
        both, "row", 0, 0, axis_index_groups=[list(range(core, peers, 2)) for core in range(2)]
    )
    spread = pl.pallas_call(
        step_kernel,
        out_shape=jax.ShapeDtypeStruct((peers, 2 * modes, share, pixels), F32),
        in_specs=[in_vmem()],
        out_specs=in_vmem(),
        compiler_params=params,
    )(parts)
    gathered = lax.all_to_all(spread, "row", 0, 0)

    object_grad = pl.pallas_call(
        functools.partial(add_kernel, pixels),
        out_shape=jax.ShapeDtypeStruct(tile.shape, F32),
        in_specs=[in_smem()] * 3 + [in_vmem()] * (3 * len(CHUNKS)),
        out_specs=in_vmem(),
        compiler_params=params,
        cost_estimate=pl.CostEstimate(flops=0, bytes_accessed=5 << 20, transcendentals=0),
    )(offsets, middle, far, *mid, *back_own, *back_far).reshape(object_slices.shape)

    probe_step = pl.pallas_call(
        order_kernel,
        out_shape=jax.ShapeDtypeStruct((2 * modes, pixels, pixels), F32),
        in_specs=[in_vmem()],
        out_specs=in_vmem(),
        compiler_params=params,
    )(gathered).reshape(probe_modes.shape)
    return (object_grad, probe_step)


def solution(mesh):
    in_specs = (
        P(None, None, ("grp", "row"), None),
        P("grp", None, None, None),
        P(),
        P(("grp", "row"), None, None),
        P(("grp", "row"), None),
        P(("grp", "row")),
    )
    out_specs = (P(None, None, ("grp", "row"), None), P("grp", None, None, None))
    return jax.shard_map(local, mesh=mesh, in_specs=in_specs, out_specs=out_specs, check_vma=False)
```

```python
import functools

import jax
import jax.numpy as jnp
import numpy as np
from jax import lax
from jax.experimental import pallas as pl
from jax.experimental.pallas import tpu as pltpu
from jax.sharding import PartitionSpec as P

CHUNKS = (8,)
BATCH = 2
VMEM_LIMIT = 48 * 1024 * 1024
F32 = jnp.float32
BF16 = jnp.bfloat16


def shifted(array, axis, by):
    peers = lax.axis_size(axis)
    return lax.ppermute(array, axis, [(i, (i + by) % peers) for i in range(peers)])


def fourier_tables(pixels):
    indices = np.arange(pixels)
    angles = 2.0 * np.pi * (indices[:, None] * indices[None, :] % pixels) / pixels
    re = np.cos(angles) / np.sqrt(pixels)
    im = -np.sin(angles) / np.sqrt(pixels)
    left = np.block([[re, -im], [im, re]]).astype(np.float32)
    high = left.astype(BF16)
    low = (left - high.astype(np.float32)).astype(BF16)
    return np.stack([high, low, high.T, low.T])


def pieces(array):
    high = array.astype(BF16)
    return high, (array - high.astype(F32)).astype(BF16)


def transform(tables, conj, waves):
    at_left, at_right = (2, 0) if conj else (0, 2)
    left = jnp.concatenate([tables[at_left], tables[at_left + 1], tables[at_left]], axis=1)
    right = jnp.concatenate([tables[at_right], tables[at_right], tables[at_right + 1]], axis=0)
    stacked = jnp.concatenate([jnp.concatenate(wave, axis=0) for wave in waves], axis=1)
    high, low = pieces(stacked)
    half = jnp.dot(left, jnp.concatenate([high, high, low], axis=0), preferred_element_type=F32)
    pixels = half.shape[0] // 2
    places = [i * pixels for i in range(len(waves))]
    turned = jnp.concatenate(
        [
            jnp.concatenate([half[:pixels, at : at + pixels], half[pixels:, at : at + pixels]], axis=1)
            for at in places
        ],
        axis=0,
    )
    high, low = pieces(turned)
    whole = jnp.dot(jnp.concatenate([high, low, high], axis=1), right, preferred_element_type=F32)
    return [(whole[at : at + pixels, :pixels], whole[at : at + pixels, pixels:]) for at in places]


def times(one, two):
    return one[0] * two[0] - one[1] * two[1], one[0] * two[1] + one[1] * two[0]


def conj_times(one, two):
    return one[0] * two[0] + one[1] * two[1], one[0] * two[1] - one[1] * two[0]


def place(column, columns, pixels):
    base = jnp.minimum(column // pixels * pixels, columns - 2 * pixels)
    return pl.multiple_of(base, pixels), column - base


def cut(tile, column, pixels):
    base, shift = place(column, tile.shape[-1], pixels)
    rows = tile.shape[1]
    wide = tile[:, :, pl.ds(base, 2 * pixels)].reshape(-1, 2 * pixels)
    turned = pltpu.roll(wide, 2 * pixels - shift, 1)
    return turned[:, :pixels].reshape(-1, rows, pixels)


def cut_kernel(pixels, chunks, own, far, tile, *outs):
    for (first, size), up, down in zip(chunks, outs[::2], outs[1::2]):
        for at in range(size):
            up[at] = cut(tile, own[first + at, 1], pixels)
            down[at] = cut(tile, far[first + at, 1], pixels)


def add_kernel(pixels, own, mid, far, *refs):
    *refs, out = refs
    out[...] = jnp.zeros_like(out)
    count = len(refs) // 3
    lane = lax.broadcasted_iota(jnp.int32, (1, 1, pixels), 2)
    for offsets, group in ((mid, refs[:count]), (own, refs[count : 2 * count]), (far, refs[2 * count :])):
        first = 0
        for parts in group:

            def add(at, carry, parts=parts, first=first, offsets=offsets):
                base, shift = place(offsets[first + at, 1], out.shape[-1], pixels)
                part = parts[at]
                turned = pltpu.roll(part.reshape(-1, pixels), lax.rem(shift, pixels), 1).reshape(part.shape)
                out[:, :, pl.ds(base, pixels)] += jnp.where(lane >= shift, turned, 0.0)
                out[:, :, pl.ds(pl.multiple_of(base + pixels, pixels), pixels)] += jnp.where(
                    lane < shift, turned, 0.0
                )
                return carry

            lax.fori_loop(0, parts.shape[0], add, 0)
            first += parts.shape[0]


def slot_kernel(
    first, offsets, tile, above, below, target, probe, prop, tables, so_far,
    out_above, out_mid, out_below, total, *refs,
):
    shares, (window, patch, grads, exit_wave, far) = refs[:-5], refs[-5:]
    size = above.shape[0]
    modes, _, pixels, _ = probe.shape
    rows = above.shape[2]
    total[...] = so_far[...]
    held = [(s, m) for s in range(BATCH) for m in range(modes)]

    def is_live(at):
        return jnp.max(target[first + at, :8]) > 0.0

    def leave(slots):
        for at in slots:
            for out in (out_above, out_mid, out_below):
                out[at] = jnp.zeros(out.shape[1:], F32)

    def visit(slots):
        starts = [lax.rem(offsets[first + at, 0], rows) for at in slots]
        live = [jnp.where(is_live(at), 1.0, 0.0).astype(F32) for at in slots]
        for s, at in enumerate(slots):
            window[:, :rows] = above[at]
            window[:, rows : 2 * rows] = cut(tile, offsets[first + at, 1], pixels)
            window[:, 2 * rows :] = below[at]
            patch[s] = window[:, pl.ds(starts[s], pixels), :]
            total[2 * modes] += live[s] * (patch[s, 0] * patch[s, 0] + patch[s, 1] * patch[s, 1])
        waves = [times((probe[m, 0], probe[m, 1]), (patch[s, 0], patch[s, 1])) for s, m in held]
        waves = transform(tables, False, waves)
        waves = [times((prop[0], prop[1]), wave) for wave in waves]
        waves = transform(tables, True, waves)
        for (s, m), wave in zip(held, waves):
            exit_wave[s, m, 0], exit_wave[s, m, 1] = wave
        waves = [times(wave, (patch[s, 2], patch[s, 3])) for (s, m), wave in zip(held, waves)]
        waves = transform(tables, False, waves)
        intensity = [jnp.zeros((pixels, pixels), F32)] * BATCH
        for (s, m), wave in zip(held, waves):
            far[s, m, 0], far[s, m, 1] = wave
            intensity[s] = intensity[s] + wave[0] * wave[0] + wave[1] * wave[1]
        misfit = [2.0 * live[s] * (intensity[s] - target[first + at]) for s, at in enumerate(slots)]
        waves = [(misfit[s] * far[s, m, 0], misfit[s] * far[s, m, 1]) for s, m in held]
        waves = transform(tables, True, waves)
        grads[...] = jnp.zeros_like(grads)
        for (s, m), wave in zip(held, waves):
            re, im = conj_times((exit_wave[s, m, 0], exit_wave[s, m, 1]), wave)
            grads[s, 2] += re
            grads[s, 3] += im
        waves = [conj_times((patch[s, 2], patch[s, 3]), wave) for (s, m), wave in zip(held, waves)]
        waves = transform(tables, False, waves)
        waves = [conj_times((prop[0], prop[1]), wave) for wave in waves]
        waves = transform(tables, True, waves)
        for (s, m), wave in zip(held, waves):
            re, im = conj_times((patch[s, 0], patch[s, 1]), wave)
            total[2 * m] += re
            total[2 * m + 1] += im
            re, im = conj_times((probe[m, 0], probe[m, 1]), wave)
            grads[s, 0] += re
            grads[s, 1] += im
        for s, at in enumerate(slots):
            window[...] = jnp.zeros_like(window)
            window[:, pl.ds(starts[s], pixels), :] = grads[s]
            out_above[at] = window[:, :rows]
            out_mid[at] = window[:, rows : 2 * rows]
            out_below[at] = window[:, 2 * rows :]

    def step(index, carry):
        slots = [index * BATCH + s for s in range(BATCH)]
        some = is_live(slots[0])
        pl.when(some)(lambda: visit(slots))
        pl.when(jnp.logical_not(some))(lambda: leave(slots))
        return carry

    lax.fori_loop(0, size // BATCH, step, 0)

    if shares:
        own, other = shares
        chips, _, share, _ = own.shape
        core = lax.rem(offsets[0, 0] // rows + 1, 2)
        for chip in range(chips):
            for plane in range(2 * modes + 1):
                own[chip, plane] = total[plane, pl.ds((2 * chip + core) * share, share)]
                other[chip, plane] = total[plane, pl.ds((2 * chip + 1 - core) * share, share)]


def step_kernel(parts, out):
    summed = parts[0]
    for at in range(1, parts.shape[0]):
        summed = summed + parts[at]
    step = summed[:-1] / (summed[-1:] + 1.0)
    for at in range(out.shape[0]):
        out[at] = step


def order_kernel(rows, offsets, own, other, out):
    chips, _, share, _ = own.shape
    core = lax.rem(offsets[0, 0] // rows, 2)
    for chip in range(chips):
        out[:, pl.ds((2 * chip + core) * share, share)] = own[chip]
        out[:, pl.ds((2 * chip + 1 - core) * share, share)] = other[chip]


def in_smem():
    return pl.BlockSpec(memory_space=pltpu.SMEM)


def in_vmem():
    return pl.BlockSpec(memory_space=pltpu.VMEM)


def local(object_slices, probe_modes, propagator_phase, measured, offsets, counts):
    slices, _, tile_rows, columns = object_slices.shape
    modes, _, pixels, _ = probe_modes.shape
    planes = 2 * slices
    peers = lax.axis_size("row")
    params = pltpu.CompilerParams(vmem_limit_bytes=VMEM_LIMIT)
    tile = object_slices.reshape(planes, tile_rows, columns)
    starts = [sum(CHUNKS[:i]) for i in range(len(CHUNKS))]

    far = shifted(offsets, "row", 2)
    middle = shifted(offsets, "row", 1)
    live = lax.broadcasted_iota(jnp.int32, (measured.shape[0], 1, 1), 0) < counts[0]
    target = shifted(jnp.where(live, measured, 0.0), "row", 1)
    far, target = lax.optimization_barrier((far, target))

    def strips(chunks):
        shapes = []
        for _, size in chunks:
            shapes += [jax.ShapeDtypeStruct((size, planes, tile_rows, pixels), F32)] * 2
        outs = pl.pallas_call(
            functools.partial(cut_kernel, pixels, chunks),
            out_shape=shapes,
            in_specs=[in_smem()] * 2 + [in_vmem()],
            out_specs=[in_vmem()] * len(shapes),
            compiler_params=params,
            cost_estimate=pl.CostEstimate(flops=0, bytes_accessed=4 << 20, transcendentals=0),
        )(offsets, far, tile)
        return list(zip(outs[::2], outs[1::2]))

    chunks = list(zip(starts, CHUNKS))
    above, below = [], []
    for up, down in strips(chunks[:1]) + (strips(chunks[1:]) if len(chunks) > 1 else []):
        if above:
            up, down, _, _ = lax.optimization_barrier((up, down, above[-1], below[-1]))
        above.append(shifted(up, "row", 1))
        below.append(shifted(down, "row", -1))
    prop = jnp.stack([jnp.cos(propagator_phase), jnp.sin(propagator_phase)])
    tables = jnp.asarray(fourier_tables(pixels))

    share = pixels // peers
    total = jnp.zeros((2 * modes + 1, pixels, pixels), F32)
    mid, back_own, back_far = [], [], []
    for index, (first, size) in enumerate(zip(starts, CHUNKS)):
        strip = jax.ShapeDtypeStruct((size, planes, tile_rows, pixels), F32)
        part = jax.ShapeDtypeStruct((peers // 2, 2 * modes + 1, share, pixels), F32)
        shares = [part, part] if index == len(CHUNKS) - 1 else []
        field = pltpu.VMEM((BATCH, planes, pixels, pixels), F32)
        kept = pltpu.VMEM((BATCH, modes, 2, pixels, pixels), F32)
        to_above, to_mid, to_below, total, *shares = pl.pallas_call(
            functools.partial(slot_kernel, first),
            out_shape=[strip, strip, strip, jax.ShapeDtypeStruct(total.shape, F32)] + shares,
            in_specs=[in_smem()] + [in_vmem()] * 8,
            out_specs=[in_vmem()] * (4 + len(shares)),
            scratch_shapes=[pltpu.VMEM((planes, 3 * tile_rows, pixels), F32), field, field, kept, kept],
            compiler_params=params,
            cost_estimate=pl.CostEstimate(
                flops=size * 6 * modes * 3 * 16 * pixels**3, bytes_accessed=8 << 20, transcendentals=0
            ),
        )(middle, tile, above[index], below[index], target, probe_modes, prop, tables, total)
        mid.append(to_mid)
        back_own.append(shifted(to_above, "row", -1))
        back_far.append(shifted(to_below, "row", 1))

    own, other = shares
    own, other, back_own[:-1], back_far[:-1] = lax.optimization_barrier(
        (own, other, back_own[:-1], back_far[:-1])
    )
    swap = [(i, i ^ 1) for i in range(peers)]
    cores = [list(range(core, peers, 2)) for core in range(2)]
    both = own + lax.ppermute(other, "row", swap)
    both, back_own, back_far = lax.optimization_barrier((both, back_own, back_far))
    parts = lax.all_to_all(both, "row", 0, 0, axis_index_groups=cores)
    spread = pl.pallas_call(
        step_kernel,
        out_shape=jax.ShapeDtypeStruct((peers // 2, 2 * modes, share, pixels), F32),
        in_specs=[in_vmem()],
        out_specs=in_vmem(),
        compiler_params=params,
    )(parts)
    gathered = lax.all_to_all(spread, "row", 0, 0, axis_index_groups=cores)

    object_grad = pl.pallas_call(
        functools.partial(add_kernel, pixels),
        out_shape=jax.ShapeDtypeStruct(tile.shape, F32),
        in_specs=[in_smem()] * 3 + [in_vmem()] * (3 * len(CHUNKS)),
        out_specs=in_vmem(),
        compiler_params=params,
        cost_estimate=pl.CostEstimate(flops=0, bytes_accessed=5 << 20, transcendentals=0),
    )(offsets, middle, far, *mid, *back_own, *back_far).reshape(object_slices.shape)

    probe_step = pl.pallas_call(
        functools.partial(order_kernel, tile_rows),
        out_shape=jax.ShapeDtypeStruct((2 * modes, pixels, pixels), F32),
        in_specs=[in_smem()] + [in_vmem()] * 2,
        out_specs=in_vmem(),
        compiler_params=params,
    )(offsets, gathered, lax.ppermute(gathered, "row", swap)).reshape(probe_modes.shape)
    return (object_grad, probe_step)


def solution(mesh):
    in_specs = (
        P(None, None, ("grp", "row"), None),
        P("grp", None, None, None),
        P(),
        P(("grp", "row"), None, None),
        P(("grp", "row"), None),
        P(("grp", "row")),
    )
    out_specs = (P(None, None, ("grp", "row"), None), P("grp", None, None, None))
    return jax.shard_map(local, mesh=mesh, in_specs=in_specs, out_specs=out_specs, check_vma=False)
```

```python
import functools

import jax
import jax.numpy as jnp
import numpy as np
from jax import lax
from jax.experimental import pallas as pl
from jax.experimental.pallas import tpu as pltpu
from jax.sharding import PartitionSpec as P

CHUNKS = (2, 4, 2)
BATCH = 2
VMEM_LIMIT = 48 * 1024 * 1024
F32 = jnp.float32
BF16 = jnp.bfloat16


def shifted(array, axis, by):
    peers = lax.axis_size(axis)
    return lax.ppermute(array, axis, [(i, (i + by) % peers) for i in range(peers)])


def fourier_tables(pixels):
    indices = np.arange(pixels)
    angles = 2.0 * np.pi * (indices[:, None] * indices[None, :] % pixels) / pixels
    re = np.cos(angles) / np.sqrt(pixels)
    im = -np.sin(angles) / np.sqrt(pixels)
    left = np.block([[re, -im], [im, re]]).astype(np.float32)
    high = left.astype(BF16)
    low = (left - high.astype(np.float32)).astype(BF16)
    return np.stack([high, low, high.T, low.T])


def pieces(array):
    high = array.astype(BF16)
    return high, (array - high.astype(F32)).astype(BF16)


def transform(tables, conj, waves):
    at_left, at_right = (2, 0) if conj else (0, 2)
    left = jnp.concatenate([tables[at_left], tables[at_left + 1], tables[at_left]], axis=1)
    right = jnp.concatenate([tables[at_right], tables[at_right], tables[at_right + 1]], axis=0)
    stacked = jnp.concatenate([jnp.concatenate(wave, axis=0) for wave in waves], axis=1)
    high, low = pieces(stacked)
    half = jnp.dot(left, jnp.concatenate([high, high, low], axis=0), preferred_element_type=F32)
    pixels = half.shape[0] // 2
    places = [i * pixels for i in range(len(waves))]
    turned = jnp.concatenate(
        [
            jnp.concatenate([half[:pixels, at : at + pixels], half[pixels:, at : at + pixels]], axis=1)
            for at in places
        ],
        axis=0,
    )
    high, low = pieces(turned)
    whole = jnp.dot(jnp.concatenate([high, low, high], axis=1), right, preferred_element_type=F32)
    return [(whole[at : at + pixels, :pixels], whole[at : at + pixels, pixels:]) for at in places]


def times(one, two):
    return one[0] * two[0] - one[1] * two[1], one[0] * two[1] + one[1] * two[0]


def conj_times(one, two):
    return one[0] * two[0] + one[1] * two[1], one[0] * two[1] - one[1] * two[0]


def place(column, columns, pixels):
    base = jnp.minimum(column // pixels * pixels, columns - 2 * pixels)
    return pl.multiple_of(base, pixels), column - base


def cut(tile, column, pixels):
    base, shift = place(column, tile.shape[-1], pixels)
    rows = tile.shape[1]
    wide = tile[:, :, pl.ds(base, 2 * pixels)].reshape(-1, 2 * pixels)
    turned = pltpu.roll(wide, 2 * pixels - shift, 1)
    return turned[:, :pixels].reshape(-1, rows, pixels)


def cut_kernel(pixels, offsets, tile, *outs):
    first = 0
    for out in outs:
        for at in range(out.shape[0]):
            out[at] = cut(tile, offsets[first + at, 1], pixels)
        first += out.shape[0]


def add_kernel(pixels, own, mid, far, *refs):
    *refs, out = refs
    out[...] = jnp.zeros_like(out)
    count = len(refs) // 3
    lane = lax.broadcasted_iota(jnp.int32, (1, 1, pixels), 2)
    for offsets, group in ((mid, refs[:count]), (own, refs[count : 2 * count]), (far, refs[2 * count :])):
        first = 0
        for parts in group:

            def add(at, carry, parts=parts, first=first, offsets=offsets):
                base, shift = place(offsets[first + at, 1], out.shape[-1], pixels)
                part = parts[at]
                turned = pltpu.roll(part.reshape(-1, pixels), lax.rem(shift, pixels), 1).reshape(part.shape)
                out[:, :, pl.ds(base, pixels)] += jnp.where(lane >= shift, turned, 0.0)
                out[:, :, pl.ds(pl.multiple_of(base + pixels, pixels), pixels)] += jnp.where(
                    lane < shift, turned, 0.0
                )
                return carry

            lax.fori_loop(0, parts.shape[0], add, 0)
            first += parts.shape[0]


def slot_kernel(
    first, offsets, tile, above, below, target, probe, prop, tables, so_far,
    out_above, out_mid, out_below, total, *refs,
):
    shares, (window, patch, grads, exit_wave, far) = refs[:-5], refs[-5:]
    size = above.shape[0]
    modes, _, pixels, _ = probe.shape
    rows = above.shape[2]
    total[...] = so_far[...]
    held = [(s, m) for s in range(BATCH) for m in range(modes)]

    def is_live(at):
        return jnp.max(target[first + at, :8]) > 0.0

    def leave(slots):
        for at in slots:
            for out in (out_above, out_mid, out_below):
                out[at] = jnp.zeros(out.shape[1:], F32)

    def visit(slots):
        starts = [lax.rem(offsets[first + at, 0], rows) for at in slots]
        live = [jnp.where(is_live(at), 1.0, 0.0).astype(F32) for at in slots]
        for s, at in enumerate(slots):
            window[:, :rows] = above[at]
            window[:, rows : 2 * rows] = cut(tile, offsets[first + at, 1], pixels)
            window[:, 2 * rows :] = below[at]
            patch[s] = window[:, pl.ds(starts[s], pixels), :]
            total[2 * modes] += live[s] * (patch[s, 0] * patch[s, 0] + patch[s, 1] * patch[s, 1])
        waves = [times((probe[m, 0], probe[m, 1]), (patch[s, 0], patch[s, 1])) for s, m in held]
        waves = transform(tables, False, waves)
        waves = [times((prop[0], prop[1]), wave) for wave in waves]
        waves = transform(tables, True, waves)
        for (s, m), wave in zip(held, waves):
            exit_wave[s, m, 0], exit_wave[s, m, 1] = wave
        waves = [times(wave, (patch[s, 2], patch[s, 3])) for (s, m), wave in zip(held, waves)]
        waves = transform(tables, False, waves)
        intensity = [jnp.zeros((pixels, pixels), F32)] * BATCH
        for (s, m), wave in zip(held, waves):
            far[s, m, 0], far[s, m, 1] = wave
            intensity[s] = intensity[s] + wave[0] * wave[0] + wave[1] * wave[1]
        misfit = [2.0 * live[s] * (intensity[s] - target[first + at]) for s, at in enumerate(slots)]
        waves = [(misfit[s] * far[s, m, 0], misfit[s] * far[s, m, 1]) for s, m in held]
        waves = transform(tables, True, waves)
        grads[...] = jnp.zeros_like(grads)
        for (s, m), wave in zip(held, waves):
            re, im = conj_times((exit_wave[s, m, 0], exit_wave[s, m, 1]), wave)
            grads[s, 2] += re
            grads[s, 3] += im
        waves = [conj_times((patch[s, 2], patch[s, 3]), wave) for (s, m), wave in zip(held, waves)]
        waves = transform(tables, False, waves)
        waves = [conj_times((prop[0], prop[1]), wave) for wave in waves]
        waves = transform(tables, True, waves)
        for (s, m), wave in zip(held, waves):
            re, im = conj_times((patch[s, 0], patch[s, 1]), wave)
            total[2 * m] += re
            total[2 * m + 1] += im
            re, im = conj_times((probe[m, 0], probe[m, 1]), wave)
            grads[s, 0] += re
            grads[s, 1] += im
        for s, at in enumerate(slots):
            window[...] = jnp.zeros_like(window)
            window[:, pl.ds(starts[s], pixels), :] = grads[s]
            out_above[at] = window[:, :rows]
            out_mid[at] = window[:, rows : 2 * rows]
            out_below[at] = window[:, 2 * rows :]

    def step(index, carry):
        slots = [index * BATCH + s for s in range(BATCH)]
        some = is_live(slots[0])
        pl.when(some)(lambda: visit(slots))
        pl.when(jnp.logical_not(some))(lambda: leave(slots))
        return carry

    lax.fori_loop(0, size // BATCH, step, 0)

    if shares:
        own, other = shares
        chips, _, share, _ = own.shape
        core = lax.rem(offsets[0, 0] // rows + 1, 2)
        for chip in range(chips):
            for plane in range(2 * modes + 1):
                own[chip, plane] = total[plane, pl.ds((2 * chip + core) * share, share)]
                other[chip, plane] = total[plane, pl.ds((2 * chip + 1 - core) * share, share)]


def step_kernel(parts, out):
    summed = parts[0]
    for at in range(1, parts.shape[0]):
        summed = summed + parts[at]
    step = summed[:-1] / (summed[-1:] + 1.0)
    for at in range(out.shape[0]):
        out[at] = step


def order_kernel(rows, offsets, own, other, out):
    chips, _, share, _ = own.shape
    core = lax.rem(offsets[0, 0] // rows, 2)
    for chip in range(chips):
        out[:, pl.ds((2 * chip + core) * share, share)] = own[chip]
        out[:, pl.ds((2 * chip + 1 - core) * share, share)] = other[chip]


def in_smem():
    return pl.BlockSpec(memory_space=pltpu.SMEM)


def in_vmem():
    return pl.BlockSpec(memory_space=pltpu.VMEM)


def local(object_slices, probe_modes, propagator_phase, measured, offsets, counts):
    slices, _, tile_rows, columns = object_slices.shape
    modes, _, pixels, _ = probe_modes.shape
    planes = 2 * slices
    peers = lax.axis_size("row")
    params = pltpu.CompilerParams(vmem_limit_bytes=VMEM_LIMIT)
    tile = object_slices.reshape(planes, tile_rows, columns)
    starts = [sum(CHUNKS[:i]) for i in range(len(CHUNKS))]

    far = shifted(offsets, "row", 2)
    middle = shifted(offsets, "row", 1)
    middle, own_offsets, sent = lax.optimization_barrier((middle, offsets, measured))
    live = lax.broadcasted_iota(jnp.int32, (measured.shape[0], 1, 1), 0) < counts[0]
    target = shifted(jnp.where(live, sent, 0.0), "row", 1)

    def strips(places):
        return pl.pallas_call(
            functools.partial(cut_kernel, pixels),
            out_shape=[jax.ShapeDtypeStruct((size, planes, tile_rows, pixels), F32) for size in CHUNKS],
            in_specs=[in_smem(), in_vmem()],
            out_specs=[in_vmem()] * len(CHUNKS),
            compiler_params=params,
            cost_estimate=pl.CostEstimate(flops=0, bytes_accessed=4 << 20, transcendentals=0),
        )(places, tile)

    up_strips = strips(own_offsets)
    down_strips = strips(far)
    above, below = [], []
    for up, down in zip(up_strips, down_strips):
        above.append(shifted(up, "row", 1))
        below.append(shifted(down, "row", -1))
    prop = jnp.stack([jnp.cos(propagator_phase), jnp.sin(propagator_phase)])
    tables = jnp.asarray(fourier_tables(pixels))

    share = pixels // peers
    total = jnp.zeros((2 * modes + 1, pixels, pixels), F32)
    mid, back_own, back_far = [], [], []
    for index, (first, size) in enumerate(zip(starts, CHUNKS)):
        if index >= 2:
            total, back_own[index - 2], back_far[index - 2] = lax.optimization_barrier(
                (total, back_own[index - 2], back_far[index - 2])
            )
        strip = jax.ShapeDtypeStruct((size, planes, tile_rows, pixels), F32)
        part = jax.ShapeDtypeStruct((peers // 2, 2 * modes + 1, share, pixels), F32)
        shares = [part, part] if index == len(CHUNKS) - 1 else []
        field = pltpu.VMEM((BATCH, planes, pixels, pixels), F32)
        kept = pltpu.VMEM((BATCH, modes, 2, pixels, pixels), F32)
        to_above, to_mid, to_below, total, *shares = pl.pallas_call(
            functools.partial(slot_kernel, first),
            out_shape=[strip, strip, strip, jax.ShapeDtypeStruct(total.shape, F32)] + shares,
            in_specs=[in_smem()] + [in_vmem()] * 8,
            out_specs=[in_vmem()] * (4 + len(shares)),
            scratch_shapes=[pltpu.VMEM((planes, 3 * tile_rows, pixels), F32), field, field, kept, kept],
            compiler_params=params,
            cost_estimate=pl.CostEstimate(
                flops=size * 6 * modes * 3 * 16 * pixels**3, bytes_accessed=8 << 20, transcendentals=0
            ),
        )(middle, tile, above[index], below[index], target, probe_modes, prop, tables, total)
        mid.append(to_mid)
        back_own.append(shifted(to_above, "row", -1))
        back_far.append(shifted(to_below, "row", 1))

    own, other = shares
    own, other, back_own[:-1], back_far[:-1] = lax.optimization_barrier(
        (own, other, back_own[:-1], back_far[:-1])
    )
    swap = [(i, i ^ 1) for i in range(peers)]
    cores = [list(range(core, peers, 2)) for core in range(2)]
    both = own + lax.ppermute(other, "row", swap)
    both, back_own, back_far = lax.optimization_barrier((both, back_own, back_far))
    parts = lax.all_to_all(both, "row", 0, 0, axis_index_groups=cores)
    spread = pl.pallas_call(
        step_kernel,
        out_shape=jax.ShapeDtypeStruct((peers // 2, 2 * modes, share, pixels), F32),
        in_specs=[in_vmem()],
        out_specs=in_vmem(),
        compiler_params=params,
    )(parts)
    gathered = lax.all_to_all(spread, "row", 0, 0, axis_index_groups=cores)

    object_grad = pl.pallas_call(
        functools.partial(add_kernel, pixels),
        out_shape=jax.ShapeDtypeStruct(tile.shape, F32),
        in_specs=[in_smem()] * 3 + [in_vmem()] * (3 * len(CHUNKS)),
        out_specs=in_vmem(),
        compiler_params=params,
        cost_estimate=pl.CostEstimate(flops=0, bytes_accessed=5 << 20, transcendentals=0),
    )(offsets, middle, far, *mid, *back_own, *back_far).reshape(object_slices.shape)

    probe_step = pl.pallas_call(
        functools.partial(order_kernel, tile_rows),
        out_shape=jax.ShapeDtypeStruct((2 * modes, pixels, pixels), F32),
        in_specs=[in_smem()] + [in_vmem()] * 2,
        out_specs=in_vmem(),
        compiler_params=params,
    )(offsets, gathered, lax.ppermute(gathered, "row", swap)).reshape(probe_modes.shape)
    return (object_grad, probe_step)


def solution(mesh):
    in_specs = (
        P(None, None, ("grp", "row"), None),
        P("grp", None, None, None),
        P(),
        P(("grp", "row"), None, None),
        P(("grp", "row"), None),
        P(("grp", "row")),
    )
    out_specs = (P(None, None, ("grp", "row"), None), P("grp", None, None, None))
    return jax.shard_map(local, mesh=mesh, in_specs=in_specs, out_specs=out_specs, check_vma=False)
```

```python
import functools

import jax
import jax.numpy as jnp
import numpy as np
from jax import lax
from jax.experimental import pallas as pl
from jax.experimental.pallas import tpu as pltpu
from jax.sharding import PartitionSpec as P

CHUNKS = (2, 4, 2)
BATCH = 2
VMEM_LIMIT = 48 * 1024 * 1024
F32 = jnp.float32
BF16 = jnp.bfloat16


def shifted(array, axis, by):
    peers = lax.axis_size(axis)
    return lax.ppermute(array, axis, [(i, (i + by) % peers) for i in range(peers)])


def fourier_tables(pixels):
    indices = np.arange(pixels)
    angles = 2.0 * np.pi * (indices[:, None] * indices[None, :] % pixels) / pixels
    re = np.cos(angles) / np.sqrt(pixels)
    im = -np.sin(angles) / np.sqrt(pixels)
    left = np.block([[re, -im], [im, re]]).astype(np.float32)
    high = left.astype(BF16)
    low = (left - high.astype(np.float32)).astype(BF16)
    return np.stack([high, low, high.T, low.T])


def pieces(array):
    high = array.astype(BF16)
    return high, (array - high.astype(F32)).astype(BF16)


def transform(tables, conj, waves):
    at_left, at_right = (2, 0) if conj else (0, 2)
    left = jnp.concatenate([tables[at_left], tables[at_left + 1], tables[at_left]], axis=1)
    right = jnp.concatenate([tables[at_right], tables[at_right], tables[at_right + 1]], axis=0)
    stacked = jnp.concatenate([jnp.concatenate(wave, axis=0) for wave in waves], axis=1)
    high, low = pieces(stacked)
    half = jnp.dot(left, jnp.concatenate([high, high, low], axis=0), preferred_element_type=F32)
    pixels = half.shape[0] // 2
    places = [i * pixels for i in range(len(waves))]
    turned = jnp.concatenate(
        [
            jnp.concatenate([half[:pixels, at : at + pixels], half[pixels:, at : at + pixels]], axis=1)
            for at in places
        ],
        axis=0,
    )
    high, low = pieces(turned)
    whole = jnp.dot(jnp.concatenate([high, low, high], axis=1), right, preferred_element_type=F32)
    return [(whole[at : at + pixels, :pixels], whole[at : at + pixels, pixels:]) for at in places]


def times(one, two):
    return one[0] * two[0] - one[1] * two[1], one[0] * two[1] + one[1] * two[0]


def conj_times(one, two):
    return one[0] * two[0] + one[1] * two[1], one[0] * two[1] - one[1] * two[0]


def place(column, columns, pixels):
    base = jnp.minimum(column // pixels * pixels, columns - 2 * pixels)
    return pl.multiple_of(base, pixels), column - base


def cut(tile, column, pixels):
    base, shift = place(column, tile.shape[-1], pixels)
    rows = tile.shape[1]
    wide = tile[:, :, pl.ds(base, 2 * pixels)].reshape(-1, 2 * pixels)
    turned = pltpu.roll(wide, 2 * pixels - shift, 1)
    return turned[:, :pixels].reshape(-1, rows, pixels)


def is_even(offsets, rows):
    return lax.rem(offsets[0, 0] // rows, 2) == 0


def cut_kernel(pixels, chunks, own, far, counts, tile, measured, *outs):
    planes, rows, _ = tile.shape
    even = is_even(own, rows)
    for (first, size), near, cross in zip(chunks, outs[::2], outs[1::2]):
        for at in range(size):
            slot = first + at
            near[at, :planes] = cut(tile, jnp.where(even, own[slot, 1], far[slot, 1]), pixels)
            cross[at, :planes] = cut(tile, jnp.where(even, far[slot, 1], own[slot, 1]), pixels)
            live = jnp.where(slot < counts[0], 1.0, 0.0).astype(F32)
            target = (measured[slot] * live).reshape(-1, rows, pixels)
            near[at, planes:] = target
            cross[at, planes:] = target


def add_kernel(pixels, groups, own, middle, far, *refs):
    parts, before, out = refs[: len(groups)], refs[len(groups) : -1], refs[-1]
    rows = out.shape[1]
    even = is_even(own, rows)
    out[...] = before[0][...] if before else jnp.zeros_like(out)
    lane = lax.broadcasted_iota(jnp.int32, (1, 1, pixels), 2)
    for (kind, first), strips in zip(groups, parts):

        def add(at, carry, kind=kind, first=first, strips=strips):
            slot = first + at
            if kind == "mid":
                column = middle[slot, 1]
            elif kind == "near":
                column = jnp.where(even, own[slot, 1], far[slot, 1])
            else:
                column = jnp.where(even, far[slot, 1], own[slot, 1])
            base, shift = place(column, out.shape[-1], pixels)
            part = strips[at]
            turned = pltpu.roll(part.reshape(-1, pixels), lax.rem(shift, pixels), 1).reshape(part.shape)
            out[:, :, pl.ds(base, pixels)] += jnp.where(lane >= shift, turned, 0.0)
            out[:, :, pl.ds(pl.multiple_of(base + pixels, pixels), pixels)] += jnp.where(
                lane < shift, turned, 0.0
            )
            return carry

        lax.fori_loop(0, strips.shape[0], add, 0)


def slot_kernel(
    first, offsets, tile, near, cross, probe, prop, tables, so_far,
    out_near, out_mid, out_cross, total, *refs,
):
    shares, (window, patch, grads, exit_wave, far) = refs[:-5], refs[-5:]
    size = near.shape[0]
    modes, _, pixels, _ = probe.shape
    planes, rows, _ = tile.shape
    even = jnp.logical_not(is_even(offsets, rows))
    total[...] = so_far[...]
    held = [(s, m) for s in range(BATCH) for m in range(modes)]

    def is_live(at):
        return jnp.max(jnp.where(even, cross[at, planes, :8], near[at, planes, :8])) > 0.0

    def leave(slots):
        for at in slots:
            for out in (out_near, out_mid, out_cross):
                out[at] = jnp.zeros(out.shape[1:], F32)

    def visit(slots):
        starts = [lax.rem(offsets[first + at, 0], rows) for at in slots]
        live = [jnp.where(is_live(at), 1.0, 0.0).astype(F32) for at in slots]
        for s, at in enumerate(slots):
            window[:, :rows] = jnp.where(even, cross[at, :planes], near[at, :planes])
            window[:, rows : 2 * rows] = cut(tile, offsets[first + at, 1], pixels)
            window[:, 2 * rows :] = jnp.where(even, near[at, :planes], cross[at, :planes])
            patch[s] = window[:, pl.ds(starts[s], pixels), :]
            total[2 * modes] += live[s] * (patch[s, 0] * patch[s, 0] + patch[s, 1] * patch[s, 1])
        waves = [times((probe[m, 0], probe[m, 1]), (patch[s, 0], patch[s, 1])) for s, m in held]
        waves = transform(tables, False, waves)
        waves = [times((prop[0], prop[1]), wave) for wave in waves]
        waves = transform(tables, True, waves)
        for (s, m), wave in zip(held, waves):
            exit_wave[s, m, 0], exit_wave[s, m, 1] = wave
        waves = [times(wave, (patch[s, 2], patch[s, 3])) for (s, m), wave in zip(held, waves)]
        waves = transform(tables, False, waves)
        intensity = [jnp.zeros((pixels, pixels), F32)] * BATCH
        for (s, m), wave in zip(held, waves):
            far[s, m, 0], far[s, m, 1] = wave
            intensity[s] = intensity[s] + wave[0] * wave[0] + wave[1] * wave[1]
        target = [
            jnp.where(even, cross[at, planes:], near[at, planes:]).reshape(pixels, pixels) for at in slots
        ]
        misfit = [2.0 * live[s] * (intensity[s] - target[s]) for s in range(BATCH)]
        waves = [(misfit[s] * far[s, m, 0], misfit[s] * far[s, m, 1]) for s, m in held]
        waves = transform(tables, True, waves)
        grads[...] = jnp.zeros_like(grads)
        for (s, m), wave in zip(held, waves):
            re, im = conj_times((exit_wave[s, m, 0], exit_wave[s, m, 1]), wave)
            grads[s, 2] += re
            grads[s, 3] += im
        waves = [conj_times((patch[s, 2], patch[s, 3]), wave) for (s, m), wave in zip(held, waves)]
        waves = transform(tables, False, waves)
        waves = [conj_times((prop[0], prop[1]), wave) for wave in waves]
        waves = transform(tables, True, waves)
        for (s, m), wave in zip(held, waves):
            re, im = conj_times((patch[s, 0], patch[s, 1]), wave)
            total[2 * m] += re
            total[2 * m + 1] += im
            re, im = conj_times((probe[m, 0], probe[m, 1]), wave)
            grads[s, 0] += re
            grads[s, 1] += im
        for s, at in enumerate(slots):
            window[...] = jnp.zeros_like(window)
            window[:, pl.ds(starts[s], pixels), :] = grads[s]
            out_near[at] = jnp.where(even, window[:, 2 * rows :], window[:, :rows])
            out_mid[at] = window[:, rows : 2 * rows]
            out_cross[at] = jnp.where(even, window[:, :rows], window[:, 2 * rows :])

    def step(index, carry):
        slots = [index * BATCH + s for s in range(BATCH)]
        some = is_live(slots[0])
        pl.when(some)(lambda: visit(slots))
        pl.when(jnp.logical_not(some))(lambda: leave(slots))
        return carry

    lax.fori_loop(0, size // BATCH, step, 0)

    if shares:
        own, other = shares
        chips, _, share, _ = own.shape
        core = jnp.where(even, 0, 1)
        for chip in range(chips):
            for plane in range(2 * modes + 1):
                own[chip, plane] = total[plane, pl.ds((2 * chip + core) * share, share)]
                other[chip, plane] = total[plane, pl.ds((2 * chip + 1 - core) * share, share)]


def step_kernel(parts, out):
    summed = parts[0]
    for at in range(1, parts.shape[0]):
        summed = summed + parts[at]
    step = summed[:-1] / (summed[-1:] + 1.0)
    for at in range(out.shape[0]):
        out[at] = step


def order_kernel(rows, offsets, own, other, out):
    chips, _, share, _ = own.shape
    core = jnp.where(is_even(offsets, rows), 0, 1)
    for chip in range(chips):
        out[:, pl.ds((2 * chip + core) * share, share)] = own[chip]
        out[:, pl.ds((2 * chip + 1 - core) * share, share)] = other[chip]


def in_smem():
    return pl.BlockSpec(memory_space=pltpu.SMEM)


def in_vmem():
    return pl.BlockSpec(memory_space=pltpu.VMEM)


def local(object_slices, probe_modes, propagator_phase, measured, offsets, counts):
    slices, _, tile_rows, columns = object_slices.shape
    modes, _, pixels, _ = probe_modes.shape
    planes = 2 * slices
    peers = lax.axis_size("row")
    params = pltpu.CompilerParams(vmem_limit_bytes=VMEM_LIMIT)
    tile = object_slices.reshape(planes, tile_rows, columns)
    starts = [sum(CHUNKS[:i]) for i in range(len(CHUNKS))]

    pair = [(i, i ^ 1) for i in range(peers)]
    other_pair = [(i, (i - 1) % peers if i % 2 == 0 else (i + 1) % peers) for i in range(peers)]
    far = shifted(offsets, "row", 2)
    middle = shifted(offsets, "row", 1)

    def strips(chunks):
        shapes = []
        for _, size in chunks:
            message = (size, planes + pixels // tile_rows, tile_rows, pixels)
            shapes += [jax.ShapeDtypeStruct(message, F32)] * 2
        outs = pl.pallas_call(
            functools.partial(cut_kernel, pixels, chunks),
            out_shape=shapes,
            in_specs=[in_smem()] * 3 + [in_vmem()] * 2,
            out_specs=[in_vmem()] * len(shapes),
            compiler_params=params,
            cost_estimate=pl.CostEstimate(flops=0, bytes_accessed=4 << 20, transcendentals=0),
        )(offsets, far, counts, tile, measured)
        return list(zip(outs[::2], outs[1::2]))

    chunks = list(zip(starts, CHUNKS))
    near, cross = [], []
    for to_near, to_cross in strips(chunks[:1]) + strips(chunks[1:]):
        if near:
            to_near, to_cross, _, _ = lax.optimization_barrier((to_near, to_cross, near[-1], cross[-1]))
        cross.append(lax.ppermute(to_cross, "row", other_pair))
        near.append(lax.ppermute(to_near, "row", pair))
    prop = jnp.stack([jnp.cos(propagator_phase), jnp.sin(propagator_phase)])
    tables = jnp.asarray(fourier_tables(pixels))

    share = pixels // peers
    total = jnp.zeros((2 * modes + 1, pixels, pixels), F32)
    mid, back_near, back_cross = [], [], []
    for index, (first, size) in enumerate(zip(starts, CHUNKS)):
        if index >= 2:
            total, back_near[index - 2], back_cross[index - 2] = lax.optimization_barrier(
                (total, back_near[index - 2], back_cross[index - 2])
            )
        strip = jax.ShapeDtypeStruct((size, planes, tile_rows, pixels), F32)
        part = jax.ShapeDtypeStruct((peers // 2, 2 * modes + 1, share, pixels), F32)
        shares = [part, part] if index == len(CHUNKS) - 1 else []
        field = pltpu.VMEM((BATCH, planes, pixels, pixels), F32)
        kept = pltpu.VMEM((BATCH, modes, 2, pixels, pixels), F32)
        to_near, to_mid, to_cross, total, *shares = pl.pallas_call(
            functools.partial(slot_kernel, first),
            out_shape=[strip, strip, strip, jax.ShapeDtypeStruct(total.shape, F32)] + shares,
            in_specs=[in_smem()] + [in_vmem()] * 7,
            out_specs=[in_vmem()] * (4 + len(shares)),
            scratch_shapes=[pltpu.VMEM((planes, 3 * tile_rows, pixels), F32), field, field, kept, kept],
            compiler_params=params,
            cost_estimate=pl.CostEstimate(
                flops=size * 6 * modes * 3 * 16 * pixels**3, bytes_accessed=8 << 20, transcendentals=0
            ),
        )(middle, tile, near[index], cross[index], probe_modes, prop, tables, total)
        mid.append(to_mid)
        back_near.append(lax.ppermute(to_near, "row", pair))
        back_cross.append(lax.ppermute(to_cross, "row", other_pair))

    def added(groups, strips, *before):
        return pl.pallas_call(
            functools.partial(add_kernel, pixels, groups),
            out_shape=jax.ShapeDtypeStruct(tile.shape, F32),
            in_specs=[in_smem()] * 3 + [in_vmem()] * (len(strips) + len(before)),
            out_specs=in_vmem(),
            compiler_params=params,
            input_output_aliases={3 + len(strips): 0} if before else {},
            cost_estimate=pl.CostEstimate(flops=0, bytes_accessed=5 << 20, transcendentals=0),
        )(offsets, middle, far, *strips, *before)

    cores = [list(range(core, peers, 2)) for core in range(2)]
    own, other = shares
    both = own + lax.ppermute(other, "row", pair)
    early = added(
        [("mid", first) for first in starts] + [(kind, first) for first in starts[:-1] for kind in ("near", "cross")],
        mid + [part for parts in zip(back_near[:-1], back_cross[:-1]) for part in parts],
    )
    both, early, last_near, last_cross = lax.optimization_barrier(
        (both, early, back_near[-1], back_cross[-1])
    )
    parts = lax.all_to_all(both, "row", 0, 0, axis_index_groups=cores)
    spread = pl.pallas_call(
        step_kernel,
        out_shape=jax.ShapeDtypeStruct((peers // 2, 2 * modes, share, pixels), F32),
        in_specs=[in_vmem()],
        out_specs=in_vmem(),
        compiler_params=params,
    )(parts)
    gathered = lax.all_to_all(spread, "row", 0, 0, axis_index_groups=cores)

    object_grad = added([("near", starts[-1]), ("cross", starts[-1])], [last_near, last_cross], early)
    object_grad = object_grad.reshape(object_slices.shape)

    probe_step = pl.pallas_call(
        functools.partial(order_kernel, tile_rows),
        out_shape=jax.ShapeDtypeStruct((2 * modes, pixels, pixels), F32),
        in_specs=[in_smem()] + [in_vmem()] * 2,
        out_specs=in_vmem(),
        compiler_params=params,
    )(offsets, gathered, lax.ppermute(gathered, "row", pair)).reshape(probe_modes.shape)
    return (object_grad, probe_step)


def solution(mesh):
    in_specs = (
        P(None, None, ("grp", "row"), None),
        P("grp", None, None, None),
        P(),
        P(("grp", "row"), None, None),
        P(("grp", "row"), None),
        P(("grp", "row")),
    )
    out_specs = (P(None, None, ("grp", "row"), None), P("grp", None, None, None))
    return jax.shard_map(local, mesh=mesh, in_specs=in_specs, out_specs=out_specs, check_vma=False)
```

```python
import functools

import jax
import jax.numpy as jnp
import numpy as np
from jax import lax
from jax.experimental import pallas as pl
from jax.experimental.pallas import tpu as pltpu
from jax.sharding import PartitionSpec as P

CHUNKS = (2, 4, 2)
BATCH = 2
VMEM_LIMIT = 48 * 1024 * 1024
F32 = jnp.float32
BF16 = jnp.bfloat16


def shifted(array, axis, by):
    peers = lax.axis_size(axis)
    return lax.ppermute(array, axis, [(i, (i + by) % peers) for i in range(peers)])


def fourier_tables(pixels):
    indices = np.arange(pixels)
    angles = 2.0 * np.pi * (indices[:, None] * indices[None, :] % pixels) / pixels
    re = np.cos(angles) / np.sqrt(pixels)
    im = -np.sin(angles) / np.sqrt(pixels)
    left = np.block([[re, -im], [im, re]]).astype(np.float32)
    high = left.astype(BF16)
    low = (left - high.astype(np.float32)).astype(BF16)
    return np.stack([high, low, high.T, low.T])


def pieces(array):
    high = array.astype(BF16)
    return high, (array - high.astype(F32)).astype(BF16)


def transform(tables, conj, waves):
    at_left, at_right = (2, 0) if conj else (0, 2)
    left = jnp.concatenate([tables[at_left], tables[at_left + 1], tables[at_left]], axis=1)
    right = jnp.concatenate([tables[at_right], tables[at_right], tables[at_right + 1]], axis=0)
    stacked = jnp.concatenate([jnp.concatenate(wave, axis=0) for wave in waves], axis=1)
    high, low = pieces(stacked)
    half = jnp.dot(left, jnp.concatenate([high, high, low], axis=0), preferred_element_type=F32)
    pixels = half.shape[0] // 2
    places = [i * pixels for i in range(len(waves))]
    turned = jnp.concatenate(
        [
            jnp.concatenate([half[:pixels, at : at + pixels], half[pixels:, at : at + pixels]], axis=1)
            for at in places
        ],
        axis=0,
    )
    high, low = pieces(turned)
    whole = jnp.dot(jnp.concatenate([high, low, high], axis=1), right, preferred_element_type=F32)
    return [(whole[at : at + pixels, :pixels], whole[at : at + pixels, pixels:]) for at in places]


def times(one, two):
    return one[0] * two[0] - one[1] * two[1], one[0] * two[1] + one[1] * two[0]


def conj_times(one, two):
    return one[0] * two[0] + one[1] * two[1], one[0] * two[1] - one[1] * two[0]


def place(column, columns, pixels):
    base = jnp.minimum(column // pixels * pixels, columns - 2 * pixels)
    return pl.multiple_of(base, pixels), column - base


def cut(tile, column, pixels):
    base, shift = place(column, tile.shape[-1], pixels)
    rows = tile.shape[1]
    wide = tile[:, :, pl.ds(base, 2 * pixels)].reshape(-1, 2 * pixels)
    turned = pltpu.roll(wide, 2 * pixels - shift, 1)
    return turned[:, :pixels].reshape(-1, rows, pixels)


def is_even(offsets, rows):
    return lax.rem(offsets[0, 0] // rows, 2) == 0


def cut_kernel(pixels, chunks, own, far, counts, tile, measured, *outs):
    planes, rows, _ = tile.shape
    even = is_even(own, rows)
    for (first, size), near, cross in zip(chunks, outs[::2], outs[1::2], strict=True):
        for at in range(size):
            slot = first + at
            strip = at * (planes + pixels // rows)
            near[strip : strip + planes] = cut(tile, jnp.where(even, own[slot, 1], far[slot, 1]), pixels)
            cross[strip : strip + planes] = cut(tile, jnp.where(even, far[slot, 1], own[slot, 1]), pixels)
            live = jnp.where(slot < counts[0], 1.0, 0.0).astype(F32)
            target = (measured[slot] * live).reshape(-1, rows, pixels)
            near[strip + planes : strip + planes + pixels // rows] = target
            cross[strip + planes : strip + planes + pixels // rows] = target


def add_kernel(pixels, groups, own, middle, far, *refs):
    parts, before, out = refs[: len(groups)], refs[len(groups) : -1], refs[-1]
    planes, rows, _ = out.shape
    even = is_even(own, rows)
    out[...] = before[0][...] if before else jnp.zeros_like(out)
    lane = lax.broadcasted_iota(jnp.int32, (1, 1, pixels), 2)
    for (kind, first, size, unit), strips in zip(groups, parts):

        def add(at, carry, kind=kind, first=first, unit=unit, strips=strips):
            slot = first + at
            if kind == "mid":
                column = middle[slot, 1]
            elif kind == "near":
                column = jnp.where(even, own[slot, 1], far[slot, 1])
            else:
                column = jnp.where(even, far[slot, 1], own[slot, 1])
            base, shift = place(column, out.shape[-1], pixels)
            part = strips[pl.ds(unit + at * planes, planes)]
            turned = pltpu.roll(part.reshape(-1, pixels), lax.rem(shift, pixels), 1).reshape(part.shape)
            out[:, :, pl.ds(base, pixels)] += jnp.where(lane >= shift, turned, 0.0)
            out[:, :, pl.ds(pl.multiple_of(base + pixels, pixels), pixels)] += jnp.where(
                lane < shift, turned, 0.0
            )
            return carry

        lax.fori_loop(0, size, add, 0)


def slot_kernel(
    first, size, ahead, offsets, tile, near, cross, probe, prop, tables, so_far, *refs
):
    given, refs = refs[:ahead], refs[ahead:]
    out_near, out_mid, out_cross, total, *shares = refs[:-5]
    window, patch, grads, exit_wave, far = refs[-5:]
    modes, _, pixels, _ = probe.shape
    planes, rows, _ = tile.shape
    each = planes + pixels // rows
    behind = given[0].shape[0] if given else 0
    for message, out in zip(given, (out_near, out_cross)):
        out[:behind] = message[...]
    even = jnp.logical_not(is_even(offsets, rows))
    total[...] = so_far[...]
    held = [(s, m) for s in range(BATCH) for m in range(modes)]

    def is_live(at):
        unit = at * each + planes
        return jnp.max(jnp.where(even, cross[unit, :8], near[unit, :8])) > 0.0

    def leave(slots):
        for at in slots:
            for out, unit in ((out_near, behind), (out_mid, 0), (out_cross, behind)):
                out[pl.ds(unit + at * planes, planes)] = jnp.zeros((planes, rows, pixels), F32)

    def visit(slots):
        starts = [lax.rem(offsets[first + at, 0], rows) for at in slots]
        live = [jnp.where(is_live(at), 1.0, 0.0).astype(F32) for at in slots]
        for s, at in enumerate(slots):
            strip = pl.ds(at * each, planes)
            window[:, :rows] = jnp.where(even, cross[strip], near[strip])
            window[:, rows : 2 * rows] = cut(tile, offsets[first + at, 1], pixels)
            window[:, 2 * rows :] = jnp.where(even, near[strip], cross[strip])
            patch[s] = window[:, pl.ds(starts[s], pixels), :]
            total[2 * modes] += live[s] * (patch[s, 0] * patch[s, 0] + patch[s, 1] * patch[s, 1])
        waves = [times((probe[m, 0], probe[m, 1]), (patch[s, 0], patch[s, 1])) for s, m in held]
        waves = transform(tables, False, waves)
        waves = [times((prop[0], prop[1]), wave) for wave in waves]
        waves = transform(tables, True, waves)
        for (s, m), wave in zip(held, waves):
            exit_wave[s, m, 0], exit_wave[s, m, 1] = wave
        waves = [times(wave, (patch[s, 2], patch[s, 3])) for (s, m), wave in zip(held, waves)]
        waves = transform(tables, False, waves)
        intensity = [jnp.zeros((pixels, pixels), F32)] * BATCH
        for (s, m), wave in zip(held, waves):
            far[s, m, 0], far[s, m, 1] = wave
            intensity[s] = intensity[s] + wave[0] * wave[0] + wave[1] * wave[1]
        units = [pl.ds(at * each + planes, each - planes) for at in slots]
        target = [jnp.where(even, cross[unit], near[unit]).reshape(pixels, pixels) for unit in units]
        misfit = [2.0 * live[s] * (intensity[s] - target[s]) for s in range(BATCH)]
        waves = [(misfit[s] * far[s, m, 0], misfit[s] * far[s, m, 1]) for s, m in held]
        waves = transform(tables, True, waves)
        grads[...] = jnp.zeros_like(grads)
        for (s, m), wave in zip(held, waves):
            re, im = conj_times((exit_wave[s, m, 0], exit_wave[s, m, 1]), wave)
            grads[s, 2] += re
            grads[s, 3] += im
        waves = [conj_times((patch[s, 2], patch[s, 3]), wave) for (s, m), wave in zip(held, waves)]
        waves = transform(tables, False, waves)
        waves = [conj_times((prop[0], prop[1]), wave) for wave in waves]
        waves = transform(tables, True, waves)
        for (s, m), wave in zip(held, waves):
            re, im = conj_times((patch[s, 0], patch[s, 1]), wave)
            total[2 * m] += re
            total[2 * m + 1] += im
            re, im = conj_times((probe[m, 0], probe[m, 1]), wave)
            grads[s, 0] += re
            grads[s, 1] += im
        for s, at in enumerate(slots):
            window[...] = jnp.zeros_like(window)
            window[:, pl.ds(starts[s], pixels), :] = grads[s]
            strip = pl.ds(behind + at * planes, planes)
            out_near[strip] = jnp.where(even, window[:, 2 * rows :], window[:, :rows])
            out_mid[pl.ds(at * planes, planes)] = window[:, rows : 2 * rows]
            out_cross[strip] = jnp.where(even, window[:, :rows], window[:, 2 * rows :])

    def step(index, carry):
        slots = [index * BATCH + s for s in range(BATCH)]
        some = is_live(slots[0])
        pl.when(some)(lambda: visit(slots))
        pl.when(jnp.logical_not(some))(lambda: leave(slots))
        return carry

    lax.fori_loop(0, size // BATCH, step, 0)

    if shares:
        own, other = shares
        chips, _, share, _ = own.shape
        core = jnp.where(even, 0, 1)
        for chip in range(chips):
            for plane in range(2 * modes + 1):
                own[chip, plane] = total[plane, pl.ds((2 * chip + core) * share, share)]
                other[chip, plane] = total[plane, pl.ds((2 * chip + 1 - core) * share, share)]


def step_kernel(parts, out):
    summed = parts[0]
    for at in range(1, parts.shape[0]):
        summed = summed + parts[at]
    step = summed[:-1] / (summed[-1:] + 1.0)
    for at in range(out.shape[0]):
        out[at] = step


def order_kernel(rows, offsets, own, other, out):
    chips, _, share, _ = own.shape
    core = jnp.where(is_even(offsets, rows), 0, 1)
    for chip in range(chips):
        out[:, pl.ds((2 * chip + core) * share, share)] = own[chip]
        out[:, pl.ds((2 * chip + 1 - core) * share, share)] = other[chip]


def in_smem():
    return pl.BlockSpec(memory_space=pltpu.SMEM)


def in_vmem():
    return pl.BlockSpec(memory_space=pltpu.VMEM)


def local(object_slices, probe_modes, propagator_phase, measured, offsets, counts):
    slices, _, tile_rows, columns = object_slices.shape
    modes, _, pixels, _ = probe_modes.shape
    planes = 2 * slices
    peers = lax.axis_size("row")
    params = pltpu.CompilerParams(vmem_limit_bytes=VMEM_LIMIT)
    tile = object_slices.reshape(planes, tile_rows, columns)
    starts = [sum(CHUNKS[:i]) for i in range(len(CHUNKS))]

    pair = [(i, i ^ 1) for i in range(peers)]
    other_pair = [(i, (i - 1) % peers if i % 2 == 0 else (i + 1) % peers) for i in range(peers)]
    far = shifted(offsets, "row", 2)
    middle = shifted(offsets, "row", 1)

    each = planes + pixels // tile_rows

    def units(count):
        return jax.ShapeDtypeStruct((count, tile_rows, pixels), F32)

    def strips(chunks):
        shapes = [units(size * each) for _, size in chunks for _ in range(2)]
        outs = pl.pallas_call(
            functools.partial(cut_kernel, pixels, chunks),
            out_shape=shapes,
            in_specs=[in_smem()] * 3 + [in_vmem()] * 2,
            out_specs=[in_vmem()] * len(shapes),
            compiler_params=params,
            cost_estimate=pl.CostEstimate(flops=0, bytes_accessed=4 << 20, transcendentals=0),
        )(offsets, far, counts, tile, measured)
        return list(zip(outs[::2], outs[1::2]))

    def swapped(to_near, to_cross):
        return lax.ppermute(to_near, "row", pair), lax.ppermute(to_cross, "row", other_pair)

    chunks = list(zip(starts, CHUNKS))
    waiting = strips(chunks[:1]) + strips(chunks[1:])
    arrived = [swapped(*message) for message in waiting[:2]]
    prop = jnp.stack([jnp.cos(propagator_phase), jnp.sin(propagator_phase)])
    tables = jnp.asarray(fourier_tables(pixels))

    share = pixels // peers
    total = jnp.zeros((2 * modes + 1, pixels, pixels), F32)
    mid, back = [], []
    for index, (first, size) in enumerate(chunks):
        given = waiting[index + 2] if index + 2 < len(chunks) else ()
        ahead = CHUNKS[index + 2] * each if given else 0
        part = jax.ShapeDtypeStruct((peers // 2, 2 * modes + 1, share, pixels), F32)
        shares = [part, part] if index == len(CHUNKS) - 1 else []
        message = units(ahead + size * planes)
        field = pltpu.VMEM((BATCH, planes, pixels, pixels), F32)
        kept = pltpu.VMEM((BATCH, modes, 2, pixels, pixels), F32)
        to_near, to_mid, to_cross, total, *shares = pl.pallas_call(
            functools.partial(slot_kernel, first, size, len(given)),
            out_shape=[message, units(size * planes), message, jax.ShapeDtypeStruct(total.shape, F32)] + shares,
            in_specs=[in_smem()] + [in_vmem()] * (7 + len(given)),
            out_specs=[in_vmem()] * (4 + len(shares)),
            scratch_shapes=[pltpu.VMEM((planes, 3 * tile_rows, pixels), F32), field, field, kept, kept],
            compiler_params=params,
            cost_estimate=pl.CostEstimate(
                flops=size * 6 * modes * 3 * 16 * pixels**3, bytes_accessed=8 << 20, transcendentals=0
            ),
        )(middle, tile, *arrived[index], probe_modes, prop, tables, total, *given)
        mid.append((("mid", first, size, 0), to_mid))
        message = swapped(to_near, to_cross)
        if given:
            arrived.append(message)
        back.append([((kind, first, size, ahead), part) for kind, part in zip(("near", "cross"), message)])

    def added(groups, strips, *before):
        return pl.pallas_call(
            functools.partial(add_kernel, pixels, groups),
            out_shape=jax.ShapeDtypeStruct(tile.shape, F32),
            in_specs=[in_smem()] * 3 + [in_vmem()] * (len(strips) + len(before)),
            out_specs=in_vmem(),
            compiler_params=params,
            input_output_aliases={3 + len(strips): 0} if before else {},
            cost_estimate=pl.CostEstimate(flops=0, bytes_accessed=5 << 20, transcendentals=0),
        )(offsets, middle, far, *strips, *before)

    cores = [list(range(core, peers, 2)) for core in range(2)]
    own, other = shares
    both = own + lax.ppermute(other, "row", pair)
    early = added(*zip(*(mid + [part for parts in back[:-1] for part in parts])))
    last_groups, last_strips = zip(*back[-1])
    both, early, last_strips = lax.optimization_barrier((both, early, last_strips))
    parts = lax.all_to_all(both, "row", 0, 0, axis_index_groups=cores)
    spread = pl.pallas_call(
        step_kernel,
        out_shape=jax.ShapeDtypeStruct((peers // 2, 2 * modes, share, pixels), F32),
        in_specs=[in_vmem()],
        out_specs=in_vmem(),
        compiler_params=params,
    )(parts)
    gathered = lax.all_to_all(spread, "row", 0, 0, axis_index_groups=cores)

    object_grad = added(last_groups, last_strips, early)
    object_grad = object_grad.reshape(object_slices.shape)

    probe_step = pl.pallas_call(
        functools.partial(order_kernel, tile_rows),
        out_shape=jax.ShapeDtypeStruct((2 * modes, pixels, pixels), F32),
        in_specs=[in_smem()] + [in_vmem()] * 2,
        out_specs=in_vmem(),
        compiler_params=params,
    )(offsets, gathered, lax.ppermute(gathered, "row", pair)).reshape(probe_modes.shape)
    return (object_grad, probe_step)


def solution(mesh):
    in_specs = (
        P(None, None, ("grp", "row"), None),
        P("grp", None, None, None),
        P(),
        P(("grp", "row"), None, None),
        P(("grp", "row"), None),
        P(("grp", "row")),
    )
    out_specs = (P(None, None, ("grp", "row"), None), P("grp", None, None, None))
    return jax.shard_map(local, mesh=mesh, in_specs=in_specs, out_specs=out_specs, check_vma=False)
```

```python
import functools

import jax
import jax.numpy as jnp
import numpy as np
from jax import lax
from jax.experimental import pallas as pl
from jax.experimental.pallas import tpu as pltpu
from jax.sharding import PartitionSpec as P

CHUNKS = (2, 4, 2)
BATCH = 2
VMEM_LIMIT = 48 * 1024 * 1024
F32 = jnp.float32
BF16 = jnp.bfloat16


def shifted(array, axis, by):
    peers = lax.axis_size(axis)
    return lax.ppermute(array, axis, [(i, (i + by) % peers) for i in range(peers)])


def fourier_tables(pixels):
    indices = np.arange(pixels)
    angles = 2.0 * np.pi * (indices[:, None] * indices[None, :] % pixels) / pixels
    re = np.cos(angles) / np.sqrt(pixels)
    im = -np.sin(angles) / np.sqrt(pixels)
    left = np.block([[re, -im], [im, re]]).astype(np.float32)
    high = left.astype(BF16)
    low = (left - high.astype(np.float32)).astype(BF16)
    return np.stack([high, low, high.T, low.T])


def pieces(array):
    high = array.astype(BF16)
    return high, (array - high.astype(F32)).astype(BF16)


def transform(tables, conj, groups):
    at_left, at_right = (2, 0) if conj else (0, 2)
    left = jnp.concatenate([tables[at_left], tables[at_left + 1], tables[at_left]], axis=1)
    right = jnp.concatenate([tables[at_right], tables[at_right], tables[at_right + 1]], axis=0)
    pixels = left.shape[0] // 2
    halves = []
    for waves in groups:
        stacked = jnp.concatenate([jnp.concatenate(wave, axis=0) for wave in waves], axis=1)
        high, low = pieces(stacked)
        half = jnp.dot(left, jnp.concatenate([high, high, low], axis=0), preferred_element_type=F32)
        turned = [
            jnp.concatenate([half[:pixels, at : at + pixels], half[pixels:, at : at + pixels]], axis=1)
            for at in range(0, half.shape[1], pixels)
        ]
        halves.append(pieces(jnp.concatenate(turned, axis=0)))
    wholes = []
    for high, low in halves:
        whole = jnp.dot(jnp.concatenate([high, low, high], axis=1), right, preferred_element_type=F32)
        wholes.append(
            [
                (whole[at : at + pixels, :pixels], whole[at : at + pixels, pixels:])
                for at in range(0, whole.shape[0], pixels)
            ]
        )
    return wholes


def times(one, two):
    return one[0] * two[0] - one[1] * two[1], one[0] * two[1] + one[1] * two[0]


def conj_times(one, two):
    return one[0] * two[0] + one[1] * two[1], one[0] * two[1] - one[1] * two[0]


def place(column, columns, pixels):
    base = jnp.minimum(column // pixels * pixels, columns - 2 * pixels)
    return pl.multiple_of(base, pixels), column - base


def cut(tile, column, pixels):
    base, shift = place(column, tile.shape[-1], pixels)
    rows = tile.shape[1]
    wide = tile[:, :, pl.ds(base, 2 * pixels)].reshape(-1, 2 * pixels)
    turned = pltpu.roll(wide, 2 * pixels - shift, 1)
    return turned[:, :pixels].reshape(-1, rows, pixels)


def is_even(offsets, rows):
    return lax.rem(offsets[0, 0] // rows, 2) == 0


def cut_kernel(pixels, chunks, own, far, counts, tile, measured, *outs):
    planes, rows, _ = tile.shape
    even = is_even(own, rows)
    for (first, size), near, cross in zip(chunks, outs[::2], outs[1::2], strict=True):
        for at in range(size):
            slot = first + at
            strip = at * (planes + pixels // rows)
            near[strip : strip + planes] = cut(tile, jnp.where(even, own[slot, 1], far[slot, 1]), pixels)
            cross[strip : strip + planes] = cut(tile, jnp.where(even, far[slot, 1], own[slot, 1]), pixels)
            live = jnp.where(slot < counts[0], 1.0, 0.0).astype(F32)
            target = (measured[slot] * live).reshape(-1, rows, pixels)
            near[strip + planes : strip + planes + pixels // rows] = target
            cross[strip + planes : strip + planes + pixels // rows] = target
        if first == 0:
            for slot in range(measured.shape[0]):
                for entry in range(2):
                    line = jnp.full((1, pixels), own[slot, entry], jnp.int32).astype(F32)
                    near[near.shape[0] - 1, 2 * slot + entry : 2 * slot + entry + 1] = line
                    cross[cross.shape[0] - 1, 2 * slot + entry : 2 * slot + entry + 1] = line


def add_kernel(pixels, groups, own, middle, far, *refs):
    parts, before, out = refs[: len(groups)], refs[len(groups) : -1], refs[-1]
    planes, rows, _ = out.shape
    even = is_even(own, rows)
    out[...] = before[0][...] if before else jnp.zeros_like(out)
    lane = lax.broadcasted_iota(jnp.int32, (1, 1, pixels), 2)
    for (kind, first, size, unit), strips in zip(groups, parts):

        def add(at, carry, kind=kind, first=first, unit=unit, strips=strips):
            slot = first + at
            if kind == "mid":
                column = middle[slot, 1]
            elif kind == "near":
                column = jnp.where(even, own[slot, 1], far[slot, 1])
            else:
                column = jnp.where(even, far[slot, 1], own[slot, 1])
            base, shift = place(column, out.shape[-1], pixels)
            part = strips[pl.ds(unit + at * planes, planes)]
            turned = pltpu.roll(part.reshape(-1, pixels), lax.rem(shift, pixels), 1).reshape(part.shape)
            out[:, :, pl.ds(base, pixels)] += jnp.where(lane >= shift, turned, 0.0)
            out[:, :, pl.ds(pl.multiple_of(base + pixels, pixels), pixels)] += jnp.where(
                lane < shift, turned, 0.0
            )
            return carry

        lax.fori_loop(0, size, add, 0)


def slot_kernel(
    first, size, ahead, own_offsets, *refs
):
    if first == 0:
        offsets, refs = refs[-6], refs[:-6] + refs[-5:]
    else:
        offsets, *refs = refs
    tile, near, cross, probe, prop, tables, so_far, *refs = refs
    given, refs = refs[:ahead], refs[ahead:]
    out_near, out_mid, out_cross, total, *shares = refs[:-5]
    window, patch, grads, exit_wave, far = refs[-5:]
    modes, _, pixels, _ = probe.shape
    planes, rows, _ = tile.shape
    each = planes + pixels // rows
    behind = given[0].shape[0] if given else 0
    for message, out in zip(given, (out_near, out_cross)):
        out[:behind] = message[...]
    even = is_even(own_offsets, rows)
    if first == 0:
        for slot in range(offsets.shape[0]):
            for entry in range(2):
                line = pl.ds(2 * slot + entry, 1)
                value = jnp.where(even, cross[cross.shape[0] - 1, line], near[near.shape[0] - 1, line])
                offsets[slot, entry] = jnp.max(value).astype(jnp.int32)
    total[...] = so_far[...]
    held = range(BATCH)

    def is_live(at):
        unit = at * each + planes
        return jnp.max(jnp.where(even, cross[unit, :8], near[unit, :8])) > 0.0

    def leave(slots):
        for at in slots:
            for out, unit in ((out_near, behind), (out_mid, 0), (out_cross, behind)):
                out[pl.ds(unit + at * planes, planes)] = jnp.zeros((planes, rows, pixels), F32)

    def visit(slots):
        starts = [lax.rem(offsets[first + at, 0], rows) for at in slots]
        live = [jnp.where(is_live(at), 1.0, 0.0).astype(F32) for at in slots]
        for s, at in enumerate(slots):
            strip = pl.ds(at * each, planes)
            window[:, :rows] = jnp.where(even, cross[strip], near[strip])
            window[:, rows : 2 * rows] = cut(tile, offsets[first + at, 1], pixels)
            window[:, 2 * rows :] = jnp.where(even, near[strip], cross[strip])
            patch[s] = window[:, pl.ds(starts[s], pixels), :]
            total[2 * modes] += live[s] * (patch[s, 0] * patch[s, 0] + patch[s, 1] * patch[s, 1])
        all_modes = range(modes)
        groups = [
            [times((probe[m, 0], probe[m, 1]), (patch[s, 0], patch[s, 1])) for m in all_modes] for s in held
        ]
        groups = transform(tables, False, groups)
        groups = [[times((prop[0], prop[1]), wave) for wave in waves] for waves in groups]
        groups = transform(tables, True, groups)
        for s in held:
            for m in all_modes:
                exit_wave[s, m, 0], exit_wave[s, m, 1] = groups[s][m]
            groups[s] = [times(wave, (patch[s, 2], patch[s, 3])) for wave in groups[s]]
        groups = transform(tables, False, groups)
        for s, at in enumerate(slots):
            intensity = jnp.zeros((pixels, pixels), F32)
            for m in all_modes:
                wave = groups[s][m]
                far[s, m, 0], far[s, m, 1] = wave
                intensity = intensity + wave[0] * wave[0] + wave[1] * wave[1]
            unit = pl.ds(at * each + planes, each - planes)
            target = jnp.where(even, cross[unit], near[unit]).reshape(pixels, pixels)
            misfit = 2.0 * live[s] * (intensity - target)
            groups[s] = [(misfit * far[s, m, 0], misfit * far[s, m, 1]) for m in all_modes]
        groups = transform(tables, True, groups)
        for s in held:
            grad_re, grad_im = jnp.zeros((pixels, pixels), F32), jnp.zeros((pixels, pixels), F32)
            for m in all_modes:
                re, im = conj_times((exit_wave[s, m, 0], exit_wave[s, m, 1]), groups[s][m])
                grad_re, grad_im = grad_re + re, grad_im + im
            grads[s, 2], grads[s, 3] = grad_re, grad_im
            groups[s] = [conj_times((patch[s, 2], patch[s, 3]), wave) for wave in groups[s]]
        groups = transform(tables, False, groups)
        groups = [[conj_times((prop[0], prop[1]), wave) for wave in waves] for waves in groups]
        groups = transform(tables, True, groups)
        for s in held:
            grad_re, grad_im = jnp.zeros((pixels, pixels), F32), jnp.zeros((pixels, pixels), F32)
            for m in all_modes:
                re, im = conj_times((patch[s, 0], patch[s, 1]), groups[s][m])
                total[2 * m] += re
                total[2 * m + 1] += im
                re, im = conj_times((probe[m, 0], probe[m, 1]), groups[s][m])
                grad_re, grad_im = grad_re + re, grad_im + im
            grads[s, 0], grads[s, 1] = grad_re, grad_im
        for s, at in enumerate(slots):
            window[...] = jnp.zeros_like(window)
            window[:, pl.ds(starts[s], pixels), :] = grads[s]
            strip = pl.ds(behind + at * planes, planes)
            out_near[strip] = jnp.where(even, window[:, 2 * rows :], window[:, :rows])
            out_mid[pl.ds(at * planes, planes)] = window[:, rows : 2 * rows]
            out_cross[strip] = jnp.where(even, window[:, :rows], window[:, 2 * rows :])

    def step(index, carry):
        slots = [index * BATCH + s for s in range(BATCH)]
        some = is_live(slots[0])
        pl.when(some)(lambda: visit(slots))
        pl.when(jnp.logical_not(some))(lambda: leave(slots))
        return carry

    lax.fori_loop(0, size // BATCH, step, 0)

    if shares:
        own, other = shares
        chips, _, share, _ = own.shape
        core = jnp.where(even, 0, 1)
        for chip in range(chips):
            for plane in range(2 * modes + 1):
                own[chip, plane] = total[plane, pl.ds((2 * chip + core) * share, share)]
                other[chip, plane] = total[plane, pl.ds((2 * chip + 1 - core) * share, share)]


def step_kernel(parts, out):
    summed = parts[0]
    for at in range(1, parts.shape[0]):
        summed = summed + parts[at]
    step = summed[:-1] / (summed[-1:] + 1.0)
    for at in range(out.shape[0]):
        out[at] = step


def order_kernel(rows, offsets, own, other, out):
    chips, _, share, _ = own.shape
    core = jnp.where(is_even(offsets, rows), 0, 1)
    for chip in range(chips):
        out[:, pl.ds((2 * chip + core) * share, share)] = own[chip]
        out[:, pl.ds((2 * chip + 1 - core) * share, share)] = other[chip]


def in_smem():
    return pl.BlockSpec(memory_space=pltpu.SMEM)


def in_vmem():
    return pl.BlockSpec(memory_space=pltpu.VMEM)


def local(object_slices, probe_modes, propagator_phase, measured, offsets, counts):
    slices, _, tile_rows, columns = object_slices.shape
    modes, _, pixels, _ = probe_modes.shape
    planes = 2 * slices
    peers = lax.axis_size("row")
    params = pltpu.CompilerParams(vmem_limit_bytes=VMEM_LIMIT)
    tile = object_slices.reshape(planes, tile_rows, columns)
    starts = [sum(CHUNKS[:i]) for i in range(len(CHUNKS))]

    pair = [(i, i ^ 1) for i in range(peers)]
    other_pair = [(i, (i - 1) % peers if i % 2 == 0 else (i + 1) % peers) for i in range(peers)]
    far = shifted(offsets, "row", 2)

    each = planes + pixels // tile_rows

    def units(count):
        return jax.ShapeDtypeStruct((count, tile_rows, pixels), F32)

    def strips(chunks):
        shapes = [units(size * each + (first == 0)) for first, size in chunks for _ in range(2)]
        outs = pl.pallas_call(
            functools.partial(cut_kernel, pixels, chunks),
            out_shape=shapes,
            in_specs=[in_smem()] * 3 + [in_vmem()] * 2,
            out_specs=[in_vmem()] * len(shapes),
            compiler_params=params,
            cost_estimate=pl.CostEstimate(flops=0, bytes_accessed=4 << 20, transcendentals=0),
        )(offsets, far, counts, tile, measured)
        return list(zip(outs[::2], outs[1::2]))

    def swapped(to_near, to_cross):
        return lax.ppermute(to_near, "row", pair), lax.ppermute(to_cross, "row", other_pair)

    chunks = list(zip(starts, CHUNKS))
    waiting = strips(chunks[:1]) + strips(chunks[1:])
    arrived = [swapped(*message) for message in waiting[:2]]
    prop = jnp.stack([jnp.cos(propagator_phase), jnp.sin(propagator_phase)])
    tables = jnp.asarray(fourier_tables(pixels))

    share = pixels // peers
    total = jnp.zeros((2 * modes + 1, pixels, pixels), F32)
    mid, back, places = [], [], [offsets]
    for index, (first, size) in enumerate(chunks):
        given = waiting[index + 2] if index + 2 < len(chunks) else ()
        ahead = CHUNKS[index + 2] * each if given else 0
        part = jax.ShapeDtypeStruct((peers // 2, 2 * modes + 1, share, pixels), F32)
        shares = [part, part] if index == len(CHUNKS) - 1 else []
        message = units(ahead + size * planes)
        field = pltpu.VMEM((BATCH, planes, pixels, pixels), F32)
        kept = pltpu.VMEM((BATCH, modes, 2, pixels, pixels), F32)
        to_near, to_mid, to_cross, total, *shares = pl.pallas_call(
            functools.partial(slot_kernel, first, size, len(given)),
            out_shape=[message, units(size * planes), message, jax.ShapeDtypeStruct(total.shape, F32)]
            + shares
            + ([] if index else [jax.ShapeDtypeStruct(offsets.shape, jnp.int32)]),
            in_specs=[in_smem()] * len(places) + [in_vmem()] * (7 + len(given)),
            out_specs=[in_vmem()] * (4 + len(shares)) + ([] if index else [in_smem()]),
            scratch_shapes=[pltpu.VMEM((planes, 3 * tile_rows, pixels), F32), field, field, kept, kept],
            compiler_params=params,
            cost_estimate=pl.CostEstimate(
                flops=size * 6 * modes * 3 * 16 * pixels**3, bytes_accessed=8 << 20, transcendentals=0
            ),
        )(*places, tile, *arrived[index], probe_modes, prop, tables, total, *given)
        if index == 0:
            middle = shares.pop()
            places.append(middle)
        mid.append((("mid", first, size, 0), to_mid))
        message = swapped(to_near, to_cross)
        if given:
            arrived.append(message)
        back.append([((kind, first, size, ahead), part) for kind, part in zip(("near", "cross"), message)])

    def added(groups, strips, *before):
        return pl.pallas_call(
            functools.partial(add_kernel, pixels, groups),
            out_shape=jax.ShapeDtypeStruct(tile.shape, F32),
            in_specs=[in_smem()] * 3 + [in_vmem()] * (len(strips) + len(before)),
            out_specs=in_vmem(),
            compiler_params=params,
            input_output_aliases={3 + len(strips): 0} if before else {},
            cost_estimate=pl.CostEstimate(flops=0, bytes_accessed=5 << 20, transcendentals=0),
        )(offsets, middle, far, *strips, *before)

    cores = [list(range(core, peers, 2)) for core in range(2)]
    own, other = shares
    both = own + lax.ppermute(other, "row", pair)
    early = added(*zip(*(mid + [part for parts in back[:-1] for part in parts])))
    last_groups, last_strips = zip(*back[-1])
    both, early, last_strips = lax.optimization_barrier((both, early, last_strips))
    parts = lax.all_to_all(both, "row", 0, 0, axis_index_groups=cores)
    spread = pl.pallas_call(
        step_kernel,
        out_shape=jax.ShapeDtypeStruct((peers // 2, 2 * modes, share, pixels), F32),
        in_specs=[in_vmem()],
        out_specs=in_vmem(),
        compiler_params=params,
    )(parts)
    gathered = lax.all_to_all(spread, "row", 0, 0, axis_index_groups=cores)

    object_grad = added(last_groups, last_strips, early)
    object_grad = object_grad.reshape(object_slices.shape)

    probe_step = pl.pallas_call(
        functools.partial(order_kernel, tile_rows),
        out_shape=jax.ShapeDtypeStruct((2 * modes, pixels, pixels), F32),
        in_specs=[in_smem()] + [in_vmem()] * 2,
        out_specs=in_vmem(),
        compiler_params=params,
    )(offsets, gathered, lax.ppermute(gathered, "row", pair)).reshape(probe_modes.shape)
    return (object_grad, probe_step)


def solution(mesh):
    in_specs = (
        P(None, None, ("grp", "row"), None),
        P("grp", None, None, None),
        P(),
        P(("grp", "row"), None, None),
        P(("grp", "row"), None),
        P(("grp", "row")),
    )
    out_specs = (P(None, None, ("grp", "row"), None), P("grp", None, None, None))
    return jax.shard_map(local, mesh=mesh, in_specs=in_specs, out_specs=out_specs, check_vma=False)
```

```python
import functools

import jax
import jax.numpy as jnp
import numpy as np
from jax import lax
from jax.experimental import pallas as pl
from jax.experimental.pallas import tpu as pltpu
from jax.sharding import PartitionSpec as P

CHUNKS = (2, 4, 2)
BATCH = 2
VMEM_LIMIT = 48 * 1024 * 1024
F32 = jnp.float32
BF16 = jnp.bfloat16


def shifted(array, axis, by):
    peers = lax.axis_size(axis)
    return lax.ppermute(array, axis, [(i, (i + by) % peers) for i in range(peers)])


def fourier_tables(pixels):
    indices = np.arange(pixels)
    angles = 2.0 * np.pi * (indices[:, None] * indices[None, :] % pixels) / pixels
    re = np.cos(angles) / np.sqrt(pixels)
    im = -np.sin(angles) / np.sqrt(pixels)
    left = np.block([[re, -im], [im, re]]).astype(np.float32)
    high = left.astype(BF16)
    low = (left - high.astype(np.float32)).astype(BF16)
    return np.stack([high, low, high.T, low.T])


def pieces(array):
    high = array.astype(BF16)
    return high, (array - high.astype(F32)).astype(BF16)


def transform(tables, conj, groups):
    at_left, at_right = (2, 0) if conj else (0, 2)
    left = jnp.concatenate([tables[at_left], tables[at_left + 1], tables[at_left]], axis=1)
    right = jnp.concatenate([tables[at_right], tables[at_right], tables[at_right + 1]], axis=0)
    pixels = left.shape[0] // 2
    halves = []
    for waves in groups:
        stacked = jnp.concatenate([jnp.concatenate(wave, axis=0) for wave in waves], axis=1)
        high, low = pieces(stacked)
        half = jnp.dot(left, jnp.concatenate([high, high, low], axis=0), preferred_element_type=F32)
        turned = [
            jnp.concatenate([half[:pixels, at : at + pixels], half[pixels:, at : at + pixels]], axis=1)
            for at in range(0, half.shape[1], pixels)
        ]
        halves.append(pieces(jnp.concatenate(turned, axis=0)))
    wholes = []
    for high, low in halves:
        whole = jnp.dot(jnp.concatenate([high, low, high], axis=1), right, preferred_element_type=F32)
        wholes.append(
            [
                (whole[at : at + pixels, :pixels], whole[at : at + pixels, pixels:])
                for at in range(0, whole.shape[0], pixels)
            ]
        )
    return wholes


def times(one, two):
    return one[0] * two[0] - one[1] * two[1], one[0] * two[1] + one[1] * two[0]


def conj_times(one, two):
    return one[0] * two[0] + one[1] * two[1], one[0] * two[1] - one[1] * two[0]


def place(column, columns, pixels):
    base = jnp.minimum(column // pixels * pixels, columns - 2 * pixels)
    return pl.multiple_of(base, pixels), column - base


def cut(tile, column, pixels):
    base, shift = place(column, tile.shape[-1], pixels)
    rows = tile.shape[1]
    wide = tile[:, :, pl.ds(base, 2 * pixels)].reshape(-1, 2 * pixels)
    turned = pltpu.roll(wide, 2 * pixels - shift, 1)
    return turned[:, :pixels].reshape(-1, rows, pixels)


def is_even(offsets, rows):
    return lax.rem(offsets[0, 0] // rows, 2) == 0


def cut_kernel(pixels, chunks, own, far, tile, *outs):
    planes, rows, _ = tile.shape
    even = is_even(own, rows)
    for (first, size), near, cross in zip(chunks, outs[::2], outs[1::2], strict=True):
        for at in range(size):
            slot = first + at
            strip = at * planes
            near[strip : strip + planes] = cut(tile, jnp.where(even, own[slot, 1], far[slot, 1]), pixels)
            cross[strip : strip + planes] = cut(tile, jnp.where(even, far[slot, 1], own[slot, 1]), pixels)
        if first == 0:
            for slot in range(own.shape[0]):
                for entry in range(2):
                    line = jnp.full((1, pixels), own[slot, entry], jnp.int32).astype(F32)
                    near[near.shape[0] - 1, 2 * slot + entry : 2 * slot + entry + 1] = line
                    cross[cross.shape[0] - 1, 2 * slot + entry : 2 * slot + entry + 1] = line


def add_kernel(pixels, groups, own, middle, far, *refs):
    parts, before, out = refs[: len(groups)], refs[len(groups) : -1], refs[-1]
    planes, rows, _ = out.shape
    even = is_even(own, rows)
    out[...] = before[0][...] if before else jnp.zeros_like(out)
    lane = lax.broadcasted_iota(jnp.int32, (1, 1, pixels), 2)
    for (kind, first, size, unit), strips in zip(groups, parts):

        def add(at, carry, kind=kind, first=first, unit=unit, strips=strips):
            slot = first + at
            if kind == "mid":
                column = middle[slot, 1]
            elif kind == "near":
                column = jnp.where(even, own[slot, 1], far[slot, 1])
            else:
                column = jnp.where(even, far[slot, 1], own[slot, 1])
            base, shift = place(column, out.shape[-1], pixels)
            part = strips[pl.ds(unit + at * planes, planes)]
            turned = pltpu.roll(part.reshape(-1, pixels), lax.rem(shift, pixels), 1).reshape(part.shape)
            out[:, :, pl.ds(base, pixels)] += jnp.where(lane >= shift, turned, 0.0)
            out[:, :, pl.ds(pl.multiple_of(base + pixels, pixels), pixels)] += jnp.where(
                lane < shift, turned, 0.0
            )
            return carry

        lax.fori_loop(0, size, add, 0)


def slot_kernel(
    first, size, ahead, own_offsets, *refs
):
    if first == 0:
        offsets, refs = refs[-6], refs[:-6] + refs[-5:]
    else:
        offsets, *refs = refs
    tile, near, cross, target, probe, prop, tables, so_far, *refs = refs
    given, refs = refs[:ahead], refs[ahead:]
    out_near, out_mid, out_cross, total, *shares = refs[:-5]
    window, patch, grads, exit_wave, far = refs[-5:]
    modes, _, pixels, _ = probe.shape
    planes, rows, _ = tile.shape
    behind = given[0].shape[0] if given else 0
    for message, out in zip(given, (out_near, out_cross)):
        out[:behind] = message[...]
    even = is_even(own_offsets, rows)
    if first == 0:
        for slot in range(offsets.shape[0]):
            for entry in range(2):
                line = pl.ds(2 * slot + entry, 1)
                value = jnp.where(even, cross[cross.shape[0] - 1, line], near[near.shape[0] - 1, line])
                offsets[slot, entry] = jnp.max(value).astype(jnp.int32)
    total[...] = so_far[...]
    held = range(BATCH)

    def is_live(at):
        return jnp.max(target[first + at, :8]) > 0.0

    def leave(slots):
        for at in slots:
            for out, unit in ((out_near, behind), (out_mid, 0), (out_cross, behind)):
                out[pl.ds(unit + at * planes, planes)] = jnp.zeros((planes, rows, pixels), F32)

    def visit(slots):
        starts = [lax.rem(offsets[first + at, 0], rows) for at in slots]
        live = [jnp.where(is_live(at), 1.0, 0.0).astype(F32) for at in slots]
        for s, at in enumerate(slots):
            strip = pl.ds(at * planes, planes)
            window[:, :rows] = jnp.where(even, cross[strip], near[strip])
            window[:, rows : 2 * rows] = cut(tile, offsets[first + at, 1], pixels)
            window[:, 2 * rows :] = jnp.where(even, near[strip], cross[strip])
            patch[s] = window[:, pl.ds(starts[s], pixels), :]
            total[2 * modes] += live[s] * (patch[s, 0] * patch[s, 0] + patch[s, 1] * patch[s, 1])
        all_modes = range(modes)
        groups = [
            [times((probe[m, 0], probe[m, 1]), (patch[s, 0], patch[s, 1])) for m in all_modes] for s in held
        ]
        groups = transform(tables, False, groups)
        groups = [[times((prop[0], prop[1]), wave) for wave in waves] for waves in groups]
        groups = transform(tables, True, groups)
        for s in held:
            for m in all_modes:
                exit_wave[s, m, 0], exit_wave[s, m, 1] = groups[s][m]
            groups[s] = [times(wave, (patch[s, 2], patch[s, 3])) for wave in groups[s]]
        groups = transform(tables, False, groups)
        for s, at in enumerate(slots):
            intensity = jnp.zeros((pixels, pixels), F32)
            for m in all_modes:
                wave = groups[s][m]
                far[s, m, 0], far[s, m, 1] = wave
                intensity = intensity + wave[0] * wave[0] + wave[1] * wave[1]
            misfit = 2.0 * live[s] * (intensity - target[first + at])
            groups[s] = [(misfit * far[s, m, 0], misfit * far[s, m, 1]) for m in all_modes]
        groups = transform(tables, True, groups)
        for s in held:
            grad_re, grad_im = jnp.zeros((pixels, pixels), F32), jnp.zeros((pixels, pixels), F32)
            for m in all_modes:
                re, im = conj_times((exit_wave[s, m, 0], exit_wave[s, m, 1]), groups[s][m])
                grad_re, grad_im = grad_re + re, grad_im + im
            grads[s, 2], grads[s, 3] = grad_re, grad_im
            groups[s] = [conj_times((patch[s, 2], patch[s, 3]), wave) for wave in groups[s]]
        groups = transform(tables, False, groups)
        groups = [[conj_times((prop[0], prop[1]), wave) for wave in waves] for waves in groups]
        groups = transform(tables, True, groups)
        for s in held:
            grad_re, grad_im = jnp.zeros((pixels, pixels), F32), jnp.zeros((pixels, pixels), F32)
            for m in all_modes:
                re, im = conj_times((patch[s, 0], patch[s, 1]), groups[s][m])
                total[2 * m] += re
                total[2 * m + 1] += im
                re, im = conj_times((probe[m, 0], probe[m, 1]), groups[s][m])
                grad_re, grad_im = grad_re + re, grad_im + im
            grads[s, 0], grads[s, 1] = grad_re, grad_im
        for s, at in enumerate(slots):
            window[...] = jnp.zeros_like(window)
            window[:, pl.ds(starts[s], pixels), :] = grads[s]
            strip = pl.ds(behind + at * planes, planes)
            out_near[strip] = jnp.where(even, window[:, 2 * rows :], window[:, :rows])
            out_mid[pl.ds(at * planes, planes)] = window[:, rows : 2 * rows]
            out_cross[strip] = jnp.where(even, window[:, :rows], window[:, 2 * rows :])

    def step(index, carry):
        slots = [index * BATCH + s for s in range(BATCH)]
        some = is_live(slots[0])
        pl.when(some)(lambda: visit(slots))
        pl.when(jnp.logical_not(some))(lambda: leave(slots))
        return carry

    lax.fori_loop(0, size // BATCH, step, 0)

    if shares:
        own, other = shares
        chips, _, share, _ = own.shape
        core = jnp.where(even, 0, 1)
        for chip in range(chips):
            for plane in range(2 * modes + 1):
                own[chip, plane] = total[plane, pl.ds((2 * chip + core) * share, share)]
                other[chip, plane] = total[plane, pl.ds((2 * chip + 1 - core) * share, share)]


def step_kernel(parts, out):
    summed = parts[0]
    for at in range(1, parts.shape[0]):
        summed = summed + parts[at]
    step = summed[:-1] / (summed[-1:] + 1.0)
    for at in range(out.shape[0]):
        out[at] = step


def order_kernel(rows, offsets, own, other, out):
    chips, _, share, _ = own.shape
    core = jnp.where(is_even(offsets, rows), 0, 1)
    for chip in range(chips):
        out[:, pl.ds((2 * chip + core) * share, share)] = own[chip]
        out[:, pl.ds((2 * chip + 1 - core) * share, share)] = other[chip]


def in_smem():
    return pl.BlockSpec(memory_space=pltpu.SMEM)


def in_vmem():
    return pl.BlockSpec(memory_space=pltpu.VMEM)


def local(object_slices, probe_modes, propagator_phase, measured, offsets, counts):
    slices, _, tile_rows, columns = object_slices.shape
    modes, _, pixels, _ = probe_modes.shape
    planes = 2 * slices
    peers = lax.axis_size("row")
    params = pltpu.CompilerParams(vmem_limit_bytes=VMEM_LIMIT)
    tile = object_slices.reshape(planes, tile_rows, columns)
    starts = [sum(CHUNKS[:i]) for i in range(len(CHUNKS))]

    pair = [(i, i ^ 1) for i in range(peers)]
    other_pair = [(i, (i - 1) % peers if i % 2 == 0 else (i + 1) % peers) for i in range(peers)]
    far = shifted(offsets, "row", 2)

    live = lax.broadcasted_iota(jnp.int32, (measured.shape[0], 1, 1), 0) < counts[0]
    target = jnp.where(live, measured, 0.0)
    far, target = lax.optimization_barrier((far, target))
    target = shifted(target, "row", 1)

    def units(count):
        return jax.ShapeDtypeStruct((count, tile_rows, pixels), F32)

    def strips(chunks):
        shapes = [units(size * planes + (first == 0)) for first, size in chunks for _ in range(2)]
        outs = pl.pallas_call(
            functools.partial(cut_kernel, pixels, chunks),
            out_shape=shapes,
            in_specs=[in_smem()] * 2 + [in_vmem()],
            out_specs=[in_vmem()] * len(shapes),
            compiler_params=params,
            cost_estimate=pl.CostEstimate(flops=0, bytes_accessed=4 << 20, transcendentals=0),
        )(offsets, far, tile)
        return list(zip(outs[::2], outs[1::2]))

    def swapped(to_near, to_cross):
        return lax.ppermute(to_near, "row", pair), lax.ppermute(to_cross, "row", other_pair)

    chunks = list(zip(starts, CHUNKS))
    waiting = strips(chunks[:1]) + strips(chunks[1:])
    arrived = [swapped(*waiting[0])]
    if len(waiting) > 1:
        arrived[0], following = lax.optimization_barrier((arrived[0], waiting[1]))
        arrived.append(swapped(*following))
    prop = jnp.stack([jnp.cos(propagator_phase), jnp.sin(propagator_phase)])
    tables = jnp.asarray(fourier_tables(pixels))

    share = pixels // peers
    total = jnp.zeros((2 * modes + 1, pixels, pixels), F32)
    mid, back, places = [], [], [offsets]
    for index, (first, size) in enumerate(chunks):
        given = waiting[index + 2] if index + 2 < len(chunks) else ()
        ahead = CHUNKS[index + 2] * planes if given else 0
        part = jax.ShapeDtypeStruct((peers // 2, 2 * modes + 1, share, pixels), F32)
        shares = [part, part] if index == len(CHUNKS) - 1 else []
        message = units(ahead + size * planes)
        field = pltpu.VMEM((BATCH, planes, pixels, pixels), F32)
        kept = pltpu.VMEM((BATCH, modes, 2, pixels, pixels), F32)
        to_near, to_mid, to_cross, total, *shares = pl.pallas_call(
            functools.partial(slot_kernel, first, size, len(given)),
            out_shape=[message, units(size * planes), message, jax.ShapeDtypeStruct(total.shape, F32)]
            + shares
            + ([] if index else [jax.ShapeDtypeStruct(offsets.shape, jnp.int32)]),
            in_specs=[in_smem()] * len(places) + [in_vmem()] * (8 + len(given)),
            out_specs=[in_vmem()] * (4 + len(shares)) + ([] if index else [in_smem()]),
            scratch_shapes=[pltpu.VMEM((planes, 3 * tile_rows, pixels), F32), field, field, kept, kept],
            compiler_params=params,
            cost_estimate=pl.CostEstimate(
                flops=size * 6 * modes * 3 * 16 * pixels**3, bytes_accessed=8 << 20, transcendentals=0
            ),
        )(*places, tile, *arrived[index], target, probe_modes, prop, tables, total, *given)
        if index == 0:
            middle = shares.pop()
            places.append(middle)
        mid.append((("mid", first, size, 0), to_mid))
        message = swapped(to_near, to_cross)
        if given:
            arrived.append(message)
        back.append([((kind, first, size, ahead), part) for kind, part in zip(("near", "cross"), message)])

    def added(groups, strips, *before):
        return pl.pallas_call(
            functools.partial(add_kernel, pixels, groups),
            out_shape=jax.ShapeDtypeStruct(tile.shape, F32),
            in_specs=[in_smem()] * 3 + [in_vmem()] * (len(strips) + len(before)),
            out_specs=in_vmem(),
            compiler_params=params,
            input_output_aliases={3 + len(strips): 0} if before else {},
            cost_estimate=pl.CostEstimate(flops=0, bytes_accessed=5 << 20, transcendentals=0),
        )(offsets, middle, far, *strips, *before)

    cores = [list(range(core, peers, 2)) for core in range(2)]
    own, other = shares
    both = own + lax.ppermute(other, "row", pair)
    early = added(*zip(*(mid + [part for parts in back[:-1] for part in parts])))
    last_groups, last_strips = zip(*back[-1])
    both, early, last_strips = lax.optimization_barrier((both, early, last_strips))
    parts = lax.all_to_all(both, "row", 0, 0, axis_index_groups=cores)
    spread = pl.pallas_call(
        step_kernel,
        out_shape=jax.ShapeDtypeStruct((peers // 2, 2 * modes, share, pixels), F32),
        in_specs=[in_vmem()],
        out_specs=in_vmem(),
        compiler_params=params,
    )(parts)
    gathered = lax.all_to_all(spread, "row", 0, 0, axis_index_groups=cores)

    object_grad = added(last_groups, last_strips, early)
    object_grad = object_grad.reshape(object_slices.shape)

    probe_step = pl.pallas_call(
        functools.partial(order_kernel, tile_rows),
        out_shape=jax.ShapeDtypeStruct((2 * modes, pixels, pixels), F32),
        in_specs=[in_smem()] + [in_vmem()] * 2,
        out_specs=in_vmem(),
        compiler_params=params,
    )(offsets, gathered, lax.ppermute(gathered, "row", pair)).reshape(probe_modes.shape)
    return (object_grad, probe_step)


def solution(mesh):
    in_specs = (
        P(None, None, ("grp", "row"), None),
        P("grp", None, None, None),
        P(),
        P(("grp", "row"), None, None),
        P(("grp", "row"), None),
        P(("grp", "row")),
    )
    out_specs = (P(None, None, ("grp", "row"), None), P("grp", None, None, None))
    return jax.shard_map(local, mesh=mesh, in_specs=in_specs, out_specs=out_specs, check_vma=False)
```

```python
import functools

import jax
import jax.numpy as jnp
import numpy as np
from jax import lax
from jax.experimental import pallas as pl
from jax.experimental.pallas import tpu as pltpu
from jax.sharding import PartitionSpec as P

CHUNKS = (4, 4)
BATCH = 2
VMEM_LIMIT = 48 * 1024 * 1024
F32 = jnp.float32
BF16 = jnp.bfloat16


def shifted(array, axis, by):
    peers = lax.axis_size(axis)
    return lax.ppermute(array, axis, [(i, (i + by) % peers) for i in range(peers)])


def fourier_tables(pixels):
    indices = np.arange(pixels)
    angles = 2.0 * np.pi * (indices[:, None] * indices[None, :] % pixels) / pixels
    re = np.cos(angles) / np.sqrt(pixels)
    im = -np.sin(angles) / np.sqrt(pixels)
    left = np.block([[re, -im], [im, re]]).astype(np.float32)
    high = left.astype(BF16)
    low = (left - high.astype(np.float32)).astype(BF16)
    return np.stack([high, low, high.T, low.T])


def pieces(array):
    high = array.astype(BF16)
    return high, (array - high.astype(F32)).astype(BF16)


def transform(tables, conj, groups):
    at_left, at_right = (2, 0) if conj else (0, 2)
    left = jnp.concatenate([tables[at_left], tables[at_left + 1], tables[at_left]], axis=1)
    right = jnp.concatenate([tables[at_right], tables[at_right], tables[at_right + 1]], axis=0)
    pixels = left.shape[0] // 2
    halves = []
    for waves in groups:
        stacked = jnp.concatenate([jnp.concatenate(wave, axis=0) for wave in waves], axis=1)
        high, low = pieces(stacked)
        half = jnp.dot(left, jnp.concatenate([high, high, low], axis=0), preferred_element_type=F32)
        turned = [
            jnp.concatenate([half[:pixels, at : at + pixels], half[pixels:, at : at + pixels]], axis=1)
            for at in range(0, half.shape[1], pixels)
        ]
        halves.append(pieces(jnp.concatenate(turned, axis=0)))
    wholes = []
    for high, low in halves:
        whole = jnp.dot(jnp.concatenate([high, low, high], axis=1), right, preferred_element_type=F32)
        wholes.append(
            [
                (whole[at : at + pixels, :pixels], whole[at : at + pixels, pixels:])
                for at in range(0, whole.shape[0], pixels)
            ]
        )
    return wholes


def times(one, two):
    return one[0] * two[0] - one[1] * two[1], one[0] * two[1] + one[1] * two[0]


def conj_times(one, two):
    return one[0] * two[0] + one[1] * two[1], one[0] * two[1] - one[1] * two[0]


def place(column, columns, pixels):
    base = jnp.minimum(column // pixels * pixels, columns - 2 * pixels)
    return pl.multiple_of(base, pixels), column - base


def cut(tile, column, pixels):
    base, shift = place(column, tile.shape[-1], pixels)
    rows = tile.shape[1]
    wide = tile[:, :, pl.ds(base, 2 * pixels)].reshape(-1, 2 * pixels)
    turned = pltpu.roll(wide, 2 * pixels - shift, 1)
    return turned[:, :pixels].reshape(-1, rows, pixels)


def is_even(offsets, rows):
    return lax.rem(offsets[0, 0] // rows, 2) == 0


def cut_kernel(pixels, chunks, own, far, tile, *outs):
    planes, rows, _ = tile.shape
    even = is_even(own, rows)
    for (first, size), near, cross in zip(chunks, outs[::2], outs[1::2], strict=True):
        for at in range(size):
            slot = first + at
            strip = at * planes
            near[strip : strip + planes] = cut(tile, jnp.where(even, own[slot, 1], far[slot, 1]), pixels)
            cross[strip : strip + planes] = cut(tile, jnp.where(even, far[slot, 1], own[slot, 1]), pixels)
        if first == 0:
            for slot in range(own.shape[0]):
                for entry in range(2):
                    line = jnp.full((1, pixels), own[slot, entry], jnp.int32).astype(F32)
                    near[near.shape[0] - 1, 2 * slot + entry : 2 * slot + entry + 1] = line
                    cross[cross.shape[0] - 1, 2 * slot + entry : 2 * slot + entry + 1] = line


def add_kernel(pixels, groups, own, middle, far, *refs):
    *parts, out = refs
    planes, rows, _ = out.shape
    even = is_even(own, rows)
    out[...] = jnp.zeros_like(out)
    lane = lax.broadcasted_iota(jnp.int32, (1, 1, pixels), 2)
    for (kind, first, size, unit), strips in zip(groups, parts):

        def add(at, carry, kind=kind, first=first, unit=unit, strips=strips):
            slot = first + at
            if kind == "mid":
                column = middle[slot, 1]
            elif kind == "near":
                column = jnp.where(even, own[slot, 1], far[slot, 1])
            else:
                column = jnp.where(even, far[slot, 1], own[slot, 1])
            base, shift = place(column, out.shape[-1], pixels)
            part = strips[pl.ds(unit + at * planes, planes)]
            turned = pltpu.roll(part.reshape(-1, pixels), lax.rem(shift, pixels), 1).reshape(part.shape)
            out[:, :, pl.ds(base, pixels)] += jnp.where(lane >= shift, turned, 0.0)
            out[:, :, pl.ds(pl.multiple_of(base + pixels, pixels), pixels)] += jnp.where(
                lane < shift, turned, 0.0
            )
            return carry

        lax.fori_loop(0, size, add, 0)


def slot_kernel(
    first, size, ahead, own_offsets, *refs
):
    if first == 0:
        offsets, refs = refs[-6], refs[:-6] + refs[-5:]
    else:
        offsets, *refs = refs
    tile, near, cross, target, probe, prop, tables, so_far, *refs = refs
    given, refs = refs[:ahead], refs[ahead:]
    out_near, out_mid, out_cross, total, *shares = refs[:-5]
    window, patch, grads, exit_wave, far = refs[-5:]
    modes, _, pixels, _ = probe.shape
    planes, rows, _ = tile.shape
    behind = given[0].shape[0] if given else 0
    for message, out in zip(given, (out_near, out_cross)):
        out[:behind] = message[...]
    even = is_even(own_offsets, rows)
    if first == 0:
        for slot in range(offsets.shape[0]):
            for entry in range(2):
                line = pl.ds(2 * slot + entry, 1)
                value = jnp.where(even, cross[cross.shape[0] - 1, line], near[near.shape[0] - 1, line])
                offsets[slot, entry] = jnp.max(value).astype(jnp.int32)
    total[...] = so_far[...]
    held = range(BATCH)

    def is_live(at):
        return jnp.max(target[first + at, :8]) > 0.0

    def leave(slots):
        for at in slots:
            for out, unit in ((out_near, behind), (out_mid, 0), (out_cross, behind)):
                out[pl.ds(unit + at * planes, planes)] = jnp.zeros((planes, rows, pixels), F32)

    def visit(slots):
        starts = [lax.rem(offsets[first + at, 0], rows) for at in slots]
        live = [jnp.where(is_live(at), 1.0, 0.0).astype(F32) for at in slots]
        for s, at in enumerate(slots):
            strip = pl.ds(at * planes, planes)
            window[:, :rows] = jnp.where(even, cross[strip], near[strip])
            window[:, rows : 2 * rows] = cut(tile, offsets[first + at, 1], pixels)
            window[:, 2 * rows :] = jnp.where(even, near[strip], cross[strip])
            patch[s] = window[:, pl.ds(starts[s], pixels), :]
            total[2 * modes] += live[s] * (patch[s, 0] * patch[s, 0] + patch[s, 1] * patch[s, 1])
        all_modes = range(modes)
        groups = [
            [times((probe[m, 0], probe[m, 1]), (patch[s, 0], patch[s, 1])) for m in all_modes] for s in held
        ]
        groups = transform(tables, False, groups)
        groups = [[times((prop[0], prop[1]), wave) for wave in waves] for waves in groups]
        groups = transform(tables, True, groups)
        for s in held:
            for m in all_modes:
                exit_wave[s, m, 0], exit_wave[s, m, 1] = groups[s][m]
            groups[s] = [times(wave, (patch[s, 2], patch[s, 3])) for wave in groups[s]]
        groups = transform(tables, False, groups)
        for s, at in enumerate(slots):
            intensity = jnp.zeros((pixels, pixels), F32)
            for m in all_modes:
                wave = groups[s][m]
                far[s, m, 0], far[s, m, 1] = wave
                intensity = intensity + wave[0] * wave[0] + wave[1] * wave[1]
            misfit = 2.0 * live[s] * (intensity - target[first + at])
            groups[s] = [(misfit * far[s, m, 0], misfit * far[s, m, 1]) for m in all_modes]
        groups = transform(tables, True, groups)
        for s in held:
            grad_re, grad_im = jnp.zeros((pixels, pixels), F32), jnp.zeros((pixels, pixels), F32)
            for m in all_modes:
                re, im = conj_times((exit_wave[s, m, 0], exit_wave[s, m, 1]), groups[s][m])
                grad_re, grad_im = grad_re + re, grad_im + im
            grads[s, 2], grads[s, 3] = grad_re, grad_im
            groups[s] = [conj_times((patch[s, 2], patch[s, 3]), wave) for wave in groups[s]]
        groups = transform(tables, False, groups)
        groups = [[conj_times((prop[0], prop[1]), wave) for wave in waves] for waves in groups]
        groups = transform(tables, True, groups)
        for s in held:
            grad_re, grad_im = jnp.zeros((pixels, pixels), F32), jnp.zeros((pixels, pixels), F32)
            for m in all_modes:
                re, im = conj_times((patch[s, 0], patch[s, 1]), groups[s][m])
                total[2 * m] += re
                total[2 * m + 1] += im
                re, im = conj_times((probe[m, 0], probe[m, 1]), groups[s][m])
                grad_re, grad_im = grad_re + re, grad_im + im
            grads[s, 0], grads[s, 1] = grad_re, grad_im
        for s, at in enumerate(slots):
            window[...] = jnp.zeros_like(window)
            window[:, pl.ds(starts[s], pixels), :] = grads[s]
            strip = pl.ds(behind + at * planes, planes)
            out_near[strip] = jnp.where(even, window[:, 2 * rows :], window[:, :rows])
            out_mid[pl.ds(at * planes, planes)] = window[:, rows : 2 * rows]
            out_cross[strip] = jnp.where(even, window[:, :rows], window[:, 2 * rows :])

    def step(index, carry):
        slots = [index * BATCH + s for s in range(BATCH)]
        some = is_live(slots[0])
        pl.when(some)(lambda: visit(slots))
        pl.when(jnp.logical_not(some))(lambda: leave(slots))
        return carry

    lax.fori_loop(0, size // BATCH, step, 0)

    if shares:
        own, other = shares
        chips, _, share, _ = own.shape
        core = jnp.where(even, 0, 1)
        for chip in range(chips):
            for plane in range(2 * modes + 1):
                own[chip, plane] = total[plane, pl.ds((2 * chip + core) * share, share)]
                other[chip, plane] = total[plane, pl.ds((2 * chip + 1 - core) * share, share)]


def step_kernel(parts, out):
    summed = parts[0]
    for at in range(1, parts.shape[0]):
        summed = summed + parts[at]
    step = summed[:-1] / (summed[-1:] + 1.0)
    for at in range(out.shape[0]):
        out[at] = step


def order_kernel(rows, offsets, own, other, out):
    chips, _, share, _ = own.shape
    core = jnp.where(is_even(offsets, rows), 0, 1)
    for chip in range(chips):
        out[:, pl.ds((2 * chip + core) * share, share)] = own[chip]
        out[:, pl.ds((2 * chip + 1 - core) * share, share)] = other[chip]


def in_smem():
    return pl.BlockSpec(memory_space=pltpu.SMEM)


def in_vmem():
    return pl.BlockSpec(memory_space=pltpu.VMEM)


def local(object_slices, probe_modes, propagator_phase, measured, offsets, counts):
    slices, _, tile_rows, columns = object_slices.shape
    modes, _, pixels, _ = probe_modes.shape
    planes = 2 * slices
    peers = lax.axis_size("row")
    params = pltpu.CompilerParams(vmem_limit_bytes=VMEM_LIMIT)
    tile = object_slices.reshape(planes, tile_rows, columns)
    starts = [sum(CHUNKS[:i]) for i in range(len(CHUNKS))]

    pair = [(i, i ^ 1) for i in range(peers)]
    other_pair = [(i, (i - 1) % peers if i % 2 == 0 else (i + 1) % peers) for i in range(peers)]
    far = shifted(offsets, "row", 2)

    live = lax.broadcasted_iota(jnp.int32, (measured.shape[0], 1, 1), 0) < counts[0]
    target = jnp.where(live, measured, 0.0)
    far, target = lax.optimization_barrier((far, target))
    target = shifted(target, "row", 1)

    def units(count):
        return jax.ShapeDtypeStruct((count, tile_rows, pixels), F32)

    def strips(chunks):
        shapes = [units(size * planes + (first == 0)) for first, size in chunks for _ in range(2)]
        outs = pl.pallas_call(
            functools.partial(cut_kernel, pixels, chunks),
            out_shape=shapes,
            in_specs=[in_smem()] * 2 + [in_vmem()],
            out_specs=[in_vmem()] * len(shapes),
            compiler_params=params,
            cost_estimate=pl.CostEstimate(flops=0, bytes_accessed=4 << 20, transcendentals=0),
        )(offsets, far, tile)
        return list(zip(outs[::2], outs[1::2]))

    def swapped(to_near, to_cross):
        return lax.ppermute(to_near, "row", pair), lax.ppermute(to_cross, "row", other_pair)

    chunks = list(zip(starts, CHUNKS))
    waiting = strips(chunks[:1]) + strips(chunks[1:])
    arrived = [swapped(*waiting[0])]
    if len(waiting) > 1:
        arrived[0], following = lax.optimization_barrier((arrived[0], waiting[1]))
        arrived.append(swapped(*following))
    prop = jnp.stack([jnp.cos(propagator_phase), jnp.sin(propagator_phase)])
    tables = jnp.asarray(fourier_tables(pixels))

    share = pixels // peers
    total = jnp.zeros((2 * modes + 1, pixels, pixels), F32)
    mid, back, mid_groups, back_groups, places = [], [], [], [], [offsets]
    for index, (first, size) in enumerate(chunks):
        given = waiting[index + 2] if index + 2 < len(chunks) else ()
        ahead = CHUNKS[index + 2] * planes if given else 0
        part = jax.ShapeDtypeStruct((peers // 2, 2 * modes + 1, share, pixels), F32)
        shares = [part, part] if index == len(CHUNKS) - 1 else []
        message = units(ahead + size * planes)
        field = pltpu.VMEM((BATCH, planes, pixels, pixels), F32)
        kept = pltpu.VMEM((BATCH, modes, 2, pixels, pixels), F32)
        to_near, to_mid, to_cross, total, *shares = pl.pallas_call(
            functools.partial(slot_kernel, first, size, len(given)),
            out_shape=[message, units(size * planes), message, jax.ShapeDtypeStruct(total.shape, F32)]
            + shares
            + ([] if index else [jax.ShapeDtypeStruct(offsets.shape, jnp.int32)]),
            in_specs=[in_smem()] * len(places) + [in_vmem()] * (8 + len(given)),
            out_specs=[in_vmem()] * (4 + len(shares)) + ([] if index else [in_smem()]),
            scratch_shapes=[pltpu.VMEM((planes, 3 * tile_rows, pixels), F32), field, field, kept, kept],
            compiler_params=params,
            cost_estimate=pl.CostEstimate(
                flops=size * 6 * modes * 3 * 16 * pixels**3, bytes_accessed=8 << 20, transcendentals=0
            ),
        )(*places, tile, *arrived[index], target, probe_modes, prop, tables, total, *given)
        if index == 0:
            middle = shares.pop()
            places.append(middle)
        mid_groups.append(("mid", first, size, 0))
        mid.append(to_mid)
        message = swapped(to_near, to_cross)
        if given:
            arrived.append(message)
        back_groups += [(kind, first, size, ahead) for kind in ("near", "cross")]
        back.append(message)

    def added(groups, strips):
        return pl.pallas_call(
            functools.partial(add_kernel, pixels, groups),
            out_shape=jax.ShapeDtypeStruct(tile.shape, F32),
            in_specs=[in_smem()] * 3 + [in_vmem()] * len(strips),
            out_specs=in_vmem(),
            compiler_params=params,
            cost_estimate=pl.CostEstimate(flops=0, bytes_accessed=5 << 20, transcendentals=0),
        )(offsets, middle, far, *strips)

    cores = [list(range(core, peers, 2)) for core in range(2)]
    own, other = shares
    own, other, back[:-1] = lax.optimization_barrier((own, other, back[:-1]))
    both = own + lax.ppermute(other, "row", pair)
    parts = lax.all_to_all(both, "row", 0, 0, axis_index_groups=cores)
    spread = pl.pallas_call(
        step_kernel,
        out_shape=jax.ShapeDtypeStruct((peers // 2, 2 * modes, share, pixels), F32),
        in_specs=[in_vmem()],
        out_specs=in_vmem(),
        compiler_params=params,
    )(parts)
    groups = mid_groups + back_groups
    strips = mid + [part for message in back for part in message]
    spread, strips = lax.optimization_barrier((spread, strips))
    gathered = lax.all_to_all(spread, "row", 0, 0, axis_index_groups=cores)
    gathered, strips = lax.optimization_barrier((gathered, strips))

    object_grad = added(groups, strips)
    object_grad = object_grad.reshape(object_slices.shape)

    probe_step = pl.pallas_call(
        functools.partial(order_kernel, tile_rows),
        out_shape=jax.ShapeDtypeStruct((2 * modes, pixels, pixels), F32),
        in_specs=[in_smem()] + [in_vmem()] * 2,
        out_specs=in_vmem(),
        compiler_params=params,
    )(offsets, gathered, lax.ppermute(gathered, "row", pair)).reshape(probe_modes.shape)
    return (object_grad, probe_step)


def solution(mesh):
    in_specs = (
        P(None, None, ("grp", "row"), None),
        P("grp", None, None, None),
        P(),
        P(("grp", "row"), None, None),
        P(("grp", "row"), None),
        P(("grp", "row")),
    )
    out_specs = (P(None, None, ("grp", "row"), None), P("grp", None, None, None))
    return jax.shard_map(local, mesh=mesh, in_specs=in_specs, out_specs=out_specs, check_vma=False)
```

```python
import functools

import jax
import jax.numpy as jnp
import numpy as np
from jax import lax
from jax.experimental import pallas as pl
from jax.experimental.pallas import tpu as pltpu
from jax.sharding import PartitionSpec as P

CHUNKS = (4, 4)
BATCH = 2
VMEM_LIMIT = 48 * 1024 * 1024
F32 = jnp.float32
BF16 = jnp.bfloat16


def shifted(array, axis, by):
    peers = lax.axis_size(axis)
    return lax.ppermute(array, axis, [(i, (i + by) % peers) for i in range(peers)])


def fourier_tables(pixels):
    indices = np.arange(pixels)
    angles = 2.0 * np.pi * (indices[:, None] * indices[None, :] % pixels) / pixels
    re = np.cos(angles) / np.sqrt(pixels)
    im = -np.sin(angles) / np.sqrt(pixels)
    left = np.block([[re, -im], [im, re]]).astype(np.float32)
    high = left.astype(BF16)
    low = (left - high.astype(np.float32)).astype(BF16)
    return np.stack([high, low, high.T, low.T])


def pieces(array):
    high = array.astype(BF16)
    return high, (array - high.astype(F32)).astype(BF16)


def transform(tables, conj, groups):
    at_left, at_right = (2, 0) if conj else (0, 2)
    left = jnp.concatenate([tables[at_left], tables[at_left + 1], tables[at_left]], axis=1)
    right = jnp.concatenate([tables[at_right], tables[at_right], tables[at_right + 1]], axis=0)
    pixels = left.shape[0] // 2
    halves = []
    for waves in groups:
        stacked = jnp.concatenate([jnp.concatenate(wave, axis=0) for wave in waves], axis=1)
        high, low = pieces(stacked)
        half = jnp.dot(left, jnp.concatenate([high, high, low], axis=0), preferred_element_type=F32)
        turned = [
            jnp.concatenate([half[:pixels, at : at + pixels], half[pixels:, at : at + pixels]], axis=1)
            for at in range(0, half.shape[1], pixels)
        ]
        halves.append(pieces(jnp.concatenate(turned, axis=0)))
    wholes = []
    for high, low in halves:
        whole = jnp.dot(jnp.concatenate([high, low, high], axis=1), right, preferred_element_type=F32)
        wholes.append(
            [
                (whole[at : at + pixels, :pixels], whole[at : at + pixels, pixels:])
                for at in range(0, whole.shape[0], pixels)
            ]
        )
    return wholes


def times(one, two):
    return one[0] * two[0] - one[1] * two[1], one[0] * two[1] + one[1] * two[0]


def conj_times(one, two):
    return one[0] * two[0] + one[1] * two[1], one[0] * two[1] - one[1] * two[0]


def place(column, columns, pixels):
    base = jnp.minimum(column // pixels * pixels, columns - 2 * pixels)
    return pl.multiple_of(base, pixels), column - base


def cut(tile, column, pixels):
    base, shift = place(column, tile.shape[-1], pixels)
    rows = tile.shape[1]
    wide = tile[:, :, pl.ds(base, 2 * pixels)].reshape(-1, 2 * pixels)
    turned = pltpu.roll(wide, 2 * pixels - shift, 1)
    return turned[:, :pixels].reshape(-1, rows, pixels)


def is_even(offsets, rows):
    return lax.rem(offsets[0, 0] // rows, 2) == 0


def pack_kernel(offsets, counts, measured, out):
    slots, _, pixels = measured.shape
    for slot in range(slots):
        live = jnp.where(slot < counts[0], 1.0, 0.0).astype(F32)
        out[slot] = measured[slot] * live
        for entry in range(2):
            line = jnp.full((1, pixels), offsets[slot, entry], jnp.int32).astype(F32)
            out[slots, 2 * slot + entry : 2 * slot + entry + 1] = line


def cut_kernel(pixels, chunks, own, far, tile, *outs):
    planes, rows, _ = tile.shape
    even = is_even(own, rows)
    for (first, size), near, cross in zip(chunks, outs[::2], outs[1::2], strict=True):
        for at in range(size):
            slot = first + at
            strip = at * planes
            near[strip : strip + planes] = cut(tile, jnp.where(even, own[slot, 1], far[slot, 1]), pixels)
            cross[strip : strip + planes] = cut(tile, jnp.where(even, far[slot, 1], own[slot, 1]), pixels)


def add_kernel(pixels, groups, own, middle, far, *refs):
    *parts, out = refs
    planes, rows, _ = out.shape
    even = is_even(own, rows)
    out[...] = jnp.zeros_like(out)
    lane = lax.broadcasted_iota(jnp.int32, (1, 1, pixels), 2)
    for (kind, first, size, unit), strips in zip(groups, parts):

        def add(at, carry, kind=kind, first=first, unit=unit, strips=strips):
            slot = first + at
            if kind == "mid":
                column = middle[slot, 1]
            elif kind == "near":
                column = jnp.where(even, own[slot, 1], far[slot, 1])
            else:
                column = jnp.where(even, far[slot, 1], own[slot, 1])
            base, shift = place(column, out.shape[-1], pixels)
            part = strips[pl.ds(unit + at * planes, planes)]
            turned = pltpu.roll(part.reshape(-1, pixels), lax.rem(shift, pixels), 1).reshape(part.shape)
            out[:, :, pl.ds(base, pixels)] += jnp.where(lane >= shift, turned, 0.0)
            out[:, :, pl.ds(pl.multiple_of(base + pixels, pixels), pixels)] += jnp.where(
                lane < shift, turned, 0.0
            )
            return carry

        lax.fori_loop(0, size, add, 0)


def slot_kernel(
    first, size, ahead, own_offsets, *refs
):
    if first == 0:
        offsets, refs = refs[-6], refs[:-6] + refs[-5:]
    else:
        offsets, *refs = refs
    tile, near, cross, target, probe, prop, tables, so_far, *refs = refs
    given, refs = refs[:ahead], refs[ahead:]
    out_near, out_mid, out_cross, total, *shares = refs[:-5]
    window, patch, grads, exit_wave, far = refs[-5:]
    modes, _, pixels, _ = probe.shape
    planes, rows, _ = tile.shape
    behind = given[0].shape[0] if given else 0
    for message, out in zip(given, (out_near, out_cross)):
        out[:behind] = message[...]
    even = is_even(own_offsets, rows)
    if first == 0:
        for slot in range(offsets.shape[0]):
            for entry in range(2):
                line = 2 * slot + entry
                value = target[target.shape[0] - 1, line : line + 1]
                offsets[slot, entry] = jnp.max(value).astype(jnp.int32)
    total[...] = so_far[...]
    held = range(BATCH)

    def is_live(at):
        return jnp.max(target[first + at, :8]) > 0.0

    def leave(slots):
        for at in slots:
            for out, unit in ((out_near, behind), (out_mid, 0), (out_cross, behind)):
                out[pl.ds(unit + at * planes, planes)] = jnp.zeros((planes, rows, pixels), F32)

    def visit(slots):
        starts = [lax.rem(offsets[first + at, 0], rows) for at in slots]
        live = [jnp.where(is_live(at), 1.0, 0.0).astype(F32) for at in slots]
        for s, at in enumerate(slots):
            strip = pl.ds(at * planes, planes)
            window[:, :rows] = jnp.where(even, cross[strip], near[strip])
            window[:, rows : 2 * rows] = cut(tile, offsets[first + at, 1], pixels)
            window[:, 2 * rows :] = jnp.where(even, near[strip], cross[strip])
            patch[s] = window[:, pl.ds(starts[s], pixels), :]
            total[2 * modes] += live[s] * (patch[s, 0] * patch[s, 0] + patch[s, 1] * patch[s, 1])
        all_modes = range(modes)
        groups = [
            [times((probe[m, 0], probe[m, 1]), (patch[s, 0], patch[s, 1])) for m in all_modes] for s in held
        ]
        groups = transform(tables, False, groups)
        groups = [[times((prop[0], prop[1]), wave) for wave in waves] for waves in groups]
        groups = transform(tables, True, groups)
        for s in held:
            for m in all_modes:
                exit_wave[s, m, 0], exit_wave[s, m, 1] = groups[s][m]
            groups[s] = [times(wave, (patch[s, 2], patch[s, 3])) for wave in groups[s]]
        groups = transform(tables, False, groups)
        for s, at in enumerate(slots):
            intensity = jnp.zeros((pixels, pixels), F32)
            for m in all_modes:
                wave = groups[s][m]
                far[s, m, 0], far[s, m, 1] = wave
                intensity = intensity + wave[0] * wave[0] + wave[1] * wave[1]
            misfit = 2.0 * live[s] * (intensity - target[first + at])
            groups[s] = [(misfit * far[s, m, 0], misfit * far[s, m, 1]) for m in all_modes]
        groups = transform(tables, True, groups)
        for s in held:
            grad_re, grad_im = jnp.zeros((pixels, pixels), F32), jnp.zeros((pixels, pixels), F32)
            for m in all_modes:
                re, im = conj_times((exit_wave[s, m, 0], exit_wave[s, m, 1]), groups[s][m])
                grad_re, grad_im = grad_re + re, grad_im + im
            grads[s, 2], grads[s, 3] = grad_re, grad_im
            groups[s] = [conj_times((patch[s, 2], patch[s, 3]), wave) for wave in groups[s]]
        groups = transform(tables, False, groups)
        groups = [[conj_times((prop[0], prop[1]), wave) for wave in waves] for waves in groups]
        groups = transform(tables, True, groups)
        for s in held:
            grad_re, grad_im = jnp.zeros((pixels, pixels), F32), jnp.zeros((pixels, pixels), F32)
            for m in all_modes:
                re, im = conj_times((patch[s, 0], patch[s, 1]), groups[s][m])
                total[2 * m] += re
                total[2 * m + 1] += im
                re, im = conj_times((probe[m, 0], probe[m, 1]), groups[s][m])
                grad_re, grad_im = grad_re + re, grad_im + im
            grads[s, 0], grads[s, 1] = grad_re, grad_im
        for s, at in enumerate(slots):
            window[...] = jnp.zeros_like(window)
            window[:, pl.ds(starts[s], pixels), :] = grads[s]
            strip = pl.ds(behind + at * planes, planes)
            out_near[strip] = jnp.where(even, window[:, 2 * rows :], window[:, :rows])
            out_mid[pl.ds(at * planes, planes)] = window[:, rows : 2 * rows]
            out_cross[strip] = jnp.where(even, window[:, :rows], window[:, 2 * rows :])

    def step(index, carry):
        slots = [index * BATCH + s for s in range(BATCH)]
        some = is_live(slots[0])
        pl.when(some)(lambda: visit(slots))
        pl.when(jnp.logical_not(some))(lambda: leave(slots))
        return carry

    lax.fori_loop(0, size // BATCH, step, 0)

    if shares:
        own, other = shares
        chips, _, share, _ = own.shape
        core = jnp.where(even, 0, 1)
        for chip in range(chips):
            for plane in range(2 * modes + 1):
                own[chip, plane] = total[plane, pl.ds((2 * chip + core) * share, share)]
                other[chip, plane] = total[plane, pl.ds((2 * chip + 1 - core) * share, share)]


def step_kernel(parts, out):
    summed = parts[0]
    for at in range(1, parts.shape[0]):
        summed = summed + parts[at]
    step = summed[:-1] / (summed[-1:] + 1.0)
    for at in range(out.shape[0]):
        out[at] = step


def order_kernel(rows, offsets, own, other, out):
    chips, _, share, _ = own.shape
    core = jnp.where(is_even(offsets, rows), 0, 1)
    for chip in range(chips):
        out[:, pl.ds((2 * chip + core) * share, share)] = own[chip]
        out[:, pl.ds((2 * chip + 1 - core) * share, share)] = other[chip]


def in_smem():
    return pl.BlockSpec(memory_space=pltpu.SMEM)


def in_vmem():
    return pl.BlockSpec(memory_space=pltpu.VMEM)


def local(object_slices, probe_modes, propagator_phase, measured, offsets, counts):
    slices, _, tile_rows, columns = object_slices.shape
    modes, _, pixels, _ = probe_modes.shape
    planes = 2 * slices
    peers = lax.axis_size("row")
    params = pltpu.CompilerParams(vmem_limit_bytes=VMEM_LIMIT)
    tile = object_slices.reshape(planes, tile_rows, columns)
    starts = [sum(CHUNKS[:i]) for i in range(len(CHUNKS))]

    pair = [(i, i ^ 1) for i in range(peers)]
    other_pair = [(i, (i - 1) % peers if i % 2 == 0 else (i + 1) % peers) for i in range(peers)]
    far = shifted(offsets, "row", 2)

    target = pl.pallas_call(
        pack_kernel,
        out_shape=jax.ShapeDtypeStruct((measured.shape[0] + 1, pixels, pixels), F32),
        in_specs=[in_smem()] * 2 + [in_vmem()],
        out_specs=in_vmem(),
        compiler_params=params,
        cost_estimate=pl.CostEstimate(flops=0, bytes_accessed=1 << 20, transcendentals=0),
    )(offsets, counts, measured)
    far, target = lax.optimization_barrier((far, target))
    target = shifted(target, "row", 1)

    def units(count):
        return jax.ShapeDtypeStruct((count, tile_rows, pixels), F32)

    def strips(chunks, far):
        shapes = [units(size * planes) for _, size in chunks for _ in range(2)]
        outs = pl.pallas_call(
            functools.partial(cut_kernel, pixels, chunks),
            out_shape=shapes,
            in_specs=[in_smem()] * 2 + [in_vmem()],
            out_specs=[in_vmem()] * len(shapes),
            compiler_params=params,
            cost_estimate=pl.CostEstimate(flops=0, bytes_accessed=4 << 20, transcendentals=0),
        )(offsets, far, tile)
        return list(zip(outs[::2], outs[1::2]))

    def swapped(to_near, to_cross):
        return lax.ppermute(to_near, "row", pair), lax.ppermute(to_cross, "row", other_pair)

    chunks = list(zip(starts, CHUNKS))
    far_later, target = lax.optimization_barrier((far, target))
    waiting = strips(chunks[:1], far) + strips(chunks[1:], far_later)
    arrived = [swapped(*waiting[0])]
    if len(waiting) > 1:
        arrived[0], following = lax.optimization_barrier((arrived[0], waiting[1]))
        arrived.append(swapped(*following))
    prop = jnp.stack([jnp.cos(propagator_phase), jnp.sin(propagator_phase)])
    tables = jnp.asarray(fourier_tables(pixels))

    share = pixels // peers
    total = jnp.zeros((2 * modes + 1, pixels, pixels), F32)
    mid, back, mid_groups, back_groups, places = [], [], [], [], [offsets]
    for index, (first, size) in enumerate(chunks):
        given = waiting[index + 2] if index + 2 < len(chunks) else ()
        ahead = CHUNKS[index + 2] * planes if given else 0
        part = jax.ShapeDtypeStruct((peers // 2, 2 * modes + 1, share, pixels), F32)
        shares = [part, part] if index == len(CHUNKS) - 1 else []
        message = units(ahead + size * planes)
        field = pltpu.VMEM((BATCH, planes, pixels, pixels), F32)
        kept = pltpu.VMEM((BATCH, modes, 2, pixels, pixels), F32)
        to_near, to_mid, to_cross, total, *shares = pl.pallas_call(
            functools.partial(slot_kernel, first, size, len(given)),
            out_shape=[message, units(size * planes), message, jax.ShapeDtypeStruct(total.shape, F32)]
            + shares
            + ([] if index else [jax.ShapeDtypeStruct(offsets.shape, jnp.int32)]),
            in_specs=[in_smem()] * len(places) + [in_vmem()] * (8 + len(given)),
            out_specs=[in_vmem()] * (4 + len(shares)) + ([] if index else [in_smem()]),
            scratch_shapes=[pltpu.VMEM((planes, 3 * tile_rows, pixels), F32), field, field, kept, kept],
            compiler_params=params,
            cost_estimate=pl.CostEstimate(
                flops=size * 6 * modes * 3 * 16 * pixels**3, bytes_accessed=8 << 20, transcendentals=0
            ),
        )(*places, tile, *arrived[index], target, probe_modes, prop, tables, total, *given)
        if index == 0:
            middle = shares.pop()
            places.append(middle)
        mid_groups.append(("mid", first, size, 0))
        mid.append(to_mid)
        message = swapped(to_near, to_cross)
        if given:
            arrived.append(message)
        back_groups += [(kind, first, size, ahead) for kind in ("near", "cross")]
        back.append(message)

    def added(groups, strips):
        return pl.pallas_call(
            functools.partial(add_kernel, pixels, groups),
            out_shape=jax.ShapeDtypeStruct(tile.shape, F32),
            in_specs=[in_smem()] * 3 + [in_vmem()] * len(strips),
            out_specs=in_vmem(),
            compiler_params=params,
            cost_estimate=pl.CostEstimate(flops=0, bytes_accessed=5 << 20, transcendentals=0),
        )(offsets, middle, far, *strips)

    cores = [list(range(core, peers, 2)) for core in range(2)]
    own, other = shares
    own, other, back[:-1] = lax.optimization_barrier((own, other, back[:-1]))
    both = own + lax.ppermute(other, "row", pair)
    parts = lax.all_to_all(both, "row", 0, 0, axis_index_groups=cores)
    spread = pl.pallas_call(
        step_kernel,
        out_shape=jax.ShapeDtypeStruct((peers // 2, 2 * modes, share, pixels), F32),
        in_specs=[in_vmem()],
        out_specs=in_vmem(),
        compiler_params=params,
    )(parts)
    groups = mid_groups + back_groups
    strips = mid + [part for message in back for part in message]
    spread, strips = lax.optimization_barrier((spread, strips))
    gathered = lax.all_to_all(spread, "row", 0, 0, axis_index_groups=cores)
    gathered, strips = lax.optimization_barrier((gathered, strips))

    object_grad = added(groups, strips)
    object_grad = object_grad.reshape(object_slices.shape)

    probe_step = pl.pallas_call(
        functools.partial(order_kernel, tile_rows),
        out_shape=jax.ShapeDtypeStruct((2 * modes, pixels, pixels), F32),
        in_specs=[in_smem()] + [in_vmem()] * 2,
        out_specs=in_vmem(),
        compiler_params=params,
    )(offsets, gathered, lax.ppermute(gathered, "row", pair)).reshape(probe_modes.shape)
    return (object_grad, probe_step)


def solution(mesh):
    in_specs = (
        P(None, None, ("grp", "row"), None),
        P("grp", None, None, None),
        P(),
        P(("grp", "row"), None, None),
        P(("grp", "row"), None),
        P(("grp", "row")),
    )
    out_specs = (P(None, None, ("grp", "row"), None), P("grp", None, None, None))
    return jax.shard_map(local, mesh=mesh, in_specs=in_specs, out_specs=out_specs, check_vma=False)
```

```python
import functools

import jax
import jax.numpy as jnp
import numpy as np
from jax import lax
from jax.experimental import pallas as pl
from jax.experimental.pallas import tpu as pltpu
from jax.sharding import PartitionSpec as P

CHUNKS = (4, 4)
BATCH = 4
VMEM_LIMIT = 48 * 1024 * 1024
F32 = jnp.float32
BF16 = jnp.bfloat16


def shifted(array, axis, by):
    peers = lax.axis_size(axis)
    return lax.ppermute(array, axis, [(i, (i + by) % peers) for i in range(peers)])


def fourier_tables(pixels):
    indices = np.arange(pixels)
    angles = 2.0 * np.pi * (indices[:, None] * indices[None, :] % pixels) / pixels
    re = np.cos(angles) / np.sqrt(pixels)
    im = -np.sin(angles) / np.sqrt(pixels)
    left = np.block([[re, -im], [im, re]]).astype(np.float32)
    high = left.astype(BF16)
    low = (left - high.astype(np.float32)).astype(BF16)
    return np.stack([high, low, high.T, low.T])


def pieces(array):
    high = array.astype(BF16)
    return high, (array - high.astype(F32)).astype(BF16)


def transform(tables, conj, groups):
    at_left, at_right = (2, 0) if conj else (0, 2)
    left = jnp.concatenate([tables[at_left], tables[at_left + 1], tables[at_left]], axis=1)
    right = jnp.concatenate([tables[at_right], tables[at_right], tables[at_right + 1]], axis=0)
    pixels = left.shape[0] // 2
    halves = []
    for waves in groups:
        stacked = jnp.concatenate([jnp.concatenate(wave, axis=0) for wave in waves], axis=1)
        high, low = pieces(stacked)
        half = jnp.dot(left, jnp.concatenate([high, high, low], axis=0), preferred_element_type=F32)
        turned = [
            jnp.concatenate([half[:pixels, at : at + pixels], half[pixels:, at : at + pixels]], axis=1)
            for at in range(0, half.shape[1], pixels)
        ]
        halves.append(pieces(jnp.concatenate(turned, axis=0)))
    wholes = []
    for high, low in halves:
        whole = jnp.dot(jnp.concatenate([high, low, high], axis=1), right, preferred_element_type=F32)
        wholes.append(
            [
                (whole[at : at + pixels, :pixels], whole[at : at + pixels, pixels:])
                for at in range(0, whole.shape[0], pixels)
            ]
        )
    return wholes


def times(one, two):
    return one[0] * two[0] - one[1] * two[1], one[0] * two[1] + one[1] * two[0]


def conj_times(one, two):
    return one[0] * two[0] + one[1] * two[1], one[0] * two[1] - one[1] * two[0]


def place(column, columns, pixels):
    base = jnp.minimum(column // pixels * pixels, columns - 2 * pixels)
    return pl.multiple_of(base, pixels), column - base


def cut(tile, column, pixels):
    base, shift = place(column, tile.shape[-1], pixels)
    rows = tile.shape[1]
    wide = tile[:, :, pl.ds(base, 2 * pixels)].reshape(-1, 2 * pixels)
    turned = pltpu.roll(wide, 2 * pixels - shift, 1)
    return turned[:, :pixels].reshape(-1, rows, pixels)


def rows_of(index, share):
    return pl.ds(pl.multiple_of(index * share, share), share)


def is_even(offsets, rows):
    return lax.rem(offsets[0, 0] // rows, 2) == 0


def pack_kernel(chunks, offsets, counts, measured, *outs):
    slots, _, pixels = measured.shape
    for (first, size), out in zip(chunks, outs):
        for at in range(size):
            live = jnp.where(first + at < counts[0], 1.0, 0.0).astype(F32)
            out[at] = measured[first + at] * live
    first_out = outs[0]
    for slot in range(slots):
        for entry in range(2):
            line = jnp.full((1, pixels), offsets[slot, entry], jnp.int32).astype(F32)
            first_out[chunks[0][1], 2 * slot + entry : 2 * slot + entry + 1] = line


def cut_kernel(pixels, chunks, own, far, tile, *outs):
    planes, rows, _ = tile.shape
    even = is_even(own, rows)
    for (first, size), near, cross in zip(chunks, outs[::2], outs[1::2], strict=True):
        for at in range(size):
            slot = first + at
            strip = at * planes
            near[strip : strip + planes] = cut(tile, jnp.where(even, own[slot, 1], far[slot, 1]), pixels)
            cross[strip : strip + planes] = cut(tile, jnp.where(even, far[slot, 1], own[slot, 1]), pixels)


def add_kernel(pixels, groups, own, middle, far, *refs):
    *parts, out = refs
    planes, rows, _ = out.shape
    even = is_even(own, rows)
    out[...] = jnp.zeros_like(out)
    lane = lax.broadcasted_iota(jnp.int32, (1, 1, pixels), 2)
    for (kind, first, size, unit), strips in zip(groups, parts):

        turned = []
        for at in range(size):
            slot = first + at
            if kind == "mid":
                column = middle[slot, 1]
            elif kind == "near":
                column = jnp.where(even, own[slot, 1], far[slot, 1])
            else:
                column = jnp.where(even, far[slot, 1], own[slot, 1])
            base, shift = place(column, out.shape[-1], pixels)
            part = strips[unit + at * planes : unit + (at + 1) * planes].reshape(-1, pixels)
            part = pltpu.roll(part, lax.rem(shift, pixels), 1).reshape(planes, rows, pixels)
            turned.append((base, shift, part))
        for base, shift, part in turned:
            out[:, :, pl.ds(base, pixels)] += jnp.where(lane >= shift, part, 0.0)
            beside = pl.ds(pl.multiple_of(base + pixels, pixels), pixels)
            out[:, :, beside] += jnp.where(lane < shift, part, 0.0)


def slot_kernel(
    first, size, ahead, own_offsets, *refs
):
    if first == 0:
        offsets, refs = refs[-6], refs[:-6] + refs[-5:]
    else:
        offsets, *refs = refs
    tile, near, cross, target, probe, prop, tables, so_far, *refs = refs
    given, refs = refs[:ahead], refs[ahead:]
    out_near, out_mid, out_cross, total, *shares = refs[:-5]
    window, patch, grads, exit_wave, far = refs[-5:]
    modes, _, pixels, _ = probe.shape
    planes, rows, _ = tile.shape
    behind = given[0].shape[0] if given else 0
    for message, out in zip(given, (out_near, out_cross)):
        out[:behind] = message[...]
    even = is_even(own_offsets, rows)
    if first == 0:
        for slot in range(offsets.shape[0]):
            for entry in range(2):
                line = 2 * slot + entry
                value = target[target.shape[0] - 1, line : line + 1]
                offsets[slot, entry] = jnp.max(value).astype(jnp.int32)
    total[...] = so_far[...]
    held = range(BATCH)

    def is_live(at):
        return jnp.max(target[at, :8]) > 0.0

    def leave(slots):
        for at in slots:
            for out, unit in ((out_near, behind), (out_mid, 0), (out_cross, behind)):
                out[pl.ds(unit + at * planes, planes)] = jnp.zeros((planes, rows, pixels), F32)

    def visit(slots):
        starts = [lax.rem(offsets[first + at, 0], rows) for at in slots]
        live = [jnp.where(is_live(at), 1.0, 0.0).astype(F32) for at in slots]
        for s, at in enumerate(slots):
            strip = pl.ds(at * planes, planes)
            window[:, :rows] = jnp.where(even, cross[strip], near[strip])
            window[:, rows : 2 * rows] = cut(tile, offsets[first + at, 1], pixels)
            window[:, 2 * rows :] = jnp.where(even, near[strip], cross[strip])
            patch[s] = window[:, pl.ds(starts[s], pixels), :]
            total[2 * modes] += live[s] * (patch[s, 0] * patch[s, 0] + patch[s, 1] * patch[s, 1])
        all_modes = range(modes)
        groups = [
            [times((probe[m, 0], probe[m, 1]), (patch[s, 0], patch[s, 1])) for m in all_modes] for s in held
        ]
        groups = transform(tables, False, groups)
        groups = [[times((prop[0], prop[1]), wave) for wave in waves] for waves in groups]
        groups = transform(tables, True, groups)
        for s in held:
            for m in all_modes:
                exit_wave[s, m, 0], exit_wave[s, m, 1] = groups[s][m]
            groups[s] = [times(wave, (patch[s, 2], patch[s, 3])) for wave in groups[s]]
        groups = transform(tables, False, groups)
        for s, at in enumerate(slots):
            intensity = jnp.zeros((pixels, pixels), F32)
            for m in all_modes:
                wave = groups[s][m]
                far[s, m, 0], far[s, m, 1] = wave
                intensity = intensity + wave[0] * wave[0] + wave[1] * wave[1]
            misfit = 2.0 * live[s] * (intensity - target[at])
            groups[s] = [(misfit * far[s, m, 0], misfit * far[s, m, 1]) for m in all_modes]
        groups = transform(tables, True, groups)
        for s in held:
            grad_re, grad_im = jnp.zeros((pixels, pixels), F32), jnp.zeros((pixels, pixels), F32)
            for m in all_modes:
                re, im = conj_times((exit_wave[s, m, 0], exit_wave[s, m, 1]), groups[s][m])
                grad_re, grad_im = grad_re + re, grad_im + im
            grads[s, 2], grads[s, 3] = grad_re, grad_im
            groups[s] = [conj_times((patch[s, 2], patch[s, 3]), wave) for wave in groups[s]]
        groups = transform(tables, False, groups)
        groups = [[conj_times((prop[0], prop[1]), wave) for wave in waves] for waves in groups]
        groups = transform(tables, True, groups)
        for s in held:
            grad_re, grad_im = jnp.zeros((pixels, pixels), F32), jnp.zeros((pixels, pixels), F32)
            for m in all_modes:
                re, im = conj_times((patch[s, 0], patch[s, 1]), groups[s][m])
                total[2 * m] += re
                total[2 * m + 1] += im
                re, im = conj_times((probe[m, 0], probe[m, 1]), groups[s][m])
                grad_re, grad_im = grad_re + re, grad_im + im
            grads[s, 0], grads[s, 1] = grad_re, grad_im
        for s, at in enumerate(slots):
            window[...] = jnp.zeros_like(window)
            window[:, pl.ds(starts[s], pixels), :] = grads[s]
            strip = pl.ds(behind + at * planes, planes)
            out_near[strip] = jnp.where(even, window[:, 2 * rows :], window[:, :rows])
            out_mid[pl.ds(at * planes, planes)] = window[:, rows : 2 * rows]
            out_cross[strip] = jnp.where(even, window[:, :rows], window[:, 2 * rows :])

    def step(index, carry):
        slots = [index * BATCH + s for s in range(BATCH)]
        some = is_live(slots[0])
        pl.when(some)(lambda: visit(slots))
        pl.when(jnp.logical_not(some))(lambda: leave(slots))
        return carry

    lax.fori_loop(0, size // BATCH, step, 0)

    if shares:
        own, other = shares
        chips, _, share, _ = own.shape
        core = jnp.where(even, 0, 1)
        for chip in range(chips):
            for plane in range(2 * modes + 1):
                own[chip, plane] = total[plane, rows_of(2 * chip + core, share)]
                other[chip, plane] = total[plane, rows_of(2 * chip + 1 - core, share)]


def step_kernel(parts, out):
    summed = parts[0]
    for at in range(1, parts.shape[0]):
        summed = summed + parts[at]
    step = summed[:-1] / (summed[-1:] + 1.0)
    for at in range(out.shape[0]):
        out[at] = step


def order_kernel(rows, offsets, own, other, out):
    chips, _, share, _ = own.shape
    core = jnp.where(is_even(offsets, rows), 0, 1)
    for chip in range(chips):
        out[:, rows_of(2 * chip + core, share)] = own[chip]
        out[:, rows_of(2 * chip + 1 - core, share)] = other[chip]


def in_smem():
    return pl.BlockSpec(memory_space=pltpu.SMEM)


def in_vmem():
    return pl.BlockSpec(memory_space=pltpu.VMEM)


def local(object_slices, probe_modes, propagator_phase, measured, offsets, counts):
    slices, _, tile_rows, columns = object_slices.shape
    modes, _, pixels, _ = probe_modes.shape
    planes = 2 * slices
    peers = lax.axis_size("row")
    params = pltpu.CompilerParams(vmem_limit_bytes=VMEM_LIMIT)
    tile = object_slices.reshape(planes, tile_rows, columns)
    starts = [sum(CHUNKS[:i]) for i in range(len(CHUNKS))]

    pair = [(i, i ^ 1) for i in range(peers)]
    other_pair = [(i, (i - 1) % peers if i % 2 == 0 else (i + 1) % peers) for i in range(peers)]
    far = shifted(offsets, "row", 2)

    chunks = list(zip(starts, CHUNKS))
    packed = pl.pallas_call(
        functools.partial(pack_kernel, chunks),
        out_shape=[jax.ShapeDtypeStruct((size + (first == 0), pixels, pixels), F32) for first, size in chunks],
        in_specs=[in_smem()] * 2 + [in_vmem()],
        out_specs=[in_vmem()] * len(chunks),
        compiler_params=params,
        cost_estimate=pl.CostEstimate(flops=0, bytes_accessed=1 << 20, transcendentals=0),
    )(offsets, counts, measured)
    far, packed = lax.optimization_barrier((far, packed))

    def units(count):
        return jax.ShapeDtypeStruct((count, tile_rows, pixels), F32)

    def strips(chunks, far):
        shapes = [units(size * planes) for _, size in chunks for _ in range(2)]
        outs = pl.pallas_call(
            functools.partial(cut_kernel, pixels, chunks),
            out_shape=shapes,
            in_specs=[in_smem()] * 2 + [in_vmem()],
            out_specs=[in_vmem()] * len(shapes),
            compiler_params=params,
            cost_estimate=pl.CostEstimate(flops=0, bytes_accessed=4 << 20, transcendentals=0),
        )(offsets, far, tile)
        return list(zip(outs[::2], outs[1::2]))

    def swapped(to_near, to_cross):
        return lax.ppermute(to_near, "row", pair), lax.ppermute(to_cross, "row", other_pair)

    waiting = strips(chunks[:1], far) + strips(chunks[1:], far)
    arrived = [swapped(*waiting[0])]
    targets = [shifted(packed[0], "row", 1)]
    if len(waiting) > 1:
        arrived[0], following, packed = lax.optimization_barrier((arrived[0], waiting[1], packed))
        arrived.append(swapped(*following))
        targets += [shifted(part, "row", 1) for part in packed[1:]]
    prop = jnp.stack([jnp.cos(propagator_phase), jnp.sin(propagator_phase)])
    tables = jnp.asarray(fourier_tables(pixels))

    share = pixels // peers
    total = jnp.zeros((2 * modes + 1, pixels, pixels), F32)
    mid, back, mid_groups, back_groups, places = [], [], [], [], [offsets]
    for index, (first, size) in enumerate(chunks):
        given = waiting[index + 2] if index + 2 < len(chunks) else ()
        ahead = CHUNKS[index + 2] * planes if given else 0
        part = jax.ShapeDtypeStruct((peers // 2, 2 * modes + 1, share, pixels), F32)
        shares = [part, part] if index == len(CHUNKS) - 1 else []
        message = units(ahead + size * planes)
        field = pltpu.VMEM((BATCH, planes, pixels, pixels), F32)
        kept = pltpu.VMEM((BATCH, modes, 2, pixels, pixels), F32)
        to_near, to_mid, to_cross, total, *shares = pl.pallas_call(
            functools.partial(slot_kernel, first, size, len(given)),
            out_shape=[message, units(size * planes), message, jax.ShapeDtypeStruct(total.shape, F32)]
            + shares
            + ([] if index else [jax.ShapeDtypeStruct(offsets.shape, jnp.int32)]),
            in_specs=[in_smem()] * len(places) + [in_vmem()] * (8 + len(given)),
            out_specs=[in_vmem()] * (4 + len(shares)) + ([] if index else [in_smem()]),
            scratch_shapes=[pltpu.VMEM((planes, 3 * tile_rows, pixels), F32), field, field, kept, kept],
            compiler_params=params,
            cost_estimate=pl.CostEstimate(
                flops=size * 6 * modes * 3 * 16 * pixels**3, bytes_accessed=8 << 20, transcendentals=0
            ),
        )(*places, tile, *arrived[index], targets[index], probe_modes, prop, tables, total, *given)
        if index == 0:
            middle = shares.pop()
            places.append(middle)
        mid_groups.append(("mid", first, size, 0))
        mid.append(to_mid)
        message = swapped(to_near, to_cross)
        if given:
            arrived.append(message)
        back_groups += [(kind, first, size, ahead) for kind in ("near", "cross")]
        back.append(message)

    def added(groups, strips):
        return pl.pallas_call(
            functools.partial(add_kernel, pixels, groups),
            out_shape=jax.ShapeDtypeStruct(tile.shape, F32),
            in_specs=[in_smem()] * 3 + [in_vmem()] * len(strips),
            out_specs=in_vmem(),
            compiler_params=params,
            cost_estimate=pl.CostEstimate(flops=0, bytes_accessed=5 << 20, transcendentals=0),
        )(offsets, middle, far, *strips)

    cores = [list(range(core, peers, 2)) for core in range(2)]
    own, other = shares
    own, other, back[:-1] = lax.optimization_barrier((own, other, back[:-1]))
    both = own + lax.ppermute(other, "row", pair)
    parts = lax.all_to_all(both, "row", 0, 0, axis_index_groups=cores)
    spread = pl.pallas_call(
        step_kernel,
        out_shape=jax.ShapeDtypeStruct((peers // 2, 2 * modes, share, pixels), F32),
        in_specs=[in_vmem()],
        out_specs=in_vmem(),
        compiler_params=params,
    )(parts)
    groups = mid_groups + back_groups
    strips = mid + [part for message in back for part in message]
    spread, strips = lax.optimization_barrier((spread, strips))
    gathered = lax.all_to_all(spread, "row", 0, 0, axis_index_groups=cores)
    gathered, strips = lax.optimization_barrier((gathered, strips))

    object_grad = added(groups, strips)
    object_grad = object_grad.reshape(object_slices.shape)

    probe_step = pl.pallas_call(
        functools.partial(order_kernel, tile_rows),
        out_shape=jax.ShapeDtypeStruct((2 * modes, pixels, pixels), F32),
        in_specs=[in_smem()] + [in_vmem()] * 2,
        out_specs=in_vmem(),
        compiler_params=params,
    )(offsets, gathered, lax.ppermute(gathered, "row", pair)).reshape(probe_modes.shape)
    return (object_grad, probe_step)


def solution(mesh):
    in_specs = (
        P(None, None, ("grp", "row"), None),
        P("grp", None, None, None),
        P(),
        P(("grp", "row"), None, None),
        P(("grp", "row"), None),
        P(("grp", "row")),
    )
    out_specs = (P(None, None, ("grp", "row"), None), P("grp", None, None, None))
    return jax.shard_map(local, mesh=mesh, in_specs=in_specs, out_specs=out_specs, check_vma=False)
```

```python
import functools

import jax
import jax.numpy as jnp
import numpy as np
from jax import lax
from jax.experimental import pallas as pl
from jax.experimental.pallas import tpu as pltpu
from jax.sharding import PartitionSpec as P

CHUNKS = (4, 4)
BATCH = 4
VMEM_LIMIT = 48 * 1024 * 1024
ROW = ("chip", "core")
F32 = jnp.float32
BF16 = jnp.bfloat16


def shifted(array, axis, by):
    peers = lax.axis_size(axis)
    return lax.ppermute(array, axis, [(i, (i + by) % peers) for i in range(peers)])


def fourier_tables(pixels):
    indices = np.arange(pixels)
    angles = 2.0 * np.pi * (indices[:, None] * indices[None, :] % pixels) / pixels
    re = np.cos(angles) / np.sqrt(pixels)
    im = -np.sin(angles) / np.sqrt(pixels)
    left = np.block([[re, -im], [im, re]]).astype(np.float32)
    high = left.astype(BF16)
    low = (left - high.astype(np.float32)).astype(BF16)
    return np.stack([high, low, high.T, low.T])


def pieces(array):
    high = array.astype(BF16)
    return high, (array - high.astype(F32)).astype(BF16)


def transform(tables, conj, groups):
    at_left, at_right = (2, 0) if conj else (0, 2)
    left = jnp.concatenate([tables[at_left], tables[at_left + 1], tables[at_left]], axis=1)
    right = jnp.concatenate([tables[at_right], tables[at_right], tables[at_right + 1]], axis=0)
    pixels = left.shape[0] // 2
    halves = []
    for waves in groups:
        stacked = jnp.concatenate([jnp.concatenate(wave, axis=0) for wave in waves], axis=1)
        high, low = pieces(stacked)
        half = jnp.dot(left, jnp.concatenate([high, high, low], axis=0), preferred_element_type=F32)
        turned = [
            jnp.concatenate([half[:pixels, at : at + pixels], half[pixels:, at : at + pixels]], axis=1)
            for at in range(0, half.shape[1], pixels)
        ]
        halves.append(pieces(jnp.concatenate(turned, axis=0)))
    wholes = []
    for high, low in halves:
        whole = jnp.dot(jnp.concatenate([high, low, high], axis=1), right, preferred_element_type=F32)
        wholes.append(
            [
                (whole[at : at + pixels, :pixels], whole[at : at + pixels, pixels:])
                for at in range(0, whole.shape[0], pixels)
            ]
        )
    return wholes


def times(one, two):
    return one[0] * two[0] - one[1] * two[1], one[0] * two[1] + one[1] * two[0]


def conj_times(one, two):
    return one[0] * two[0] + one[1] * two[1], one[0] * two[1] - one[1] * two[0]


def place(column, columns, pixels):
    base = jnp.minimum(column // pixels * pixels, columns - 2 * pixels)
    return pl.multiple_of(base, pixels), column - base


def cut(tile, column, pixels):
    base, shift = place(column, tile.shape[-1], pixels)
    rows = tile.shape[1]
    wide = tile[:, :, pl.ds(base, 2 * pixels)].reshape(-1, 2 * pixels)
    turned = pltpu.roll(wide, 2 * pixels - shift, 1)
    return turned[:, :pixels].reshape(-1, rows, pixels)


def rows_of(index, share):
    return pl.ds(pl.multiple_of(index * share, share), share)


def is_even(offsets, rows):
    return lax.rem(offsets[0, 0] // rows, 2) == 0


def pack_kernel(offsets, counts, measured, out):
    slots, _, pixels = measured.shape
    for slot in range(slots):
        live = jnp.where(slot < counts[0], 1.0, 0.0).astype(F32)
        out[slot] = measured[slot] * live
        for entry in range(2):
            line = jnp.full((1, pixels), offsets[slot, entry], jnp.int32).astype(F32)
            out[slots, 2 * slot + entry : 2 * slot + entry + 1] = line


def middle_kernel(pixels, target, tile, *outs):
    *parts, offsets = outs
    planes = tile.shape[0]
    for slot in range(offsets.shape[0]):
        for entry in range(2):
            line = 2 * slot + entry
            value = target[target.shape[0] - 1, line : line + 1]
            offsets[slot, entry] = jnp.max(value).astype(jnp.int32)
    slot = 0
    for part in parts:
        for at in range(part.shape[0] // planes):
            part[at * planes : (at + 1) * planes] = cut(tile, offsets[slot, 1], pixels)
            slot += 1


def cut_kernel(pixels, chunks, own, far, tile, *outs):
    planes, rows, _ = tile.shape
    even = is_even(own, rows)
    for (first, size), near, cross in zip(chunks, outs[::2], outs[1::2], strict=True):
        for at in range(size):
            slot = first + at
            strip = at * planes
            near[strip : strip + planes] = cut(tile, jnp.where(even, own[slot, 1], far[slot, 1]), pixels)
            cross[strip : strip + planes] = cut(tile, jnp.where(even, far[slot, 1], own[slot, 1]), pixels)


def add_kernel(pixels, groups, own, middle, far, *refs):
    *parts, out = refs
    planes, rows, _ = out.shape
    even = is_even(own, rows)
    out[...] = jnp.zeros_like(out)
    lane = lax.broadcasted_iota(jnp.int32, (1, 1, pixels), 2)
    for (kind, first, size, unit), strips in zip(groups, parts):

        turned = []
        for at in range(size):
            slot = first + at
            if kind == "mid":
                column = middle[slot, 1]
            elif kind == "near":
                column = jnp.where(even, own[slot, 1], far[slot, 1])
            else:
                column = jnp.where(even, far[slot, 1], own[slot, 1])
            base, shift = place(column, out.shape[-1], pixels)
            part = strips[unit + at * planes : unit + (at + 1) * planes].reshape(-1, pixels)
            part = pltpu.roll(part, lax.rem(shift, pixels), 1).reshape(planes, rows, pixels)
            turned.append((base, shift, part))
        for base, shift, part in turned:
            out[:, :, pl.ds(base, pixels)] += jnp.where(lane >= shift, part, 0.0)
            beside = pl.ds(pl.multiple_of(base + pixels, pixels), pixels)
            out[:, :, beside] += jnp.where(lane < shift, part, 0.0)


def slot_kernel(first, size, ahead, own_offsets, *refs):
    offsets, mid, near, cross, target, probe, prop, tables, *refs = refs
    so_far, refs = (refs[0], refs[1:]) if first else (None, refs)
    given, refs = refs[:ahead], refs[ahead:]
    out_near, out_mid, out_cross, total, *shares = refs[:-5]
    window, patch, grads, exit_wave, far = refs[-5:]
    modes, _, pixels, _ = probe.shape
    planes, rows = mid.shape[0] // size, mid.shape[1]
    behind = given[0].shape[0] if given else 0
    for message, out in zip(given, (out_near, out_cross)):
        out[:behind] = message[...]
    even = is_even(own_offsets, rows)
    total[...] = so_far[...] if first else jnp.zeros_like(total)
    held = range(BATCH)

    def is_live(at):
        return jnp.max(target[first + at, :8]) > 0.0

    def leave(slots):
        for at in slots:
            for out, unit in ((out_near, behind), (out_mid, 0), (out_cross, behind)):
                out[pl.ds(unit + at * planes, planes)] = jnp.zeros((planes, rows, pixels), F32)

    def visit(slots):
        starts = [lax.rem(offsets[first + at, 0], rows) for at in slots]
        live = [jnp.where(is_live(at), 1.0, 0.0).astype(F32) for at in slots]
        for s, at in enumerate(slots):
            strip = pl.ds(at * planes, planes)
            window[:, :rows] = jnp.where(even, cross[strip], near[strip])
            window[:, rows : 2 * rows] = mid[strip]
            window[:, 2 * rows :] = jnp.where(even, near[strip], cross[strip])
            patch[s] = window[:, pl.ds(starts[s], pixels), :]
            total[2 * modes] += live[s] * (patch[s, 0] * patch[s, 0] + patch[s, 1] * patch[s, 1])
        all_modes = range(modes)
        groups = [
            [times((probe[m, 0], probe[m, 1]), (patch[s, 0], patch[s, 1])) for m in all_modes] for s in held
        ]
        groups = transform(tables, False, groups)
        groups = [[times((prop[0], prop[1]), wave) for wave in waves] for waves in groups]
        groups = transform(tables, True, groups)
        for s in held:
            for m in all_modes:
                exit_wave[s, m, 0], exit_wave[s, m, 1] = groups[s][m]
            groups[s] = [times(wave, (patch[s, 2], patch[s, 3])) for wave in groups[s]]
        groups = transform(tables, False, groups)
        for s, at in enumerate(slots):
            intensity = jnp.zeros((pixels, pixels), F32)
            for m in all_modes:
                wave = groups[s][m]
                far[s, m, 0], far[s, m, 1] = wave
                intensity = intensity + wave[0] * wave[0] + wave[1] * wave[1]
            misfit = 2.0 * live[s] * (intensity - target[first + at])
            groups[s] = [(misfit * far[s, m, 0], misfit * far[s, m, 1]) for m in all_modes]
        groups = transform(tables, True, groups)
        for s in held:
            grad_re, grad_im = jnp.zeros((pixels, pixels), F32), jnp.zeros((pixels, pixels), F32)
            for m in all_modes:
                re, im = conj_times((exit_wave[s, m, 0], exit_wave[s, m, 1]), groups[s][m])
                grad_re, grad_im = grad_re + re, grad_im + im
            grads[s, 2], grads[s, 3] = grad_re, grad_im
            groups[s] = [conj_times((patch[s, 2], patch[s, 3]), wave) for wave in groups[s]]
        groups = transform(tables, False, groups)
        groups = [[conj_times((prop[0], prop[1]), wave) for wave in waves] for waves in groups]
        groups = transform(tables, True, groups)
        for s in held:
            grad_re, grad_im = jnp.zeros((pixels, pixels), F32), jnp.zeros((pixels, pixels), F32)
            for m in all_modes:
                re, im = conj_times((patch[s, 0], patch[s, 1]), groups[s][m])
                total[2 * m] += re
                total[2 * m + 1] += im
                re, im = conj_times((probe[m, 0], probe[m, 1]), groups[s][m])
                grad_re, grad_im = grad_re + re, grad_im + im
            grads[s, 0], grads[s, 1] = grad_re, grad_im
        for s, at in enumerate(slots):
            window[...] = jnp.zeros_like(window)
            window[:, pl.ds(starts[s], pixels), :] = grads[s]
            strip = pl.ds(behind + at * planes, planes)
            out_near[strip] = jnp.where(even, window[:, 2 * rows :], window[:, :rows])
            out_mid[pl.ds(at * planes, planes)] = window[:, rows : 2 * rows]
            out_cross[strip] = jnp.where(even, window[:, :rows], window[:, 2 * rows :])

    def step(index, carry):
        slots = [index * BATCH + s for s in range(BATCH)]
        some = is_live(slots[0])
        pl.when(some)(lambda: visit(slots))
        pl.when(jnp.logical_not(some))(lambda: leave(slots))
        return carry

    lax.fori_loop(0, size // BATCH, step, 0)

    if shares:
        own, other = shares
        chips, _, share, _ = own.shape
        core = jnp.where(even, 0, 1)
        for chip in range(chips):
            for plane in range(2 * modes + 1):
                own[chip, plane] = total[plane, rows_of(2 * chip + core, share)]
                other[chip, plane] = total[plane, rows_of(2 * chip + 1 - core, share)]


def step_kernel(parts, out):
    summed = parts[0]
    for at in range(1, parts.shape[0]):
        summed = summed + parts[at]
    step = summed[:-1] / (summed[-1:] + 1.0)
    for at in range(out.shape[0]):
        out[at] = step


def order_kernel(rows, offsets, own, other, out):
    chips, _, share, _ = own.shape
    core = jnp.where(is_even(offsets, rows), 0, 1)
    for chip in range(chips):
        out[:, rows_of(2 * chip + core, share)] = own[chip]
        out[:, rows_of(2 * chip + 1 - core, share)] = other[chip]


def in_smem():
    return pl.BlockSpec(memory_space=pltpu.SMEM)


def in_vmem():
    return pl.BlockSpec(memory_space=pltpu.VMEM)


def local(object_slices, probe_modes, propagator_phase, measured, offsets, counts):
    slices, _, tile_rows, columns = object_slices.shape
    modes, _, pixels, _ = probe_modes.shape
    planes = 2 * slices
    peers = lax.axis_size(ROW)
    params = pltpu.CompilerParams(vmem_limit_bytes=VMEM_LIMIT)
    tile = object_slices.reshape(planes, tile_rows, columns)
    starts = [sum(CHUNKS[:i]) for i in range(len(CHUNKS))]

    pair = [(i, i ^ 1) for i in range(peers)]
    other_pair = [(i, (i - 1) % peers if i % 2 == 0 else (i + 1) % peers) for i in range(peers)]
    far = shifted(offsets, ROW, 2)

    chunks = list(zip(starts, CHUNKS))
    target = pl.pallas_call(
        pack_kernel,
        out_shape=jax.ShapeDtypeStruct((measured.shape[0] + 1, pixels, pixels), F32),
        in_specs=[in_smem()] * 2 + [in_vmem()],
        out_specs=in_vmem(),
        compiler_params=params,
        cost_estimate=pl.CostEstimate(flops=0, bytes_accessed=1 << 20, transcendentals=0),
    )(offsets, counts, measured)
    far, target = lax.optimization_barrier((far, target))
    target = shifted(target, ROW, 1)

    def units(count):
        return jax.ShapeDtypeStruct((count, tile_rows, pixels), F32)

    def strips(chunks, far):
        shapes = [units(size * planes) for _, size in chunks for _ in range(2)]
        outs = pl.pallas_call(
            functools.partial(cut_kernel, pixels, chunks),
            out_shape=shapes,
            in_specs=[in_smem()] * 2 + [in_vmem()],
            out_specs=[in_vmem()] * len(shapes),
            compiler_params=params,
            cost_estimate=pl.CostEstimate(flops=0, bytes_accessed=4 << 20, transcendentals=0),
        )(offsets, far, tile)
        return list(zip(outs[::2], outs[1::2]))

    def swapped(to_near, to_cross):
        return lax.ppermute(to_near, ROW, pair), lax.ppermute(to_cross, ROW, other_pair)

    far_later, target = lax.optimization_barrier((far, target))
    waiting = strips(chunks[:1], far) + strips(chunks[1:], far_later)
    *middles, middle = pl.pallas_call(
        functools.partial(middle_kernel, pixels),
        out_shape=[units(size * planes) for size in CHUNKS] + [jax.ShapeDtypeStruct(offsets.shape, jnp.int32)],
        in_specs=[in_vmem()] * 2,
        out_specs=[in_vmem()] * len(CHUNKS) + [in_smem()],
        compiler_params=params,
        cost_estimate=pl.CostEstimate(flops=0, bytes_accessed=4 << 20, transcendentals=0),
    )(target, tile)
    arrived = [swapped(*waiting[0])]
    if len(waiting) > 1:
        arrived[0], following, middles = lax.optimization_barrier((arrived[0], waiting[1], middles))
        arrived.append(swapped(*following))
    prop = jnp.stack([jnp.cos(propagator_phase), jnp.sin(propagator_phase)])
    tables = jnp.asarray(fourier_tables(pixels))

    share = pixels // peers
    total = ()
    mid, back, mid_groups, back_groups = [], [], [], []
    for index, (first, size) in enumerate(chunks):
        given = waiting[index + 2] if index + 2 < len(chunks) else ()
        ahead = CHUNKS[index + 2] * planes if given else 0
        sums = jax.ShapeDtypeStruct((2 * modes + 1, pixels, pixels), F32)
        part = jax.ShapeDtypeStruct((peers // 2, 2 * modes + 1, share, pixels), F32)
        shares = [part, part] if index == len(CHUNKS) - 1 else []
        message = units(ahead + size * planes)
        field = pltpu.VMEM((BATCH, planes, pixels, pixels), F32)
        kept = pltpu.VMEM((BATCH, modes, 2, pixels, pixels), F32)
        to_near, to_mid, to_cross, *total = pl.pallas_call(
            functools.partial(slot_kernel, first, size, len(given)),
            out_shape=[message, units(size * planes), message, sums] + shares,
            in_specs=[in_smem()] * 2 + [in_vmem()] * (7 + len(total) + len(given)),
            out_specs=[in_vmem()] * (4 + len(shares)),
            scratch_shapes=[pltpu.VMEM((planes, 3 * tile_rows, pixels), F32), field, field, kept, kept],
            compiler_params=params,
            cost_estimate=pl.CostEstimate(
                flops=size * 6 * modes * 3 * 16 * pixels**3, bytes_accessed=8 << 20, transcendentals=0
            ),
        )(offsets, middle, middles[index], *arrived[index], target, probe_modes, prop, tables, *total, *given)
        total, shares = total[:1], total[1:]
        mid_groups.append(("mid", first, size, 0))
        mid.append(to_mid)
        message = swapped(to_near, to_cross)
        if given:
            arrived.append(message)
        back_groups += [(kind, first, size, ahead) for kind in ("near", "cross")]
        back.append(message)

    def added(groups, strips):
        return pl.pallas_call(
            functools.partial(add_kernel, pixels, groups),
            out_shape=jax.ShapeDtypeStruct(tile.shape, F32),
            in_specs=[in_smem()] * 3 + [in_vmem()] * len(strips),
            out_specs=in_vmem(),
            compiler_params=params,
            cost_estimate=pl.CostEstimate(flops=0, bytes_accessed=5 << 20, transcendentals=0),
        )(offsets, middle, far, *strips)

    own, other = shares
    own, other, back[:-1] = lax.optimization_barrier((own, other, back[:-1]))
    both = own + lax.ppermute(other, ROW, pair)
    parts = lax.all_to_all(both, "chip", 0, 0)
    spread = pl.pallas_call(
        step_kernel,
        out_shape=jax.ShapeDtypeStruct((peers // 2, 2 * modes, share, pixels), F32),
        in_specs=[in_vmem()],
        out_specs=in_vmem(),
        compiler_params=params,
    )(parts)
    groups = mid_groups + back_groups
    strips = mid + [part for message in back for part in message]
    spread, strips = lax.optimization_barrier((spread, strips))
    gathered = lax.all_to_all(spread, "chip", 0, 0)
    gathered, strips = lax.optimization_barrier((gathered, strips))

    object_grad = added(groups, strips)
    object_grad = object_grad.reshape(object_slices.shape)

    probe_step = pl.pallas_call(
        functools.partial(order_kernel, tile_rows),
        out_shape=jax.ShapeDtypeStruct((2 * modes, pixels, pixels), F32),
        in_specs=[in_smem()] + [in_vmem()] * 2,
        out_specs=in_vmem(),
        compiler_params=params,
    )(offsets, gathered, lax.ppermute(gathered, ROW, pair)).reshape(probe_modes.shape)
    return (object_grad, probe_step)


def solution(mesh):
    groups, peers = mesh.shape["grp"], mesh.shape["row"]
    split = jax.sharding.Mesh(mesh.devices.reshape(groups, peers // 2, 2), ("grp",) + ROW)
    everywhere = ("grp",) + ROW
    in_specs = (
        P(None, None, everywhere, None),
        P("grp", None, None, None),
        P(),
        P(everywhere, None, None),
        P(everywhere, None),
        P(everywhere),
    )
    out_specs = (P(None, None, everywhere, None), P("grp", None, None, None))
    return jax.shard_map(local, mesh=split, in_specs=in_specs, out_specs=out_specs, check_vma=False)
```

```python
import functools

import jax
import jax.numpy as jnp
import numpy as np
from jax import lax
from jax.experimental import pallas as pl
from jax.experimental.pallas import tpu as pltpu
from jax.sharding import PartitionSpec as P

CHUNKS = (4, 4)
BATCH = 4
VMEM_LIMIT = 32 * 1024 * 1024
ROW = ("chip", "core")
F32 = jnp.float32
BF16 = jnp.bfloat16


def shifted(array, axis, by):
    peers = lax.axis_size(axis)
    return lax.ppermute(array, axis, [(i, (i + by) % peers) for i in range(peers)])


def real_form(matrix):
    return np.block([[matrix.real, -matrix.imag], [matrix.imag, matrix.real]]).astype(np.float32)


def two_pieces(matrix):
    high = matrix.astype(BF16)
    return high, (matrix - high.astype(np.float32)).astype(BF16)


def fourier_tables(pixels):
    half = pixels // 2
    kept, rows = np.arange(half)[:, None], np.arange(half)[None, :]
    lefts = []
    for odd in range(2):
        turns = (2 * kept + odd) * rows % pixels / pixels
        part = real_form(np.exp(-2j * np.pi * turns) / np.sqrt(pixels))
        for table in (part, part.T):
            high, low = two_pieces(table)
            lefts.append(np.block([[high, high], [low, np.zeros_like(low)]]))
    indices = np.arange(pixels)
    whole = np.exp(-2j * np.pi * (indices[:, None] * indices[None, :] % pixels) / pixels) / np.sqrt(pixels)
    rights = []
    for table in (real_form(whole).T, real_form(whole)):
        rights += two_pieces(table)
    return np.stack(lefts + rights)


def pieces(array):
    high = array.astype(BF16)
    return high, (array - high.astype(F32)).astype(BF16)


def from_left(tables, conj, waves):
    half = waves[0][0].shape[0] // 2
    pixels = 2 * half
    sides = []
    for odd in range(2):
        parts = []
        for wave in waves:
            if conj:
                parts.append(jnp.concatenate([part[odd * half : (odd + 1) * half] for part in wave], axis=0))
            elif odd:
                parts.append(jnp.concatenate([part[:half] - part[half:] for part in wave], axis=0))
            else:
                parts.append(jnp.concatenate([part[:half] + part[half:] for part in wave], axis=0))
        stacked = jnp.concatenate(pieces(jnp.concatenate(parts, axis=1)), axis=0)
        product = jnp.dot(tables[2 * odd + conj], stacked, preferred_element_type=F32)
        sides.append(product[:pixels] + product[pixels:])
    if conj:
        sides = [sides[0] + sides[1], sides[0] - sides[1]]
    turned = []
    for at in range(0, len(waves) * pixels, pixels):
        re = jnp.concatenate([side[:half, at : at + pixels] for side in sides], axis=0)
        im = jnp.concatenate([side[half:, at : at + pixels] for side in sides], axis=0)
        turned.append(jnp.concatenate([re, im], axis=1))
    return jnp.concatenate(turned, axis=0)


def transform(tables, conj, groups):
    right_high, right_low = tables[4 + 2 * conj], tables[5 + 2 * conj]
    right = jnp.concatenate([right_high, right_high, right_low], axis=0)
    halves = [pieces(from_left(tables, conj, waves)) for waves in groups]
    pixels = right.shape[1] // 2
    wholes = []
    for high, low in halves:
        whole = jnp.dot(jnp.concatenate([high, low, high], axis=1), right, preferred_element_type=F32)
        wholes.append(
            [
                (whole[at : at + pixels, :pixels], whole[at : at + pixels, pixels:])
                for at in range(0, whole.shape[0], pixels)
            ]
        )
    return wholes


def times(one, two):
    return one[0] * two[0] - one[1] * two[1], one[0] * two[1] + one[1] * two[0]


def conj_times(one, two):
    return one[0] * two[0] + one[1] * two[1], one[0] * two[1] - one[1] * two[0]


def place(column, columns, pixels):
    base = jnp.minimum(column // pixels * pixels, columns - 2 * pixels)
    return pl.multiple_of(base, pixels), column - base


def cut(tile, column, pixels):
    base, shift = place(column, tile.shape[-1], pixels)
    rows = tile.shape[1]
    wide = tile[:, :, pl.ds(base, 2 * pixels)].reshape(-1, 2 * pixels)
    turned = pltpu.roll(wide, 2 * pixels - shift, 1)
    return turned[:, :pixels].reshape(-1, rows, pixels)


def rows_of(index, share):
    return pl.ds(pl.multiple_of(index * share, share), share)


def is_even(offsets, rows):
    return lax.rem(offsets[0, 0] // rows, 2) == 0


def pack_kernel(offsets, counts, measured, out):
    slots, _, pixels = measured.shape
    for slot in range(slots):
        live = jnp.where(slot < counts[0], 1.0, 0.0).astype(F32)
        for odd in range(2):
            rows = pl.ds(odd, pixels // 2, stride=2)
            out[slot, odd * pixels // 2 : (odd + 1) * pixels // 2] = measured[slot, rows] * live
        for entry in range(2):
            line = jnp.full((1, pixels), offsets[slot, entry], jnp.int32).astype(F32)
            out[slots, 2 * slot + entry : 2 * slot + entry + 1] = line


def middle_kernel(pixels, target, tile, *outs):
    *parts, offsets = outs
    planes = tile.shape[0]
    for slot in range(offsets.shape[0]):
        for entry in range(2):
            line = 2 * slot + entry
            value = target[target.shape[0] - 1, line : line + 1]
            offsets[slot, entry] = jnp.max(value).astype(jnp.int32)
    slot = 0
    for part in parts:
        for at in range(part.shape[0] // planes):
            part[at * planes : (at + 1) * planes] = cut(tile, offsets[slot, 1], pixels)
            slot += 1


def cut_kernel(pixels, chunks, own, far, tile, *outs):
    planes, rows, _ = tile.shape
    even = is_even(own, rows)
    for (first, size), near, cross in zip(chunks, outs[::2], outs[1::2], strict=True):
        for at in range(size):
            slot = first + at
            strip = at * planes
            near[strip : strip + planes] = cut(tile, jnp.where(even, own[slot, 1], far[slot, 1]), pixels)
            cross[strip : strip + planes] = cut(tile, jnp.where(even, far[slot, 1], own[slot, 1]), pixels)


def add_kernel(pixels, groups, own, middle, far, *refs):
    *parts, out = refs
    planes, rows, _ = out.shape
    even = is_even(own, rows)
    out[...] = jnp.zeros_like(out)
    lane = lax.broadcasted_iota(jnp.int32, (1, 1, pixels), 2)
    for (kind, first, size, unit), strips in zip(groups, parts):

        turned = []
        for at in range(size):
            slot = first + at
            if kind == "mid":
                column = middle[slot, 1]
            elif kind == "near":
                column = jnp.where(even, own[slot, 1], far[slot, 1])
            else:
                column = jnp.where(even, far[slot, 1], own[slot, 1])
            base, shift = place(column, out.shape[-1], pixels)
            part = strips[unit + at * planes : unit + (at + 1) * planes].reshape(-1, pixels)
            part = pltpu.roll(part, lax.rem(shift, pixels), 1).reshape(planes, rows, pixels)
            turned.append((base, shift, part))
        for base, shift, part in turned:
            out[:, :, pl.ds(base, pixels)] += jnp.where(lane >= shift, part, 0.0)
            beside = pl.ds(pl.multiple_of(base + pixels, pixels), pixels)
            out[:, :, beside] += jnp.where(lane < shift, part, 0.0)


def slot_kernel(first, size, ahead, own_offsets, *refs):
    offsets, mid, near, cross, target, probe, prop, tables, *refs = refs
    so_far, refs = (refs[0], refs[1:]) if first else (None, refs)
    given, refs = refs[:ahead], refs[ahead:]
    out_near, out_mid, out_cross, *shares = refs[:-5]
    window, patch, grads, exit_wave, far = refs[-5:]
    total = shares.pop()
    modes, _, pixels, _ = probe.shape
    planes, rows = mid.shape[0] // size, mid.shape[1]
    behind = given[0].shape[0] if given else 0
    for message, out in zip(given, (out_near, out_cross)):
        out[:behind] = message[...]
    even = is_even(own_offsets, rows)
    total[...] = so_far[...] if first else jnp.zeros_like(total)
    held = range(BATCH)

    def is_live(at):
        return jnp.max(target[first + at, :8]) > 0.0

    def leave(slots):
        for at in slots:
            for out, unit in ((out_near, behind), (out_mid, 0), (out_cross, behind)):
                out[pl.ds(unit + at * planes, planes)] = jnp.zeros((planes, rows, pixels), F32)

    def visit(slots):
        starts = [lax.rem(offsets[first + at, 0], rows) for at in slots]
        live = [jnp.where(is_live(at), 1.0, 0.0).astype(F32) for at in slots]
        for s, at in enumerate(slots):
            strip = pl.ds(at * planes, planes)
            window[:, :rows] = jnp.where(even, cross[strip], near[strip])
            window[:, rows : 2 * rows] = mid[strip]
            window[:, 2 * rows :] = jnp.where(even, near[strip], cross[strip])
            patch[s] = window[:, pl.ds(starts[s], pixels), :]
            total[2 * modes] += live[s] * (patch[s, 0] * patch[s, 0] + patch[s, 1] * patch[s, 1])
        all_modes = range(modes)
        groups = [
            [times((probe[m, 0], probe[m, 1]), (patch[s, 0], patch[s, 1])) for m in all_modes] for s in held
        ]
        groups = transform(tables, False, groups)
        groups = [[times((prop[0], prop[1]), wave) for wave in waves] for waves in groups]
        groups = transform(tables, True, groups)
        for s in held:
            for m in all_modes:
                exit_wave[s, m, 0], exit_wave[s, m, 1] = groups[s][m]
            groups[s] = [times(wave, (patch[s, 2], patch[s, 3])) for wave in groups[s]]
        groups = transform(tables, False, groups)
        for s, at in enumerate(slots):
            intensity = jnp.zeros((pixels, pixels), F32)
            for m in all_modes:
                wave = groups[s][m]
                far[s, m, 0], far[s, m, 1] = wave
                intensity = intensity + wave[0] * wave[0] + wave[1] * wave[1]
            misfit = 2.0 * live[s] * (intensity - target[first + at])
            groups[s] = [(misfit * far[s, m, 0], misfit * far[s, m, 1]) for m in all_modes]
        groups = transform(tables, True, groups)
        for s in held:
            grad_re, grad_im = jnp.zeros((pixels, pixels), F32), jnp.zeros((pixels, pixels), F32)
            for m in all_modes:
                re, im = conj_times((exit_wave[s, m, 0], exit_wave[s, m, 1]), groups[s][m])
                grad_re, grad_im = grad_re + re, grad_im + im
            grads[s, 2], grads[s, 3] = grad_re, grad_im
            groups[s] = [conj_times((patch[s, 2], patch[s, 3]), wave) for wave in groups[s]]
        groups = transform(tables, False, groups)
        groups = [[conj_times((prop[0], prop[1]), wave) for wave in waves] for waves in groups]
        groups = transform(tables, True, groups)
        for s in held:
            grad_re, grad_im = jnp.zeros((pixels, pixels), F32), jnp.zeros((pixels, pixels), F32)
            for m in all_modes:
                re, im = conj_times((patch[s, 0], patch[s, 1]), groups[s][m])
                total[2 * m] += re
                total[2 * m + 1] += im
                re, im = conj_times((probe[m, 0], probe[m, 1]), groups[s][m])
                grad_re, grad_im = grad_re + re, grad_im + im
            grads[s, 0], grads[s, 1] = grad_re, grad_im
        for s, at in enumerate(slots):
            window[...] = jnp.zeros_like(window)
            window[:, pl.ds(starts[s], pixels), :] = grads[s]
            strip = pl.ds(behind + at * planes, planes)
            out_near[strip] = jnp.where(even, window[:, 2 * rows :], window[:, :rows])
            out_mid[pl.ds(at * planes, planes)] = window[:, rows : 2 * rows]
            out_cross[strip] = jnp.where(even, window[:, :rows], window[:, 2 * rows :])

    def step(index, carry):
        slots = [index * BATCH + s for s in range(BATCH)]
        some = is_live(slots[0])
        pl.when(some)(lambda: visit(slots))
        pl.when(jnp.logical_not(some))(lambda: leave(slots))
        return carry

    lax.fori_loop(0, size // BATCH, step, 0)

    if shares:
        own, other = shares
        chips, _, share, _ = own.shape
        core = jnp.where(even, 0, 1)
        for chip in range(chips):
            for plane in range(2 * modes + 1):
                own[chip, plane] = total[plane, rows_of(2 * chip + core, share)]
                other[chip, plane] = total[plane, rows_of(2 * chip + 1 - core, share)]


def step_kernel(parts, out):
    summed = parts[0]
    for at in range(1, parts.shape[0]):
        summed = summed + parts[at]
    step = summed[:-1] / (summed[-1:] + 1.0)
    for at in range(out.shape[0]):
        out[at] = step


def order_kernel(rows, offsets, own, other, out):
    chips, _, share, _ = own.shape
    core = jnp.where(is_even(offsets, rows), 0, 1)
    for chip in range(chips):
        out[:, rows_of(2 * chip + core, share)] = own[chip]
        out[:, rows_of(2 * chip + 1 - core, share)] = other[chip]


def in_smem():
    return pl.BlockSpec(memory_space=pltpu.SMEM)


def in_vmem():
    return pl.BlockSpec(memory_space=pltpu.VMEM)


def local(object_slices, probe_modes, propagator_phase, measured, offsets, counts):
    slices, _, tile_rows, columns = object_slices.shape
    modes, _, pixels, _ = probe_modes.shape
    planes = 2 * slices
    peers = lax.axis_size(ROW)
    params = pltpu.CompilerParams(vmem_limit_bytes=VMEM_LIMIT)
    tile = object_slices.reshape(planes, tile_rows, columns)
    starts = [sum(CHUNKS[:i]) for i in range(len(CHUNKS))]

    pair = [(i, i ^ 1) for i in range(peers)]
    other_pair = [(i, (i - 1) % peers if i % 2 == 0 else (i + 1) % peers) for i in range(peers)]
    far = shifted(offsets, ROW, 2)

    chunks = list(zip(starts, CHUNKS))
    target = pl.pallas_call(
        pack_kernel,
        out_shape=jax.ShapeDtypeStruct((measured.shape[0] + 1, pixels, pixels), F32),
        in_specs=[in_smem()] * 2 + [in_vmem()],
        out_specs=in_vmem(),
        compiler_params=params,
        cost_estimate=pl.CostEstimate(flops=0, bytes_accessed=1 << 20, transcendentals=0),
    )(offsets, counts, measured)
    far, target = lax.optimization_barrier((far, target))
    target = shifted(target, ROW, 1)

    def units(count):
        return jax.ShapeDtypeStruct((count, tile_rows, pixels), F32)

    def strips(chunks, far):
        shapes = [units(size * planes) for _, size in chunks for _ in range(2)]
        outs = pl.pallas_call(
            functools.partial(cut_kernel, pixels, chunks),
            out_shape=shapes,
            in_specs=[in_smem()] * 2 + [in_vmem()],
            out_specs=[in_vmem()] * len(shapes),
            compiler_params=params,
            cost_estimate=pl.CostEstimate(flops=0, bytes_accessed=4 << 20, transcendentals=0),
        )(offsets, far, tile)
        return list(zip(outs[::2], outs[1::2]))

    def swapped(to_near, to_cross):
        return lax.ppermute(to_near, ROW, pair), lax.ppermute(to_cross, ROW, other_pair)

    far_later, target = lax.optimization_barrier((far, target))
    waiting = strips(chunks[:1], far) + strips(chunks[1:], far_later)
    *middles, middle = pl.pallas_call(
        functools.partial(middle_kernel, pixels),
        out_shape=[units(size * planes) for size in CHUNKS] + [jax.ShapeDtypeStruct(offsets.shape, jnp.int32)],
        in_specs=[in_vmem()] * 2,
        out_specs=[in_vmem()] * len(CHUNKS) + [in_smem()],
        compiler_params=params,
        cost_estimate=pl.CostEstimate(flops=0, bytes_accessed=4 << 20, transcendentals=0),
    )(target, tile)
    arrived = [swapped(*waiting[0])]
    if len(waiting) > 1:
        arrived[0], following, middles = lax.optimization_barrier((arrived[0], waiting[1], middles))
        arrived.append(swapped(*following))
    phase = jnp.concatenate([propagator_phase[0::2], propagator_phase[1::2]], axis=0)
    prop = jnp.stack([jnp.cos(phase), jnp.sin(phase)])
    tables = jnp.asarray(fourier_tables(pixels))

    share = pixels // peers
    total = ()
    mid, back, mid_groups, back_groups = [], [], [], []
    for index, (first, size) in enumerate(chunks):
        given = waiting[index + 2] if index + 2 < len(chunks) else ()
        ahead = CHUNKS[index + 2] * planes if given else 0
        sums = jax.ShapeDtypeStruct((2 * modes + 1, pixels, pixels), F32)
        part = jax.ShapeDtypeStruct((peers // 2, 2 * modes + 1, share, pixels), F32)
        shares = [part, part] if index == len(CHUNKS) - 1 else []
        message = units(ahead + size * planes)
        field = pltpu.VMEM((BATCH, planes, pixels, pixels), F32)
        kept = pltpu.VMEM((BATCH, modes, 2, pixels, pixels), F32)
        to_near, to_mid, to_cross, *total = pl.pallas_call(
            functools.partial(slot_kernel, first, size, len(given)),
            out_shape=[message, units(size * planes), message] + (shares or [sums]),
            in_specs=[in_smem()] * 2 + [in_vmem()] * (7 + len(total) + len(given)),
            out_specs=[in_vmem()] * (3 + (len(shares) or 1)),
            scratch_shapes=([pltpu.VMEM(sums.shape, F32)] if shares else [])
            + [pltpu.VMEM((planes, 3 * tile_rows, pixels), F32), field, field, kept, kept],
            compiler_params=params,
            cost_estimate=pl.CostEstimate(
                flops=size * 6 * modes * 3 * 16 * pixels**3, bytes_accessed=8 << 20, transcendentals=0
            ),
        )(offsets, middle, middles[index], *arrived[index], target, probe_modes, prop, tables, *total, *given)
        mid_groups.append(("mid", first, size, 0))
        mid.append(to_mid)
        message = swapped(to_near, to_cross)
        if given:
            arrived.append(message)
        back_groups += [(kind, first, size, ahead) for kind in ("near", "cross")]
        back.append(message)

    def added(groups, strips):
        return pl.pallas_call(
            functools.partial(add_kernel, pixels, groups),
            out_shape=jax.ShapeDtypeStruct(tile.shape, F32),
            in_specs=[in_smem()] * 3 + [in_vmem()] * len(strips),
            out_specs=in_vmem(),
            compiler_params=params,
            cost_estimate=pl.CostEstimate(flops=0, bytes_accessed=5 << 20, transcendentals=0),
        )(offsets, middle, far, *strips)

    own, other = total
    own, other, back[:-1] = lax.optimization_barrier((own, other, back[:-1]))
    both = own + lax.ppermute(other, ROW, pair)
    parts = lax.all_to_all(both, "chip", 0, 0)
    spread = pl.pallas_call(
        step_kernel,
        out_shape=jax.ShapeDtypeStruct((peers // 2, 2 * modes, share, pixels), F32),
        in_specs=[in_vmem()],
        out_specs=in_vmem(),
        compiler_params=params,
    )(parts)
    groups = mid_groups + back_groups
    strips = mid + [part for message in back for part in message]
    spread, strips = lax.optimization_barrier((spread, strips))
    gathered = lax.all_to_all(spread, "chip", 0, 0)
    gathered, strips = lax.optimization_barrier((gathered, strips))

    object_grad = added(groups, strips)
    object_grad = object_grad.reshape(object_slices.shape)

    probe_step = pl.pallas_call(
        functools.partial(order_kernel, tile_rows),
        out_shape=jax.ShapeDtypeStruct((2 * modes, pixels, pixels), F32),
        in_specs=[in_smem()] + [in_vmem()] * 2,
        out_specs=in_vmem(),
        compiler_params=params,
    )(offsets, gathered, lax.ppermute(gathered, ROW, pair)).reshape(probe_modes.shape)
    return (object_grad, probe_step)


def solution(mesh):
    groups, peers = mesh.shape["grp"], mesh.shape["row"]
    split = jax.sharding.Mesh(mesh.devices.reshape(groups, peers // 2, 2), ("grp",) + ROW)
    everywhere = ("grp",) + ROW
    in_specs = (
        P(None, None, everywhere, None),
        P("grp", None, None, None),
        P(),
        P(everywhere, None, None),
        P(everywhere, None),
        P(everywhere),
    )
    out_specs = (P(None, None, everywhere, None), P("grp", None, None, None))
    return jax.shard_map(local, mesh=split, in_specs=in_specs, out_specs=out_specs, check_vma=False)
```

```python
import functools

import jax
import jax.numpy as jnp
import numpy as np
from jax import lax
from jax.experimental import pallas as pl
from jax.experimental.pallas import tpu as pltpu
from jax.sharding import PartitionSpec as P

CHUNKS = (4, 4)
BATCH = 4
VMEM_LIMIT = 20 * 1024 * 1024
ROW = ("chip", "core")
F32 = jnp.float32
BF16 = jnp.bfloat16


def shifted(array, axis, by):
    peers = lax.axis_size(axis)
    return lax.ppermute(array, axis, [(i, (i + by) % peers) for i in range(peers)])


def real_form(matrix):
    return np.block([[matrix.real, -matrix.imag], [matrix.imag, matrix.real]]).astype(np.float32)


def two_pieces(matrix):
    high = matrix.astype(BF16)
    return high, (matrix - high.astype(np.float32)).astype(BF16)


def fourier_tables(pixels):
    half = pixels // 2
    kept, rows = np.arange(half)[:, None], np.arange(half)[None, :]
    lefts = []
    for odd in range(2):
        turns = (2 * kept + odd) * rows % pixels / pixels
        part = real_form(np.exp(-2j * np.pi * turns) / np.sqrt(pixels))
        for table in (part, part.T):
            high, low = two_pieces(table)
            lefts.append(np.block([[high, high], [low, np.zeros_like(low)]]))
    indices = np.arange(pixels)
    whole = np.exp(-2j * np.pi * (indices[:, None] * indices[None, :] % pixels) / pixels) / np.sqrt(pixels)
    rights = []
    for table in (real_form(whole).T, real_form(whole)):
        rights += two_pieces(table)
    return np.stack(lefts + rights)


def pieces(array):
    high = array.astype(BF16)
    return high, (array - high.astype(F32)).astype(BF16)


def from_left(tables, conj, waves):
    half = waves[0][0].shape[0] // 2
    pixels = 2 * half
    sides = []
    for odd in range(2):
        parts = []
        for wave in waves:
            if conj:
                parts.append(jnp.concatenate([part[odd * half : (odd + 1) * half] for part in wave], axis=0))
            elif odd:
                parts.append(jnp.concatenate([part[:half] - part[half:] for part in wave], axis=0))
            else:
                parts.append(jnp.concatenate([part[:half] + part[half:] for part in wave], axis=0))
        stacked = jnp.concatenate(pieces(jnp.concatenate(parts, axis=1)), axis=0)
        product = jnp.dot(tables[2 * odd + conj], stacked, preferred_element_type=F32)
        sides.append(product[:pixels] + product[pixels:])
    if conj:
        sides = [sides[0] + sides[1], sides[0] - sides[1]]
    turned = []
    for at in range(0, len(waves) * pixels, pixels):
        re = jnp.concatenate([side[:half, at : at + pixels] for side in sides], axis=0)
        im = jnp.concatenate([side[half:, at : at + pixels] for side in sides], axis=0)
        turned.append(jnp.concatenate([re, im], axis=1))
    return jnp.concatenate(turned, axis=0)


def transform(tables, conj, groups):
    right_high, right_low = tables[4 + 2 * conj], tables[5 + 2 * conj]
    right = jnp.concatenate([right_high, right_high, right_low], axis=0)
    halves = [pieces(from_left(tables, conj, waves)) for waves in groups]
    pixels = right.shape[1] // 2
    wholes = []
    for high, low in halves:
        whole = jnp.dot(jnp.concatenate([high, low, high], axis=1), right, preferred_element_type=F32)
        wholes.append(
            [
                (whole[at : at + pixels, :pixels], whole[at : at + pixels, pixels:])
                for at in range(0, whole.shape[0], pixels)
            ]
        )
    return wholes


def times(one, two):
    return one[0] * two[0] - one[1] * two[1], one[0] * two[1] + one[1] * two[0]


def conj_times(one, two):
    return one[0] * two[0] + one[1] * two[1], one[0] * two[1] - one[1] * two[0]


def place(column, columns, pixels):
    base = jnp.minimum(column // pixels * pixels, columns - 2 * pixels)
    return pl.multiple_of(base, pixels), column - base


def cut(tile, column, pixels):
    base, shift = place(column, tile.shape[-1], pixels)
    rows = tile.shape[1]
    wide = tile[:, :, pl.ds(base, 2 * pixels)].reshape(-1, 2 * pixels)
    turned = pltpu.roll(wide, 2 * pixels - shift, 1)
    return turned[:, :pixels].reshape(-1, rows, pixels)


def rows_of(index, share):
    return pl.ds(pl.multiple_of(index * share, share), share)


def is_even(offsets, rows):
    return lax.rem(offsets[0, 0] // rows, 2) == 0


def pack_kernel(offsets, counts, measured, out):
    slots, _, pixels = measured.shape
    for slot in range(slots):
        live = jnp.where(slot < counts[0], 1.0, 0.0).astype(F32)
        for odd in range(2):
            rows = pl.ds(odd, pixels // 2, stride=2)
            out[slot, odd * pixels // 2 : (odd + 1) * pixels // 2] = measured[slot, rows] * live
        for entry in range(2):
            line = jnp.full((1, pixels), offsets[slot, entry], jnp.int32).astype(F32)
            out[slots, 2 * slot + entry : 2 * slot + entry + 1] = line


def middle_kernel(pixels, target, tile, *outs):
    *parts, offsets = outs
    planes = tile.shape[0]
    for slot in range(offsets.shape[0]):
        for entry in range(2):
            line = 2 * slot + entry
            value = target[target.shape[0] - 1, line : line + 1]
            offsets[slot, entry] = jnp.max(value).astype(jnp.int32)
    slot = 0
    for part in parts:
        for at in range(part.shape[0] // planes):
            part[at * planes : (at + 1) * planes] = cut(tile, offsets[slot, 1], pixels)
            slot += 1


def cut_kernel(pixels, chunks, own, far, tile, *outs):
    planes, rows, _ = tile.shape
    even = is_even(own, rows)
    for (first, size), near, cross in zip(chunks, outs[::2], outs[1::2], strict=True):
        for at in range(size):
            slot = first + at
            strip = at * planes
            near[strip : strip + planes] = cut(tile, jnp.where(even, own[slot, 1], far[slot, 1]), pixels)
            cross[strip : strip + planes] = cut(tile, jnp.where(even, far[slot, 1], own[slot, 1]), pixels)


def own_kernel(pixels, own, tile, out):
    planes = tile.shape[0]
    for at in range(out.shape[0] // planes):
        out[at * planes : (at + 1) * planes] = cut(tile, own[at, 1], pixels)


def far_kernel(pixels, own, far, tile, up, near, down):
    planes, rows, _ = tile.shape
    even = is_even(own, rows)
    for at in range(up.shape[0] // planes):
        strip = slice(at * planes, (at + 1) * planes)
        down[strip] = cut(tile, far[at, 1], pixels)
        near[strip] = jnp.where(even, up[strip], down[strip])


def add_kernel(pixels, groups, own, middle, far, *refs):
    *parts, out = refs
    planes, rows, _ = out.shape
    even = is_even(own, rows)
    out[...] = jnp.zeros_like(out)
    lane = lax.broadcasted_iota(jnp.int32, (1, 1, pixels), 2)
    for (kind, first, size, unit), strips in zip(groups, parts):

        turned = []
        for at in range(size):
            slot = first + at
            if kind == "mid":
                column = middle[slot, 1]
            elif kind == "near":
                column = jnp.where(even, own[slot, 1], far[slot, 1])
            else:
                column = jnp.where(even, far[slot, 1], own[slot, 1])
            base, shift = place(column, out.shape[-1], pixels)
            part = strips[unit + at * planes : unit + (at + 1) * planes].reshape(-1, pixels)
            part = pltpu.roll(part, lax.rem(shift, pixels), 1).reshape(planes, rows, pixels)
            turned.append((base, shift, part))
        for base, shift, part in turned:
            out[:, :, pl.ds(base, pixels)] += jnp.where(lane >= shift, part, 0.0)
            beside = pl.ds(pl.multiple_of(base + pixels, pixels), pixels)
            out[:, :, beside] += jnp.where(lane < shift, part, 0.0)


def slot_kernel(first, size, ahead, own_offsets, *refs):
    offsets, mid, near, even_cross, odd_cross, target, probe, prop, tables, *refs = refs
    so_far, refs = (refs[0], refs[1:]) if first else (None, refs)
    given, refs = refs[:ahead], refs[ahead:]
    out_near, out_mid, out_cross, *shares = refs[:-5]
    window, patch, grads, exit_wave, far = refs[-5:]
    total = shares.pop()
    modes, _, pixels, _ = probe.shape
    planes, rows = mid.shape[0] // size, mid.shape[1]
    behind = given[0].shape[0] if given else 0
    for message, out in zip(given, (out_near, out_cross)):
        out[:behind] = message[...]
    even = is_even(own_offsets, rows)
    total[...] = so_far[...] if first else jnp.zeros_like(total)
    held = range(BATCH)

    def is_live(at):
        return jnp.max(target[first + at, :8]) > 0.0

    def leave(slots):
        for at in slots:
            for out, unit in ((out_near, behind), (out_mid, 0), (out_cross, behind)):
                out[pl.ds(unit + at * planes, planes)] = jnp.zeros((planes, rows, pixels), F32)

    def visit(slots):
        starts = [lax.rem(offsets[first + at, 0], rows) for at in slots]
        live = [jnp.where(is_live(at), 1.0, 0.0).astype(F32) for at in slots]
        for s, at in enumerate(slots):
            strip = pl.ds(at * planes, planes)
            window[:, :rows] = jnp.where(even, even_cross[strip], near[strip])
            window[:, rows : 2 * rows] = mid[strip]
            window[:, 2 * rows :] = jnp.where(even, near[strip], odd_cross[strip])
            patch[s] = window[:, pl.ds(starts[s], pixels), :]
            total[2 * modes] += live[s] * (patch[s, 0] * patch[s, 0] + patch[s, 1] * patch[s, 1])
        all_modes = range(modes)
        groups = [
            [times((probe[m, 0], probe[m, 1]), (patch[s, 0], patch[s, 1])) for m in all_modes] for s in held
        ]
        groups = transform(tables, False, groups)
        groups = [[times((prop[0], prop[1]), wave) for wave in waves] for waves in groups]
        groups = transform(tables, True, groups)
        for s in held:
            for m in all_modes:
                exit_wave[s, m, 0], exit_wave[s, m, 1] = groups[s][m]
            groups[s] = [times(wave, (patch[s, 2], patch[s, 3])) for wave in groups[s]]
        groups = transform(tables, False, groups)
        for s, at in enumerate(slots):
            intensity = jnp.zeros((pixels, pixels), F32)
            for m in all_modes:
                wave = groups[s][m]
                far[s, m, 0], far[s, m, 1] = wave
                intensity = intensity + wave[0] * wave[0] + wave[1] * wave[1]
            misfit = 2.0 * live[s] * (intensity - target[first + at])
            groups[s] = [(misfit * far[s, m, 0], misfit * far[s, m, 1]) for m in all_modes]
        groups = transform(tables, True, groups)
        for s in held:
            grad_re, grad_im = jnp.zeros((pixels, pixels), F32), jnp.zeros((pixels, pixels), F32)
            for m in all_modes:
                re, im = conj_times((exit_wave[s, m, 0], exit_wave[s, m, 1]), groups[s][m])
                grad_re, grad_im = grad_re + re, grad_im + im
            grads[s, 2], grads[s, 3] = grad_re, grad_im
            groups[s] = [conj_times((patch[s, 2], patch[s, 3]), wave) for wave in groups[s]]
        groups = transform(tables, False, groups)
        groups = [[conj_times((prop[0], prop[1]), wave) for wave in waves] for waves in groups]
        groups = transform(tables, True, groups)
        for s in held:
            grad_re, grad_im = jnp.zeros((pixels, pixels), F32), jnp.zeros((pixels, pixels), F32)
            for m in all_modes:
                re, im = conj_times((patch[s, 0], patch[s, 1]), groups[s][m])
                total[2 * m] += re
                total[2 * m + 1] += im
                re, im = conj_times((probe[m, 0], probe[m, 1]), groups[s][m])
                grad_re, grad_im = grad_re + re, grad_im + im
            grads[s, 0], grads[s, 1] = grad_re, grad_im
        for s, at in enumerate(slots):
            window[...] = jnp.zeros_like(window)
            window[:, pl.ds(starts[s], pixels), :] = grads[s]
            strip = pl.ds(behind + at * planes, planes)
            out_near[strip] = jnp.where(even, window[:, 2 * rows :], window[:, :rows])
            out_mid[pl.ds(at * planes, planes)] = window[:, rows : 2 * rows]
            out_cross[strip] = jnp.where(even, window[:, :rows], window[:, 2 * rows :])

    def step(index, carry):
        slots = [index * BATCH + s for s in range(BATCH)]
        some = is_live(slots[0])
        pl.when(some)(lambda: visit(slots))
        pl.when(jnp.logical_not(some))(lambda: leave(slots))
        return carry

    lax.fori_loop(0, size // BATCH, step, 0)

    if shares:
        own, other = shares
        chips, _, share, _ = own.shape
        core = jnp.where(even, 0, 1)
        for chip in range(chips):
            for plane in range(2 * modes + 1):
                own[chip, plane] = total[plane, rows_of(2 * chip + core, share)]
                other[chip, plane] = total[plane, rows_of(2 * chip + 1 - core, share)]


def step_kernel(parts, out):
    summed = parts[0]
    for at in range(1, parts.shape[0]):
        summed = summed + parts[at]
    step = summed[:-1] / (summed[-1:] + 1.0)
    for at in range(out.shape[0]):
        out[at] = step


def order_kernel(rows, offsets, own, other, out):
    chips, _, share, _ = own.shape
    core = jnp.where(is_even(offsets, rows), 0, 1)
    for chip in range(chips):
        out[:, rows_of(2 * chip + core, share)] = own[chip]
        out[:, rows_of(2 * chip + 1 - core, share)] = other[chip]


def in_smem():
    return pl.BlockSpec(memory_space=pltpu.SMEM)


def in_vmem():
    return pl.BlockSpec(memory_space=pltpu.VMEM)


def local(object_slices, probe_modes, propagator_phase, measured, offsets, counts):
    slices, _, tile_rows, columns = object_slices.shape
    modes, _, pixels, _ = probe_modes.shape
    planes = 2 * slices
    peers = lax.axis_size(ROW)
    params = pltpu.CompilerParams(vmem_limit_bytes=VMEM_LIMIT)
    tile = object_slices.reshape(planes, tile_rows, columns)
    starts = [sum(CHUNKS[:i]) for i in range(len(CHUNKS))]

    pair = [(i, i ^ 1) for i in range(peers)]
    other_pair = [(i, (i - 1) % peers if i % 2 == 0 else (i + 1) % peers) for i in range(peers)]
    far = shifted(offsets, ROW, 2)

    chunks = list(zip(starts, CHUNKS))
    target = pl.pallas_call(
        pack_kernel,
        out_shape=jax.ShapeDtypeStruct((measured.shape[0] + 1, pixels, pixels), F32),
        in_specs=[in_smem()] * 2 + [in_vmem()],
        out_specs=in_vmem(),
        compiler_params=params,
        cost_estimate=pl.CostEstimate(flops=0, bytes_accessed=1 << 20, transcendentals=0),
    )(offsets, counts, measured)
    def units(count):
        return jax.ShapeDtypeStruct((count, tile_rows, pixels), F32)

    first_units = units(CHUNKS[0] * planes)

    def cut_first(kernel, inputs, outputs):
        return pl.pallas_call(
            functools.partial(kernel, pixels),
            out_shape=[first_units] * outputs,
            in_specs=[in_smem() if part.dtype == jnp.int32 else in_vmem() for part in inputs],
            out_specs=[in_vmem()] * outputs,
            compiler_params=params,
            cost_estimate=pl.CostEstimate(flops=0, bytes_accessed=3 << 20, transcendentals=0),
        )(*inputs)

    (up,) = cut_first(own_kernel, (offsets, tile), 1)
    from_odd = lax.ppermute(up, ROW, other_pair[1::2])
    far, target, up = lax.optimization_barrier((far, target, up))
    target = shifted(target, ROW, 1)

    def strips(chunks, far):
        shapes = [units(size * planes) for _, size in chunks for _ in range(2)]
        outs = pl.pallas_call(
            functools.partial(cut_kernel, pixels, chunks),
            out_shape=shapes,
            in_specs=[in_smem()] * 2 + [in_vmem()],
            out_specs=[in_vmem()] * len(shapes),
            compiler_params=params,
            cost_estimate=pl.CostEstimate(flops=0, bytes_accessed=4 << 20, transcendentals=0),
        )(offsets, far, tile)
        return list(zip(outs[::2], outs[1::2]))

    def swapped(to_near, to_cross):
        return lax.ppermute(to_near, ROW, pair), lax.ppermute(to_cross, ROW, other_pair)

    to_near, down = cut_first(far_kernel, (offsets, far, tile, up), 2)
    from_even = lax.ppermute(down, ROW, other_pair[0::2])
    arrived = [(lax.ppermute(to_near, ROW, pair), from_odd, from_even)]
    far_later, target = lax.optimization_barrier((far, target))
    waiting = strips(chunks[1:], far_later)
    *middles, middle = pl.pallas_call(
        functools.partial(middle_kernel, pixels),
        out_shape=[units(size * planes) for size in CHUNKS] + [jax.ShapeDtypeStruct(offsets.shape, jnp.int32)],
        in_specs=[in_vmem()] * 2,
        out_specs=[in_vmem()] * len(CHUNKS) + [in_smem()],
        compiler_params=params,
        cost_estimate=pl.CostEstimate(flops=0, bytes_accessed=4 << 20, transcendentals=0),
    )(target, tile)
    for message in waiting:
        arrived[-1], message, middles = lax.optimization_barrier((arrived[-1], message, middles))
        to_near, to_cross = swapped(*message)
        arrived.append((to_near, to_cross, to_cross))
    phase = jnp.concatenate([propagator_phase[0::2], propagator_phase[1::2]], axis=0)
    prop = jnp.stack([jnp.cos(phase), jnp.sin(phase)])
    tables = jnp.asarray(fourier_tables(pixels))

    share = pixels // peers
    total = ()
    mid, back, mid_groups, back_groups = [], [], [], []
    for index, (first, size) in enumerate(chunks):
        given, ahead = (), 0
        sums = jax.ShapeDtypeStruct((2 * modes + 1, pixels, pixels), F32)
        part = jax.ShapeDtypeStruct((peers // 2, 2 * modes + 1, share, pixels), F32)
        shares = [part, part] if index == len(CHUNKS) - 1 else []
        message = units(ahead + size * planes)
        field = pltpu.VMEM((BATCH, planes, pixels, pixels), F32)
        kept = pltpu.VMEM((BATCH, modes, 2, pixels, pixels), F32)
        to_near, to_mid, to_cross, *total = pl.pallas_call(
            functools.partial(slot_kernel, first, size, len(given)),
            out_shape=[message, units(size * planes), message] + (shares or [sums]),
            in_specs=[in_smem()] * 2 + [in_vmem()] * (8 + len(total) + len(given)),
            out_specs=[in_vmem()] * (3 + (len(shares) or 1)),
            scratch_shapes=([pltpu.VMEM(sums.shape, F32)] if shares else [])
            + [pltpu.VMEM((planes, 3 * tile_rows, pixels), F32), field, field, kept, kept],
            compiler_params=params,
            cost_estimate=pl.CostEstimate(
                flops=size * 6 * modes * 3 * 16 * pixels**3, bytes_accessed=8 << 20, transcendentals=0
            ),
        )(offsets, middle, middles[index], *arrived[index], target, probe_modes, prop, tables, *total, *given)
        mid_groups.append(("mid", first, size, 0))
        mid.append(to_mid)
        message = swapped(to_near, to_cross)
        back_groups += [(kind, first, size, ahead) for kind in ("near", "cross")]
        back.append(message)

    def added(groups, strips):
        return pl.pallas_call(
            functools.partial(add_kernel, pixels, groups),
            out_shape=jax.ShapeDtypeStruct(tile.shape, F32),
            in_specs=[in_smem()] * 3 + [in_vmem()] * len(strips),
            out_specs=in_vmem(),
            compiler_params=params,
            cost_estimate=pl.CostEstimate(flops=0, bytes_accessed=5 << 20, transcendentals=0),
        )(offsets, middle, far, *strips)

    own, other = total
    own, other, back[:-1] = lax.optimization_barrier((own, other, back[:-1]))
    both = own + lax.ppermute(other, ROW, pair)
    parts = lax.all_to_all(both, "chip", 0, 0)
    spread = pl.pallas_call(
        step_kernel,
        out_shape=jax.ShapeDtypeStruct((peers // 2, 2 * modes, share, pixels), F32),
        in_specs=[in_vmem()],
        out_specs=in_vmem(),
        compiler_params=params,
    )(parts)
    groups = mid_groups + back_groups
    strips = mid + [part for message in back for part in message]
    spread, strips = lax.optimization_barrier((spread, strips))
    gathered = lax.all_to_all(spread, "chip", 0, 0)
    gathered, strips = lax.optimization_barrier((gathered, strips))

    object_grad = added(groups, strips)
    object_grad = object_grad.reshape(object_slices.shape)

    probe_step = pl.pallas_call(
        functools.partial(order_kernel, tile_rows),
        out_shape=jax.ShapeDtypeStruct((2 * modes, pixels, pixels), F32),
        in_specs=[in_smem()] + [in_vmem()] * 2,
        out_specs=in_vmem(),
        compiler_params=params,
    )(offsets, gathered, lax.ppermute(gathered, ROW, pair)).reshape(probe_modes.shape)
    return (object_grad, probe_step)


def solution(mesh):
    groups, peers = mesh.shape["grp"], mesh.shape["row"]
    split = jax.sharding.Mesh(mesh.devices.reshape(groups, peers // 2, 2), ("grp",) + ROW)
    everywhere = ("grp",) + ROW
    in_specs = (
        P(None, None, everywhere, None),
        P("grp", None, None, None),
        P(),
        P(everywhere, None, None),
        P(everywhere, None),
        P(everywhere),
    )
    out_specs = (P(None, None, everywhere, None), P("grp", None, None, None))
    return jax.shard_map(local, mesh=split, in_specs=in_specs, out_specs=out_specs, check_vma=False)
```

```python
import functools

import jax
import jax.numpy as jnp
import numpy as np
from jax import lax
from jax.experimental import pallas as pl
from jax.experimental.pallas import tpu as pltpu
from jax.sharding import PartitionSpec as P

CHUNKS = (4, 4)
BATCH = 4
VMEM_LIMIT = 40 * 1024 * 1024
ROW = ("chip", "core")
F32 = jnp.float32
BF16 = jnp.bfloat16


def shifted(array, axis, by):
    peers = lax.axis_size(axis)
    return lax.ppermute(array, axis, [(i, (i + by) % peers) for i in range(peers)])


def real_form(matrix):
    return np.block([[matrix.real, -matrix.imag], [matrix.imag, matrix.real]]).astype(np.float32)


def two_pieces(matrix):
    high = matrix.astype(BF16)
    return high, (matrix - high.astype(np.float32)).astype(BF16)


def fourier_tables(pixels):
    half = pixels // 2
    kept, rows = np.arange(half)[:, None], np.arange(half)[None, :]
    lefts = []
    for odd in range(2):
        turns = (2 * kept + odd) * rows % pixels / pixels
        part = real_form(np.exp(-2j * np.pi * turns) / np.sqrt(pixels))
        for table in (part, part.T):
            high, low = two_pieces(table)
            lefts.append(np.block([[high, high], [low, np.zeros_like(low)]]))
    indices = np.arange(pixels)
    whole = np.exp(-2j * np.pi * (indices[:, None] * indices[None, :] % pixels) / pixels) / np.sqrt(pixels)
    rights = []
    for table in (real_form(whole).T, real_form(whole)):
        rights += two_pieces(table)
    return np.stack(lefts + rights)


def pieces(array):
    high = array.astype(BF16)
    return high, (array - high.astype(F32)).astype(BF16)


def from_left(tables, conj, waves):
    half = waves[0][0].shape[0] // 2
    pixels = 2 * half
    sides = []
    for odd in range(2):
        parts = []
        for wave in waves:
            if conj:
                parts.append(jnp.concatenate([part[odd * half : (odd + 1) * half] for part in wave], axis=0))
            elif odd:
                parts.append(jnp.concatenate([part[:half] - part[half:] for part in wave], axis=0))
            else:
                parts.append(jnp.concatenate([part[:half] + part[half:] for part in wave], axis=0))
        stacked = jnp.concatenate(pieces(jnp.concatenate(parts, axis=1)), axis=0)
        product = jnp.dot(tables[2 * odd + conj], stacked, preferred_element_type=F32)
        sides.append(product[:pixels] + product[pixels:])
    if conj:
        sides = [sides[0] + sides[1], sides[0] - sides[1]]
    turned = []
    for at in range(0, len(waves) * pixels, pixels):
        re = jnp.concatenate([side[:half, at : at + pixels] for side in sides], axis=0)
        im = jnp.concatenate([side[half:, at : at + pixels] for side in sides], axis=0)
        turned.append(jnp.concatenate([re, im], axis=1))
    return jnp.concatenate(turned, axis=0)


def transform(tables, conj, groups):
    right_high, right_low = tables[4 + 2 * conj], tables[5 + 2 * conj]
    right = jnp.concatenate([right_high, right_high, right_low], axis=0)
    halves = [pieces(from_left(tables, conj, waves)) for waves in groups]
    pixels = right.shape[1] // 2
    wholes = []
    for high, low in halves:
        whole = jnp.dot(jnp.concatenate([high, low, high], axis=1), right, preferred_element_type=F32)
        wholes.append(
            [
                (whole[at : at + pixels, :pixels], whole[at : at + pixels, pixels:])
                for at in range(0, whole.shape[0], pixels)
            ]
        )
    return wholes


def times(one, two):
    return one[0] * two[0] - one[1] * two[1], one[0] * two[1] + one[1] * two[0]


def conj_times(one, two):
    return one[0] * two[0] + one[1] * two[1], one[0] * two[1] - one[1] * two[0]


def place(column, columns, pixels):
    base = jnp.minimum(column // pixels * pixels, columns - 2 * pixels)
    return pl.multiple_of(base, pixels), column - base


def cut(tile, column, pixels):
    base, shift = place(column, tile.shape[-1], pixels)
    rows = tile.shape[1]
    wide = tile[:, :, pl.ds(base, 2 * pixels)].reshape(-1, 2 * pixels)
    turned = pltpu.roll(wide, 2 * pixels - shift, 1)
    return turned[:, :pixels].reshape(-1, rows, pixels)


def rows_of(index, share):
    return pl.ds(pl.multiple_of(index * share, share), share)


def is_even(offsets, rows):
    return lax.rem(offsets[0, 0] // rows, 2) == 0


def pack_kernel(offsets, counts, measured, out):
    slots, _, pixels = measured.shape
    for slot in range(slots):
        live = jnp.where(slot < counts[0], 1.0, 0.0).astype(F32)
        for odd in range(2):
            rows = pl.ds(odd, pixels // 2, stride=2)
            out[slot, odd * pixels // 2 : (odd + 1) * pixels // 2] = measured[slot, rows] * live
        for entry in range(2):
            line = jnp.full((1, pixels), offsets[slot, entry], jnp.int32).astype(F32)
            out[slots, 2 * slot + entry : 2 * slot + entry + 1] = line


def middle_kernel(pixels, target, tile, *outs):
    *parts, offsets = outs
    planes = tile.shape[0]
    for slot in range(offsets.shape[0]):
        for entry in range(2):
            line = 2 * slot + entry
            value = target[target.shape[0] - 1, line : line + 1]
            offsets[slot, entry] = jnp.max(value).astype(jnp.int32)
    slot = 0
    for part in parts:
        for at in range(part.shape[0] // planes):
            part[at * planes : (at + 1) * planes] = cut(tile, offsets[slot, 1], pixels)
            slot += 1


def cut_kernel(pixels, chunks, own, far, tile, *outs):
    planes, rows, _ = tile.shape
    even = is_even(own, rows)
    for (first, size), near, cross in zip(chunks, outs[::2], outs[1::2], strict=True):
        for at in range(size):
            slot = first + at
            strip = at * planes
            near[strip : strip + planes] = cut(tile, jnp.where(even, own[slot, 1], far[slot, 1]), pixels)
            cross[strip : strip + planes] = cut(tile, jnp.where(even, far[slot, 1], own[slot, 1]), pixels)


def add_kernel(pixels, groups, own, middle, far, *refs):
    *parts, out = refs
    planes, rows, _ = out.shape
    even = is_even(own, rows)
    out[...] = jnp.zeros_like(out)
    lane = lax.broadcasted_iota(jnp.int32, (1, 1, pixels), 2)
    for (kind, first, size, unit), strips in zip(groups, parts):

        turned = []
        for at in range(size):
            slot = first + at
            if kind == "mid":
                column = middle[slot, 1]
            elif kind == "near":
                column = jnp.where(even, own[slot, 1], far[slot, 1])
            else:
                column = jnp.where(even, far[slot, 1], own[slot, 1])
            base, shift = place(column, out.shape[-1], pixels)
            part = strips[unit + at * planes : unit + (at + 1) * planes].reshape(-1, pixels)
            part = pltpu.roll(part, lax.rem(shift, pixels), 1).reshape(planes, rows, pixels)
            turned.append((base, shift, part))
        for base, shift, part in turned:
            out[:, :, pl.ds(base, pixels)] += jnp.where(lane >= shift, part, 0.0)
            beside = pl.ds(pl.multiple_of(base + pixels, pixels), pixels)
            out[:, :, beside] += jnp.where(lane < shift, part, 0.0)


def slot_kernel(first, size, ahead, own_offsets, *refs):
    offsets, mid, near, cross, target, probe, prop, tables, *refs = refs
    so_far, refs = (refs[0], refs[1:]) if first else (None, refs)
    given, refs = refs[:ahead], refs[ahead:]
    out_near, out_mid, out_cross, *shares = refs[:-5]
    window, patch, grads, exit_wave, far = refs[-5:]
    total = shares.pop()
    modes, _, pixels, _ = probe.shape
    planes, rows = mid.shape[0] // size, mid.shape[1]
    behind = given[0].shape[0] if given else 0
    for message, out in zip(given, (out_near, out_cross)):
        out[:behind] = message[...]
    even = is_even(own_offsets, rows)
    total[...] = so_far[...] if first else jnp.zeros_like(total)
    held = range(BATCH)

    def is_live(at):
        return jnp.max(target[first + at, :8]) > 0.0

    def leave(slots):
        for at in slots:
            for out, unit in ((out_near, behind), (out_mid, 0), (out_cross, behind)):
                out[pl.ds(unit + at * planes, planes)] = jnp.zeros((planes, rows, pixels), F32)

    def visit(slots):
        starts = [lax.rem(offsets[first + at, 0], rows) for at in slots]
        live = [jnp.where(is_live(at), 1.0, 0.0).astype(F32) for at in slots]
        for s, at in enumerate(slots):
            strip = pl.ds(at * planes, planes)
            window[:, :rows] = jnp.where(even, cross[strip], near[strip])
            window[:, rows : 2 * rows] = mid[strip]
            window[:, 2 * rows :] = jnp.where(even, near[strip], cross[strip])
            patch[s] = window[:, pl.ds(starts[s], pixels), :]
            total[2 * modes] += live[s] * (patch[s, 0] * patch[s, 0] + patch[s, 1] * patch[s, 1])
        all_modes = range(modes)
        groups = [
            [times((probe[m, 0], probe[m, 1]), (patch[s, 0], patch[s, 1])) for m in all_modes] for s in held
        ]
        groups = transform(tables, False, groups)
        groups = [[times((prop[0], prop[1]), wave) for wave in waves] for waves in groups]
        groups = transform(tables, True, groups)
        for s in held:
            for m in all_modes:
                exit_wave[s, m, 0], exit_wave[s, m, 1] = groups[s][m]
            groups[s] = [times(wave, (patch[s, 2], patch[s, 3])) for wave in groups[s]]
        groups = transform(tables, False, groups)
        for s, at in enumerate(slots):
            intensity = jnp.zeros((pixels, pixels), F32)
            for m in all_modes:
                wave = groups[s][m]
                far[s, m, 0], far[s, m, 1] = wave
                intensity = intensity + wave[0] * wave[0] + wave[1] * wave[1]
            misfit = 2.0 * live[s] * (intensity - target[first + at])
            groups[s] = [(misfit * far[s, m, 0], misfit * far[s, m, 1]) for m in all_modes]
        groups = transform(tables, True, groups)
        for s in held:
            grad_re, grad_im = jnp.zeros((pixels, pixels), F32), jnp.zeros((pixels, pixels), F32)
            for m in all_modes:
                re, im = conj_times((exit_wave[s, m, 0], exit_wave[s, m, 1]), groups[s][m])
                grad_re, grad_im = grad_re + re, grad_im + im
            grads[s, 2], grads[s, 3] = grad_re, grad_im
            groups[s] = [conj_times((patch[s, 2], patch[s, 3]), wave) for wave in groups[s]]
        groups = transform(tables, False, groups)
        groups = [[conj_times((prop[0], prop[1]), wave) for wave in waves] for waves in groups]
        groups = transform(tables, True, groups)
        for s in held:
            grad_re, grad_im = jnp.zeros((pixels, pixels), F32), jnp.zeros((pixels, pixels), F32)
            for m in all_modes:
                re, im = conj_times((patch[s, 0], patch[s, 1]), groups[s][m])
                total[2 * m] += re
                total[2 * m + 1] += im
                re, im = conj_times((probe[m, 0], probe[m, 1]), groups[s][m])
                grad_re, grad_im = grad_re + re, grad_im + im
            grads[s, 0], grads[s, 1] = grad_re, grad_im
        for s, at in enumerate(slots):
            window[...] = jnp.zeros_like(window)
            window[:, pl.ds(starts[s], pixels), :] = grads[s]
            strip = pl.ds(behind + at * planes, planes)
            out_near[strip] = jnp.where(even, window[:, 2 * rows :], window[:, :rows])
            out_mid[pl.ds(at * planes, planes)] = window[:, rows : 2 * rows]
            out_cross[strip] = jnp.where(even, window[:, :rows], window[:, 2 * rows :])

    def step(index, carry):
        slots = [index * BATCH + s for s in range(BATCH)]
        some = is_live(slots[0])
        pl.when(some)(lambda: visit(slots))
        pl.when(jnp.logical_not(some))(lambda: leave(slots))
        return carry

    lax.fori_loop(0, size // BATCH, step, 0)

    if shares:
        own, other = shares
        chips, _, share, _ = own.shape
        core = jnp.where(even, 0, 1)
        for chip in range(chips):
            for plane in range(2 * modes + 1):
                own[chip, plane] = total[plane, rows_of(2 * chip + core, share)]
                other[chip, plane] = total[plane, rows_of(2 * chip + 1 - core, share)]


def step_kernel(parts, out):
    summed = parts[0]
    for at in range(1, parts.shape[0]):
        summed = summed + parts[at]
    step = summed[:-1] / (summed[-1:] + 1.0)
    for at in range(out.shape[0]):
        out[at] = step


def order_kernel(rows, offsets, own, other, out):
    chips, _, share, _ = own.shape
    core = jnp.where(is_even(offsets, rows), 0, 1)
    for chip in range(chips):
        out[:, rows_of(2 * chip + core, share)] = own[chip]
        out[:, rows_of(2 * chip + 1 - core, share)] = other[chip]


def in_smem():
    return pl.BlockSpec(memory_space=pltpu.SMEM)


def in_vmem():
    return pl.BlockSpec(memory_space=pltpu.VMEM)


def local(object_slices, probe_modes, propagator_phase, measured, offsets, counts):
    slices, _, tile_rows, columns = object_slices.shape
    modes, _, pixels, _ = probe_modes.shape
    planes = 2 * slices
    peers = lax.axis_size(ROW)
    params = pltpu.CompilerParams(vmem_limit_bytes=VMEM_LIMIT)
    tile = object_slices.reshape(planes, tile_rows, columns)
    starts = [sum(CHUNKS[:i]) for i in range(len(CHUNKS))]

    pair = [(i, i ^ 1) for i in range(peers)]
    other_pair = [(i, (i - 1) % peers if i % 2 == 0 else (i + 1) % peers) for i in range(peers)]
    far = shifted(offsets, ROW, 2)

    chunks = list(zip(starts, CHUNKS))
    target = pl.pallas_call(
        pack_kernel,
        out_shape=jax.ShapeDtypeStruct((measured.shape[0] + 1, pixels, pixels), F32),
        in_specs=[in_smem()] * 2 + [in_vmem()],
        out_specs=in_vmem(),
        compiler_params=params,
        cost_estimate=pl.CostEstimate(flops=0, bytes_accessed=1 << 20, transcendentals=0),
    )(offsets, counts, measured)
    far, target = lax.optimization_barrier((far, target))
    target = shifted(target, ROW, 1)

    def units(count):
        return jax.ShapeDtypeStruct((count, tile_rows, pixels), F32)

    def strips(chunks, far):
        shapes = [units(size * planes) for _, size in chunks for _ in range(2)]
        outs = pl.pallas_call(
            functools.partial(cut_kernel, pixels, chunks),
            out_shape=shapes,
            in_specs=[in_smem()] * 2 + [in_vmem()],
            out_specs=[in_vmem()] * len(shapes),
            compiler_params=params,
            cost_estimate=pl.CostEstimate(flops=0, bytes_accessed=4 << 20, transcendentals=0),
        )(offsets, far, tile)
        return list(zip(outs[::2], outs[1::2]))

    def swapped(to_near, to_cross):
        return lax.ppermute(to_near, ROW, pair), lax.ppermute(to_cross, ROW, other_pair)

    far_later, target = lax.optimization_barrier((far, target))
    waiting = strips(chunks[:1], far) + strips(chunks[1:], far_later)
    *middles, middle = pl.pallas_call(
        functools.partial(middle_kernel, pixels),
        out_shape=[units(size * planes) for size in CHUNKS] + [jax.ShapeDtypeStruct(offsets.shape, jnp.int32)],
        in_specs=[in_vmem()] * 2,
        out_specs=[in_vmem()] * len(CHUNKS) + [in_smem()],
        compiler_params=params,
        cost_estimate=pl.CostEstimate(flops=0, bytes_accessed=4 << 20, transcendentals=0),
    )(target, tile)
    arrived = [swapped(*waiting[0])]
    if len(waiting) > 1:
        arrived[0], following, middles = lax.optimization_barrier((arrived[0], waiting[1], middles))
        arrived.append(swapped(*following))
    phase = jnp.concatenate([propagator_phase[0::2], propagator_phase[1::2]], axis=0)
    prop = jnp.stack([jnp.cos(phase), jnp.sin(phase)])
    tables = jnp.asarray(fourier_tables(pixels))

    share = pixels // peers
    total = ()
    mid, back, mid_groups, back_groups = [], [], [], []
    for index, (first, size) in enumerate(chunks):
        given = waiting[index + 2] if index + 2 < len(chunks) else ()
        ahead = CHUNKS[index + 2] * planes if given else 0
        sums = jax.ShapeDtypeStruct((2 * modes + 1, pixels, pixels), F32)
        part = jax.ShapeDtypeStruct((peers // 2, 2 * modes + 1, share, pixels), F32)
        shares = [part, part] if index == len(CHUNKS) - 1 else []
        message = units(ahead + size * planes)
        field = pltpu.VMEM((BATCH, planes, pixels, pixels), F32)
        kept = pltpu.VMEM((BATCH, modes, 2, pixels, pixels), F32)
        to_near, to_mid, to_cross, *total = pl.pallas_call(
            functools.partial(slot_kernel, first, size, len(given)),
            out_shape=[message, units(size * planes), message] + (shares or [sums]),
            in_specs=[in_smem()] * 2 + [in_vmem()] * (7 + len(total) + len(given)),
            out_specs=[in_vmem()] * (3 + (len(shares) or 1)),
            scratch_shapes=([pltpu.VMEM(sums.shape, F32)] if shares else [])
            + [pltpu.VMEM((planes, 3 * tile_rows, pixels), F32), field, field, kept, kept],
            compiler_params=params,
            cost_estimate=pl.CostEstimate(
                flops=size * 6 * modes * 3 * 16 * pixels**3, bytes_accessed=8 << 20, transcendentals=0
            ),
        )(offsets, middle, middles[index], *arrived[index], target, probe_modes, prop, tables, *total, *given)
        mid_groups.append(("mid", first, size, 0))
        mid.append(to_mid)
        message = swapped(to_near, to_cross)
        if given:
            arrived.append(message)
        back_groups += [(kind, first, size, ahead) for kind in ("near", "cross")]
        back.append(message)

    def added(groups, strips):
        return pl.pallas_call(
            functools.partial(add_kernel, pixels, groups),
            out_shape=jax.ShapeDtypeStruct(tile.shape, F32),
            in_specs=[in_smem()] * 3 + [in_vmem()] * len(strips),
            out_specs=in_vmem(),
            compiler_params=params,
            cost_estimate=pl.CostEstimate(flops=0, bytes_accessed=5 << 20, transcendentals=0),
        )(offsets, middle, far, *strips)

    own, other = total
    own, other, back[:-1] = lax.optimization_barrier((own, other, back[:-1]))
    both = own + lax.ppermute(other, ROW, pair)
    parts = lax.all_to_all(both, "chip", 0, 0)
    spread = pl.pallas_call(
        step_kernel,
        out_shape=jax.ShapeDtypeStruct((peers // 2, 2 * modes, share, pixels), F32),
        in_specs=[in_vmem()],
        out_specs=in_vmem(),
        compiler_params=params,
    )(parts)
    groups = mid_groups + back_groups
    strips = mid + [part for message in back for part in message]
    spread, strips = lax.optimization_barrier((spread, strips))
    gathered = lax.all_to_all(spread, "chip", 0, 0)
    object_grad = added(groups, strips)
    gathered, object_grad = lax.optimization_barrier((gathered, object_grad))
    object_grad = object_grad.reshape(object_slices.shape)

    probe_step = pl.pallas_call(
        functools.partial(order_kernel, tile_rows),
        out_shape=jax.ShapeDtypeStruct((2 * modes, pixels, pixels), F32),
        in_specs=[in_smem()] + [in_vmem()] * 2,
        out_specs=in_vmem(),
        compiler_params=params,
    )(offsets, gathered, lax.ppermute(gathered, ROW, pair)).reshape(probe_modes.shape)
    return (object_grad, probe_step)


def solution(mesh):
    groups, peers = mesh.shape["grp"], mesh.shape["row"]
    split = jax.sharding.Mesh(mesh.devices.reshape(groups, peers // 2, 2), ("grp",) + ROW)
    everywhere = ("grp",) + ROW
    in_specs = (
        P(None, None, everywhere, None),
        P("grp", None, None, None),
        P(),
        P(everywhere, None, None),
        P(everywhere, None),
        P(everywhere),
    )
    out_specs = (P(None, None, everywhere, None), P("grp", None, None, None))
    return jax.shard_map(local, mesh=split, in_specs=in_specs, out_specs=out_specs, check_vma=False)
```

```python
import functools

import jax
import jax.numpy as jnp
import numpy as np
from jax import lax
from jax.experimental import pallas as pl
from jax.experimental.pallas import tpu as pltpu
from jax.sharding import PartitionSpec as P

CHUNKS = (4, 4)
BATCH = 4
VMEM_LIMIT = 40 * 1024 * 1024
SMALL_LIMIT = 16 * 1024 * 1024
ROW = ("chip", "core")
F32 = jnp.float32
BF16 = jnp.bfloat16


def shifted(array, axis, by):
    peers = lax.axis_size(axis)
    return lax.ppermute(array, axis, [(i, (i + by) % peers) for i in range(peers)])


def real_form(matrix):
    return np.block([[matrix.real, -matrix.imag], [matrix.imag, matrix.real]]).astype(np.float32)


def two_pieces(matrix):
    high = matrix.astype(BF16)
    return high, (matrix - high.astype(np.float32)).astype(BF16)


def fourier_tables(pixels):
    half = pixels // 2
    kept, rows = np.arange(half)[:, None], np.arange(half)[None, :]
    lefts = []
    for odd in range(2):
        turns = (2 * kept + odd) * rows % pixels / pixels
        part = real_form(np.exp(-2j * np.pi * turns) / np.sqrt(pixels))
        for table in (part, part.T):
            high, low = two_pieces(table)
            lefts.append(np.block([[high, high], [low, np.zeros_like(low)]]))
    indices = np.arange(pixels)
    whole = np.exp(-2j * np.pi * (indices[:, None] * indices[None, :] % pixels) / pixels) / np.sqrt(pixels)
    rights = []
    for table in (real_form(whole).T, real_form(whole)):
        rights += two_pieces(table)
    return np.stack(lefts + rights)


def pieces(array):
    high = array.astype(BF16)
    return high, (array - high.astype(F32)).astype(BF16)


def from_left(tables, conj, waves):
    half = waves[0][0].shape[0] // 2
    pixels = 2 * half
    sides = []
    for odd in range(2):
        parts = []
        for wave in waves:
            if conj:
                parts.append(jnp.concatenate([part[odd * half : (odd + 1) * half] for part in wave], axis=0))
            elif odd:
                parts.append(jnp.concatenate([part[:half] - part[half:] for part in wave], axis=0))
            else:
                parts.append(jnp.concatenate([part[:half] + part[half:] for part in wave], axis=0))
        stacked = jnp.concatenate(pieces(jnp.concatenate(parts, axis=1)), axis=0)
        product = jnp.dot(tables[2 * odd + conj], stacked, preferred_element_type=F32)
        sides.append(product[:pixels] + product[pixels:])
    if conj:
        sides = [sides[0] + sides[1], sides[0] - sides[1]]
    turned = []
    for at in range(0, len(waves) * pixels, pixels):
        re = jnp.concatenate([side[:half, at : at + pixels] for side in sides], axis=0)
        im = jnp.concatenate([side[half:, at : at + pixels] for side in sides], axis=0)
        turned.append(jnp.concatenate([re, im], axis=1))
    return jnp.concatenate(turned, axis=0)


def transform(tables, conj, groups):
    right_high, right_low = tables[4 + 2 * conj], tables[5 + 2 * conj]
    right = jnp.concatenate([right_high, right_high, right_low], axis=0)
    halves = [pieces(from_left(tables, conj, waves)) for waves in groups]
    pixels = right.shape[1] // 2
    wholes = []
    for high, low in halves:
        whole = jnp.dot(jnp.concatenate([high, low, high], axis=1), right, preferred_element_type=F32)
        wholes.append(
            [
                (whole[at : at + pixels, :pixels], whole[at : at + pixels, pixels:])
                for at in range(0, whole.shape[0], pixels)
            ]
        )
    return wholes


def times(one, two):
    return one[0] * two[0] - one[1] * two[1], one[0] * two[1] + one[1] * two[0]


def conj_times(one, two):
    return one[0] * two[0] + one[1] * two[1], one[0] * two[1] - one[1] * two[0]


def place(column, columns, pixels):
    base = jnp.minimum(column // pixels * pixels, columns - 2 * pixels)
    return pl.multiple_of(base, pixels), column - base


def cut(tile, column, pixels):
    base, shift = place(column, tile.shape[-1], pixels)
    rows = tile.shape[1]
    wide = tile[:, :, pl.ds(base, 2 * pixels)].reshape(-1, 2 * pixels)
    turned = pltpu.roll(wide, 2 * pixels - shift, 1)
    return turned[:, :pixels].reshape(-1, rows, pixels)


def rows_of(index, share):
    return pl.ds(pl.multiple_of(index * share, share), share)


def is_even(offsets, rows):
    return lax.rem(offsets[0, 0] // rows, 2) == 0


def pack_kernel(offsets, counts, measured, out):
    slots, _, pixels = measured.shape
    for slot in range(slots):
        live = jnp.where(slot < counts[0], 1.0, 0.0).astype(F32)
        for odd in range(2):
            rows = pl.ds(odd, pixels // 2, stride=2)
            out[slot, odd * pixels // 2 : (odd + 1) * pixels // 2] = measured[slot, rows] * live
        for entry in range(2):
            line = jnp.full((1, pixels), offsets[slot, entry], jnp.int32).astype(F32)
            out[slots, 2 * slot + entry : 2 * slot + entry + 1] = line


def middle_kernel(pixels, target, tile, *outs):
    *parts, offsets = outs
    planes = tile.shape[0]
    for slot in range(offsets.shape[0]):
        for entry in range(2):
            line = 2 * slot + entry
            value = target[target.shape[0] - 1, line : line + 1]
            offsets[slot, entry] = jnp.max(value).astype(jnp.int32)
    slot = 0
    for part in parts:
        for at in range(part.shape[0] // planes):
            part[at * planes : (at + 1) * planes] = cut(tile, offsets[slot, 1], pixels)
            slot += 1


def cut_kernel(pixels, chunks, own, far, tile, *outs):
    planes, rows, _ = tile.shape
    even = is_even(own, rows)
    for (first, size), near, cross in zip(chunks, outs[::2], outs[1::2], strict=True):
        for at in range(size):
            slot = first + at
            strip = at * planes
            near[strip : strip + planes] = cut(tile, jnp.where(even, own[slot, 1], far[slot, 1]), pixels)
            cross[strip : strip + planes] = cut(tile, jnp.where(even, far[slot, 1], own[slot, 1]), pixels)


def add_kernel(pixels, groups, own, middle, far, *refs):
    *parts, out = refs
    planes, rows, _ = out.shape
    even = is_even(own, rows)
    out[...] = jnp.zeros_like(out)
    lane = lax.broadcasted_iota(jnp.int32, (1, 1, pixels), 2)
    for (kind, first, size, unit), strips in zip(groups, parts):

        turned = []
        for at in range(size):
            slot = first + at
            if kind == "mid":
                column = middle[slot, 1]
            elif kind == "near":
                column = jnp.where(even, own[slot, 1], far[slot, 1])
            else:
                column = jnp.where(even, far[slot, 1], own[slot, 1])
            base, shift = place(column, out.shape[-1], pixels)
            part = strips[unit + at * planes : unit + (at + 1) * planes].reshape(-1, pixels)
            part = pltpu.roll(part, lax.rem(shift, pixels), 1).reshape(planes, rows, pixels)
            turned.append((base, shift, part))
        for base, shift, part in turned:
            out[:, :, pl.ds(base, pixels)] += jnp.where(lane >= shift, part, 0.0)
            beside = pl.ds(pl.multiple_of(base + pixels, pixels), pixels)
            out[:, :, beside] += jnp.where(lane < shift, part, 0.0)


def slot_kernel(first, size, ahead, own_offsets, *refs):
    offsets, mid, near, cross, target, probe, prop, tables, *refs = refs
    so_far, refs = (refs[0], refs[1:]) if first else (None, refs)
    given, refs = refs[:ahead], refs[ahead:]
    out_near, out_mid, out_cross, *shares = refs[:-5]
    window, patch, grads, exit_wave, far = refs[-5:]
    total = shares.pop()
    modes, _, pixels, _ = probe.shape
    planes, rows = mid.shape[0] // size, mid.shape[1]
    behind = given[0].shape[0] if given else 0
    for message, out in zip(given, (out_near, out_cross)):
        out[:behind] = message[...]
    even = is_even(own_offsets, rows)
    total[...] = so_far[...] if first else jnp.zeros_like(total)
    held = range(BATCH)

    def is_live(at):
        return jnp.max(target[first + at, :8]) > 0.0

    def leave(slots):
        for at in slots:
            for out, unit in ((out_near, behind), (out_mid, 0), (out_cross, behind)):
                out[pl.ds(unit + at * planes, planes)] = jnp.zeros((planes, rows, pixels), F32)

    def visit(slots):
        starts = [lax.rem(offsets[first + at, 0], rows) for at in slots]
        live = [jnp.where(is_live(at), 1.0, 0.0).astype(F32) for at in slots]
        for s, at in enumerate(slots):
            strip = pl.ds(at * planes, planes)
            window[:, :rows] = jnp.where(even, cross[strip], near[strip])
            window[:, rows : 2 * rows] = mid[strip]
            window[:, 2 * rows :] = jnp.where(even, near[strip], cross[strip])
            patch[s] = window[:, pl.ds(starts[s], pixels), :]
            total[2 * modes] += live[s] * (patch[s, 0] * patch[s, 0] + patch[s, 1] * patch[s, 1])
        all_modes = range(modes)
        groups = [
            [times((probe[m, 0], probe[m, 1]), (patch[s, 0], patch[s, 1])) for m in all_modes] for s in held
        ]
        groups = transform(tables, False, groups)
        groups = [[times((prop[0], prop[1]), wave) for wave in waves] for waves in groups]
        groups = transform(tables, True, groups)
        for s in held:
            for m in all_modes:
                exit_wave[s, m, 0], exit_wave[s, m, 1] = groups[s][m]
            groups[s] = [times(wave, (patch[s, 2], patch[s, 3])) for wave in groups[s]]
        groups = transform(tables, False, groups)
        for s, at in enumerate(slots):
            intensity = jnp.zeros((pixels, pixels), F32)
            for m in all_modes:
                wave = groups[s][m]
                far[s, m, 0], far[s, m, 1] = wave
                intensity = intensity + wave[0] * wave[0] + wave[1] * wave[1]
            misfit = 2.0 * live[s] * (intensity - target[first + at])
            groups[s] = [(misfit * far[s, m, 0], misfit * far[s, m, 1]) for m in all_modes]
        groups = transform(tables, True, groups)
        for s in held:
            grad_re, grad_im = jnp.zeros((pixels, pixels), F32), jnp.zeros((pixels, pixels), F32)
            for m in all_modes:
                re, im = conj_times((exit_wave[s, m, 0], exit_wave[s, m, 1]), groups[s][m])
                grad_re, grad_im = grad_re + re, grad_im + im
            grads[s, 2], grads[s, 3] = grad_re, grad_im
            groups[s] = [conj_times((patch[s, 2], patch[s, 3]), wave) for wave in groups[s]]
        groups = transform(tables, False, groups)
        groups = [[conj_times((prop[0], prop[1]), wave) for wave in waves] for waves in groups]
        groups = transform(tables, True, groups)
        for s in held:
            grad_re, grad_im = jnp.zeros((pixels, pixels), F32), jnp.zeros((pixels, pixels), F32)
            for m in all_modes:
                re, im = conj_times((patch[s, 0], patch[s, 1]), groups[s][m])
                total[2 * m] += re
                total[2 * m + 1] += im
                re, im = conj_times((probe[m, 0], probe[m, 1]), groups[s][m])
                grad_re, grad_im = grad_re + re, grad_im + im
            grads[s, 0], grads[s, 1] = grad_re, grad_im
        for s, at in enumerate(slots):
            window[...] = jnp.zeros_like(window)
            window[:, pl.ds(starts[s], pixels), :] = grads[s]
            strip = pl.ds(behind + at * planes, planes)
            out_near[strip] = jnp.where(even, window[:, 2 * rows :], window[:, :rows])
            out_mid[pl.ds(at * planes, planes)] = window[:, rows : 2 * rows]
            out_cross[strip] = jnp.where(even, window[:, :rows], window[:, 2 * rows :])

    def step(index, carry):
        slots = [index * BATCH + s for s in range(BATCH)]
        some = is_live(slots[0])
        pl.when(some)(lambda: visit(slots))
        pl.when(jnp.logical_not(some))(lambda: leave(slots))
        return carry

    lax.fori_loop(0, size // BATCH, step, 0)

    if shares:
        own, other = shares
        chips, _, share, _ = own.shape
        core = jnp.where(even, 0, 1)
        for chip in range(chips):
            for plane in range(2 * modes + 1):
                own[chip, plane] = total[plane, rows_of(2 * chip + core, share)]
                other[chip, plane] = total[plane, rows_of(2 * chip + 1 - core, share)]


def step_kernel(parts, out):
    summed = parts[0]
    for at in range(1, parts.shape[0]):
        summed = summed + parts[at]
    step = summed[:-1] / (summed[-1:] + 1.0)
    for at in range(out.shape[0]):
        out[at] = step


def order_kernel(rows, offsets, own, other, out):
    chips, _, share, _ = own.shape
    core = jnp.where(is_even(offsets, rows), 0, 1)
    for chip in range(chips):
        out[:, rows_of(2 * chip + core, share)] = own[chip]
        out[:, rows_of(2 * chip + 1 - core, share)] = other[chip]


def in_smem():
    return pl.BlockSpec(memory_space=pltpu.SMEM)


def in_vmem():
    return pl.BlockSpec(memory_space=pltpu.VMEM)


def local(object_slices, probe_modes, propagator_phase, measured, offsets, counts):
    slices, _, tile_rows, columns = object_slices.shape
    modes, _, pixels, _ = probe_modes.shape
    planes = 2 * slices
    peers = lax.axis_size(ROW)
    params = pltpu.CompilerParams(vmem_limit_bytes=SMALL_LIMIT)
    tile = object_slices.reshape(planes, tile_rows, columns)
    starts = [sum(CHUNKS[:i]) for i in range(len(CHUNKS))]

    pair = [(i, i ^ 1) for i in range(peers)]
    other_pair = [(i, (i - 1) % peers if i % 2 == 0 else (i + 1) % peers) for i in range(peers)]
    far = shifted(offsets, ROW, 2)

    chunks = list(zip(starts, CHUNKS))
    target = pl.pallas_call(
        pack_kernel,
        out_shape=jax.ShapeDtypeStruct((measured.shape[0] + 1, pixels, pixels), F32),
        in_specs=[in_smem()] * 2 + [in_vmem()],
        out_specs=in_vmem(),
        compiler_params=params,
        cost_estimate=pl.CostEstimate(flops=0, bytes_accessed=1 << 20, transcendentals=0),
    )(offsets, counts, measured)
    far, target = lax.optimization_barrier((far, target))
    target = shifted(target, ROW, 1)

    def units(count):
        return jax.ShapeDtypeStruct((count, tile_rows, pixels), F32)

    def strips(chunks, far):
        shapes = [units(size * planes) for _, size in chunks for _ in range(2)]
        outs = pl.pallas_call(
            functools.partial(cut_kernel, pixels, chunks),
            out_shape=shapes,
            in_specs=[in_smem()] * 2 + [in_vmem()],
            out_specs=[in_vmem()] * len(shapes),
            compiler_params=params,
            cost_estimate=pl.CostEstimate(flops=0, bytes_accessed=4 << 20, transcendentals=0),
        )(offsets, far, tile)
        return list(zip(outs[::2], outs[1::2]))

    def swapped(to_near, to_cross):
        return lax.ppermute(to_near, ROW, pair), lax.ppermute(to_cross, ROW, other_pair)

    far_later, target = lax.optimization_barrier((far, target))
    waiting = strips(chunks[:1], far) + strips(chunks[1:], far_later)
    *middles, middle = pl.pallas_call(
        functools.partial(middle_kernel, pixels),
        out_shape=[units(size * planes) for size in CHUNKS] + [jax.ShapeDtypeStruct(offsets.shape, jnp.int32)],
        in_specs=[in_vmem()] * 2,
        out_specs=[in_vmem()] * len(CHUNKS) + [in_smem()],
        compiler_params=params,
        cost_estimate=pl.CostEstimate(flops=0, bytes_accessed=4 << 20, transcendentals=0),
    )(target, tile)
    arrived = [swapped(*waiting[0])]
    if len(waiting) > 1:
        arrived[0], following, middles = lax.optimization_barrier((arrived[0], waiting[1], middles))
        arrived.append(swapped(*following))
    phase = jnp.concatenate([propagator_phase[0::2], propagator_phase[1::2]], axis=0)
    prop = jnp.stack([jnp.cos(phase), jnp.sin(phase)])
    tables = jnp.asarray(fourier_tables(pixels))

    share = pixels // peers
    total = ()
    mid, back, mid_groups, back_groups = [], [], [], []
    for index, (first, size) in enumerate(chunks):
        given = waiting[index + 2] if index + 2 < len(chunks) else ()
        ahead = CHUNKS[index + 2] * planes if given else 0
        sums = jax.ShapeDtypeStruct((2 * modes + 1, pixels, pixels), F32)
        part = jax.ShapeDtypeStruct((peers // 2, 2 * modes + 1, share, pixels), F32)
        shares = [part, part] if index == len(CHUNKS) - 1 else []
        message = units(ahead + size * planes)
        field = pltpu.VMEM((BATCH, planes, pixels, pixels), F32)
        kept = pltpu.VMEM((BATCH, modes, 2, pixels, pixels), F32)
        to_near, to_mid, to_cross, *total = pl.pallas_call(
            functools.partial(slot_kernel, first, size, len(given)),
            out_shape=[message, units(size * planes), message] + (shares or [sums]),
            in_specs=[in_smem()] * 2 + [in_vmem()] * (7 + len(total) + len(given)),
            out_specs=[in_vmem()] * (3 + (len(shares) or 1)),
            scratch_shapes=([pltpu.VMEM(sums.shape, F32)] if shares else [])
            + [pltpu.VMEM((planes, 3 * tile_rows, pixels), F32), field, field, kept, kept],
            compiler_params=pltpu.CompilerParams(vmem_limit_bytes=VMEM_LIMIT),
            cost_estimate=pl.CostEstimate(
                flops=size * 6 * modes * 3 * 16 * pixels**3, bytes_accessed=8 << 20, transcendentals=0
            ),
        )(offsets, middle, middles[index], *arrived[index], target, probe_modes, prop, tables, *total, *given)
        mid_groups.append(("mid", first, size, 0))
        mid.append(to_mid)
        message = swapped(to_near, to_cross)
        if given:
            arrived.append(message)
        back_groups += [(kind, first, size, ahead) for kind in ("near", "cross")]
        back.append(message)

    def added(groups, strips):
        return pl.pallas_call(
            functools.partial(add_kernel, pixels, groups),
            out_shape=jax.ShapeDtypeStruct(tile.shape, F32),
            in_specs=[in_smem()] * 3 + [in_vmem()] * len(strips),
            out_specs=in_vmem(),
            compiler_params=params,
            cost_estimate=pl.CostEstimate(flops=0, bytes_accessed=5 << 20, transcendentals=0),
        )(offsets, middle, far, *strips)

    own, other = total
    own, other, back[:-1] = lax.optimization_barrier((own, other, back[:-1]))
    both = own + lax.ppermute(other, ROW, pair)
    parts = lax.all_to_all(both, "chip", 0, 0)
    spread = pl.pallas_call(
        step_kernel,
        out_shape=jax.ShapeDtypeStruct((peers // 2, 2 * modes, share, pixels), F32),
        in_specs=[in_vmem()],
        out_specs=in_vmem(),
        compiler_params=params,
    )(parts)
    groups = mid_groups + back_groups
    strips = mid + [part for message in back for part in message]
    spread, strips = lax.optimization_barrier((spread, strips))
    gathered = lax.all_to_all(spread, "chip", 0, 0)
    object_grad = added(groups, strips)
    gathered, object_grad = lax.optimization_barrier((gathered, object_grad))
    object_grad = object_grad.reshape(object_slices.shape)

    probe_step = pl.pallas_call(
        functools.partial(order_kernel, tile_rows),
        out_shape=jax.ShapeDtypeStruct((2 * modes, pixels, pixels), F32),
        in_specs=[in_smem()] + [in_vmem()] * 2,
        out_specs=in_vmem(),
        compiler_params=params,
    )(offsets, gathered, lax.ppermute(gathered, ROW, pair)).reshape(probe_modes.shape)
    return (object_grad, probe_step)


def solution(mesh):
    groups, peers = mesh.shape["grp"], mesh.shape["row"]
    split = jax.sharding.Mesh(mesh.devices.reshape(groups, peers // 2, 2), ("grp",) + ROW)
    everywhere = ("grp",) + ROW
    in_specs = (
        P(None, None, everywhere, None),
        P("grp", None, None, None),
        P(),
        P(everywhere, None, None),
        P(everywhere, None),
        P(everywhere),
    )
    out_specs = (P(None, None, everywhere, None), P("grp", None, None, None))
    return jax.shard_map(local, mesh=split, in_specs=in_specs, out_specs=out_specs, check_vma=False)
```

```python
import functools

import jax
import jax.numpy as jnp
import numpy as np
from jax import lax
from jax.experimental import pallas as pl
from jax.experimental.pallas import tpu as pltpu
from jax.sharding import PartitionSpec as P

CHUNKS = (4, 4)
BATCH = 4
VMEM_LIMIT = 40 * 1024 * 1024
ROW = ("chip", "core")
F32 = jnp.float32
BF16 = jnp.bfloat16


def shifted(array, axis, by):
    peers = lax.axis_size(axis)
    return lax.ppermute(array, axis, [(i, (i + by) % peers) for i in range(peers)])


def real_form(matrix):
    return np.block([[matrix.real, -matrix.imag], [matrix.imag, matrix.real]]).astype(np.float32)


def two_pieces(matrix):
    high = matrix.astype(BF16)
    return high, (matrix - high.astype(np.float32)).astype(BF16)


def fourier_tables(pixels):
    half = pixels // 2
    kept, rows = np.arange(half)[:, None], np.arange(half)[None, :]
    lefts = []
    for odd in range(2):
        turns = (2 * kept + odd) * rows % pixels / pixels
        part = real_form(np.exp(-2j * np.pi * turns) / np.sqrt(pixels))
        for table in (part, part.T):
            high, low = two_pieces(table)
            lefts.append(np.block([[high, high], [low, np.zeros_like(low)]]))
    indices = np.arange(pixels)
    whole = np.exp(-2j * np.pi * (indices[:, None] * indices[None, :] % pixels) / pixels) / np.sqrt(pixels)
    rights = []
    for table in (real_form(whole).T, real_form(whole)):
        rights += two_pieces(table)
    return np.stack(lefts + rights)


def pieces(array):
    high = array.astype(BF16)
    return high, (array - high.astype(F32)).astype(BF16)


def from_left(tables, conj, waves):
    half = waves[0][0].shape[0] // 2
    pixels = 2 * half
    sides = []
    for odd in range(2):
        parts = []
        for wave in waves:
            if conj:
                parts.append(jnp.concatenate([part[odd * half : (odd + 1) * half] for part in wave], axis=0))
            elif odd:
                parts.append(jnp.concatenate([part[:half] - part[half:] for part in wave], axis=0))
            else:
                parts.append(jnp.concatenate([part[:half] + part[half:] for part in wave], axis=0))
        stacked = jnp.concatenate(pieces(jnp.concatenate(parts, axis=1)), axis=0)
        product = jnp.dot(tables[2 * odd + conj], stacked, preferred_element_type=F32)
        sides.append(product[:pixels] + product[pixels:])
    if conj:
        sides = [sides[0] + sides[1], sides[0] - sides[1]]
    turned = []
    for at in range(0, len(waves) * pixels, pixels):
        re = jnp.concatenate([side[:half, at : at + pixels] for side in sides], axis=0)
        im = jnp.concatenate([side[half:, at : at + pixels] for side in sides], axis=0)
        turned.append(jnp.concatenate([re, im], axis=1))
    return jnp.concatenate(turned, axis=0)


def transform(tables, conj, groups):
    right_high, right_low = tables[4 + 2 * conj], tables[5 + 2 * conj]
    right = jnp.concatenate([right_high, right_high, right_low], axis=0)
    halves = [pieces(from_left(tables, conj, waves)) for waves in groups]
    pixels = right.shape[1] // 2
    wholes = []
    for high, low in halves:
        whole = jnp.dot(jnp.concatenate([high, low, high], axis=1), right, preferred_element_type=F32)
        wholes.append(
            [
                (whole[at : at + pixels, :pixels], whole[at : at + pixels, pixels:])
                for at in range(0, whole.shape[0], pixels)
            ]
        )
    return wholes


def times(one, two):
    return one[0] * two[0] - one[1] * two[1], one[0] * two[1] + one[1] * two[0]


def conj_times(one, two):
    return one[0] * two[0] + one[1] * two[1], one[0] * two[1] - one[1] * two[0]


def place(column, columns, pixels):
    base = jnp.minimum(column // pixels * pixels, columns - 2 * pixels)
    return pl.multiple_of(base, pixels), column - base


def cut(tile, column, pixels):
    base, shift = place(column, tile.shape[-1], pixels)
    rows = tile.shape[1]
    wide = tile[:, :, pl.ds(base, 2 * pixels)].reshape(-1, 2 * pixels)
    turned = pltpu.roll(wide, 2 * pixels - shift, 1)
    return turned[:, :pixels].reshape(-1, rows, pixels)


def rows_of(index, share):
    return pl.ds(pl.multiple_of(index * share, share), share)


def is_even(offsets, rows):
    return lax.rem(offsets[0, 0] // rows, 2) == 0


def pack_kernel(offsets, counts, measured, out):
    slots, _, pixels = measured.shape
    half = pixels // 2
    for slot in range(slots):
        live = jnp.where(slot < counts[0], 1.0, 0.0).astype(F32)
        for odd in range(2):
            row = slot * pixels + odd * half
            out[row : row + half] = measured[slot, pl.ds(odd, half, stride=2)] * live
        for entry in range(2):
            line = jnp.full((1, pixels), offsets[slot, entry], jnp.int32).astype(F32)
            row = slots * pixels + 2 * slot + entry
            out[row : row + 1] = line


def middle_kernel(pixels, target, tile, *outs):
    *parts, offsets = outs
    planes = tile.shape[0]
    for slot in range(offsets.shape[0]):
        for entry in range(2):
            line = target.shape[0] - 2 * offsets.shape[0] + 2 * slot + entry
            value = target[line : line + 1]
            offsets[slot, entry] = jnp.max(value).astype(jnp.int32)
    slot = 0
    for part in parts:
        for at in range(part.shape[0] // planes):
            part[at * planes : (at + 1) * planes] = cut(tile, offsets[slot, 1], pixels)
            slot += 1


def cut_kernel(pixels, chunks, own, far, tile, *outs):
    planes, rows, _ = tile.shape
    even = is_even(own, rows)
    for (first, size), near, cross in zip(chunks, outs[::2], outs[1::2], strict=True):
        for at in range(size):
            slot = first + at
            strip = at * planes
            near[strip : strip + planes] = cut(tile, jnp.where(even, own[slot, 1], far[slot, 1]), pixels)
            cross[strip : strip + planes] = cut(tile, jnp.where(even, far[slot, 1], own[slot, 1]), pixels)


def add_kernel(pixels, groups, own, middle, far, *refs):
    *parts, out = refs
    planes, rows, _ = out.shape
    even = is_even(own, rows)
    out[...] = jnp.zeros_like(out)
    lane = lax.broadcasted_iota(jnp.int32, (1, 1, pixels), 2)
    for (kind, first, size, unit), strips in zip(groups, parts):

        turned = []
        for at in range(size):
            slot = first + at
            if kind == "mid":
                column = middle[slot, 1]
            elif kind == "near":
                column = jnp.where(even, own[slot, 1], far[slot, 1])
            else:
                column = jnp.where(even, far[slot, 1], own[slot, 1])
            base, shift = place(column, out.shape[-1], pixels)
            part = strips[unit + at * planes : unit + (at + 1) * planes].reshape(-1, pixels)
            part = pltpu.roll(part, lax.rem(shift, pixels), 1).reshape(planes, rows, pixels)
            turned.append((base, shift, part))
        for base, shift, part in turned:
            out[:, :, pl.ds(base, pixels)] += jnp.where(lane >= shift, part, 0.0)
            beside = pl.ds(pl.multiple_of(base + pixels, pixels), pixels)
            out[:, :, beside] += jnp.where(lane < shift, part, 0.0)


def slot_kernel(first, size, earlier, own_offsets, *refs):
    offsets, mid, near, cross, target, probe, prop, tables, *refs = refs
    so_far, refs = (refs[0], refs[1:]) if first else (None, refs)
    earlier, refs = refs[:earlier], refs[earlier:]
    out_near, out_mid, out_cross, *shares = refs[:-5]
    window, patch, grads, exit_wave, far = refs[-5:]
    total = shares.pop()
    modes, _, pixels, _ = probe.shape
    planes, rows = mid.shape[0] // size, mid.shape[1]
    behind = 0
    for strips in earlier:
        out_near[behind : behind + strips.shape[0]] = strips[...]
        behind += strips.shape[0]
    even = is_even(own_offsets, rows)
    total[...] = so_far[...] if first else jnp.zeros_like(total)
    held = range(BATCH)

    def is_live(at):
        return jnp.max(target[pl.ds((first + at) * pixels, 8)]) > 0.0

    def leave(slots):
        for at in slots:
            for out, unit in ((out_near, behind), (out_mid, 0), (out_cross, 0)):
                out[pl.ds(unit + at * planes, planes)] = jnp.zeros((planes, rows, pixels), F32)

    def visit(slots):
        starts = [lax.rem(offsets[first + at, 0], rows) for at in slots]
        live = [jnp.where(is_live(at), 1.0, 0.0).astype(F32) for at in slots]
        for s, at in enumerate(slots):
            strip = pl.ds(at * planes, planes)
            window[:, :rows] = jnp.where(even, cross[strip], near[strip])
            window[:, rows : 2 * rows] = mid[strip]
            window[:, 2 * rows :] = jnp.where(even, near[strip], cross[strip])
            patch[s] = window[:, pl.ds(starts[s], pixels), :]
            total[2 * modes] += live[s] * (patch[s, 0] * patch[s, 0] + patch[s, 1] * patch[s, 1])
        all_modes = range(modes)
        groups = [
            [times((probe[m, 0], probe[m, 1]), (patch[s, 0], patch[s, 1])) for m in all_modes] for s in held
        ]
        groups = transform(tables, False, groups)
        groups = [[times((prop[0], prop[1]), wave) for wave in waves] for waves in groups]
        groups = transform(tables, True, groups)
        for s in held:
            for m in all_modes:
                exit_wave[s, m, 0], exit_wave[s, m, 1] = groups[s][m]
            groups[s] = [times(wave, (patch[s, 2], patch[s, 3])) for wave in groups[s]]
        groups = transform(tables, False, groups)
        for s, at in enumerate(slots):
            intensity = jnp.zeros((pixels, pixels), F32)
            for m in all_modes:
                wave = groups[s][m]
                far[s, m, 0], far[s, m, 1] = wave
                intensity = intensity + wave[0] * wave[0] + wave[1] * wave[1]
            misfit = 2.0 * live[s] * (intensity - target[pl.ds((first + at) * pixels, pixels)])
            groups[s] = [(misfit * far[s, m, 0], misfit * far[s, m, 1]) for m in all_modes]
        groups = transform(tables, True, groups)
        for s in held:
            grad_re, grad_im = jnp.zeros((pixels, pixels), F32), jnp.zeros((pixels, pixels), F32)
            for m in all_modes:
                re, im = conj_times((exit_wave[s, m, 0], exit_wave[s, m, 1]), groups[s][m])
                grad_re, grad_im = grad_re + re, grad_im + im
            grads[s, 2], grads[s, 3] = grad_re, grad_im
            groups[s] = [conj_times((patch[s, 2], patch[s, 3]), wave) for wave in groups[s]]
        groups = transform(tables, False, groups)
        groups = [[conj_times((prop[0], prop[1]), wave) for wave in waves] for waves in groups]
        groups = transform(tables, True, groups)
        for s in held:
            grad_re, grad_im = jnp.zeros((pixels, pixels), F32), jnp.zeros((pixels, pixels), F32)
            for m in all_modes:
                re, im = conj_times((patch[s, 0], patch[s, 1]), groups[s][m])
                total[2 * m] += re
                total[2 * m + 1] += im
                re, im = conj_times((probe[m, 0], probe[m, 1]), groups[s][m])
                grad_re, grad_im = grad_re + re, grad_im + im
            grads[s, 0], grads[s, 1] = grad_re, grad_im
        for s, at in enumerate(slots):
            window[...] = jnp.zeros_like(window)
            window[:, pl.ds(starts[s], pixels), :] = grads[s]
            strip = pl.ds(at * planes, planes)
            out_near[pl.ds(behind + at * planes, planes)] = jnp.where(even, window[:, 2 * rows :], window[:, :rows])
            out_mid[pl.ds(at * planes, planes)] = window[:, rows : 2 * rows]
            out_cross[strip] = jnp.where(even, window[:, :rows], window[:, 2 * rows :])

    def step(index, carry):
        slots = [index * BATCH + s for s in range(BATCH)]
        some = is_live(slots[0])
        pl.when(some)(lambda: visit(slots))
        pl.when(jnp.logical_not(some))(lambda: leave(slots))
        return carry

    lax.fori_loop(0, size // BATCH, step, 0)

    if shares:
        own, other = shares
        chips, _, share, _ = own.shape
        core = jnp.where(even, 0, 1)
        for chip in range(chips):
            for plane in range(2 * modes + 1):
                own[chip, plane] = total[plane, rows_of(2 * chip + core, share)]
                other[chip, plane] = total[plane, rows_of(2 * chip + 1 - core, share)]


def step_kernel(parts, out):
    summed = parts[0]
    for at in range(1, parts.shape[0]):
        summed = summed + parts[at]
    step = summed[:-1] / (summed[-1:] + 1.0)
    for at in range(out.shape[0]):
        out[at] = step


def order_kernel(rows, offsets, own, other, out):
    chips, _, share, _ = own.shape
    core = jnp.where(is_even(offsets, rows), 0, 1)
    for chip in range(chips):
        out[:, rows_of(2 * chip + core, share)] = own[chip]
        out[:, rows_of(2 * chip + 1 - core, share)] = other[chip]


def in_smem():
    return pl.BlockSpec(memory_space=pltpu.SMEM)


def in_vmem():
    return pl.BlockSpec(memory_space=pltpu.VMEM)


def local(object_slices, probe_modes, propagator_phase, measured, offsets, counts):
    slices, _, tile_rows, columns = object_slices.shape
    modes, _, pixels, _ = probe_modes.shape
    planes = 2 * slices
    peers = lax.axis_size(ROW)
    params = pltpu.CompilerParams(vmem_limit_bytes=VMEM_LIMIT)
    tile = object_slices.reshape(planes, tile_rows, columns)
    starts = [sum(CHUNKS[:i]) for i in range(len(CHUNKS))]

    pair = [(i, i ^ 1) for i in range(peers)]
    other_pair = [(i, (i - 1) % peers if i % 2 == 0 else (i + 1) % peers) for i in range(peers)]
    far = shifted(offsets, ROW, 2)

    chunks = list(zip(starts, CHUNKS))
    target = pl.pallas_call(
        pack_kernel,
        out_shape=jax.ShapeDtypeStruct((measured.shape[0] * pixels + offsets.size, pixels), F32),
        in_specs=[in_smem()] * 2 + [in_vmem()],
        out_specs=in_vmem(),
        compiler_params=params,
        cost_estimate=pl.CostEstimate(flops=0, bytes_accessed=1 << 20, transcendentals=0),
    )(offsets, counts, measured)
    far, target = lax.optimization_barrier((far, target))
    target = shifted(target, ROW, 1)

    def units(count):
        return jax.ShapeDtypeStruct((count, tile_rows, pixels), F32)

    def strips(chunks, far):
        shapes = [units(size * planes) for _, size in chunks for _ in range(2)]
        outs = pl.pallas_call(
            functools.partial(cut_kernel, pixels, chunks),
            out_shape=shapes,
            in_specs=[in_smem()] * 2 + [in_vmem()],
            out_specs=[in_vmem()] * len(shapes),
            compiler_params=params,
            cost_estimate=pl.CostEstimate(flops=0, bytes_accessed=4 << 20, transcendentals=0),
        )(offsets, far, tile)
        return list(zip(outs[::2], outs[1::2]))

    def swapped(to_near, to_cross):
        return lax.ppermute(to_near, ROW, pair), lax.ppermute(to_cross, ROW, other_pair)

    far_later, target = lax.optimization_barrier((far, target))
    waiting = strips(chunks[:1], far) + strips(chunks[1:], far_later)
    *middles, middle = pl.pallas_call(
        functools.partial(middle_kernel, pixels),
        out_shape=[units(size * planes) for size in CHUNKS] + [jax.ShapeDtypeStruct(offsets.shape, jnp.int32)],
        in_specs=[in_vmem()] * 2,
        out_specs=[in_vmem()] * len(CHUNKS) + [in_smem()],
        compiler_params=params,
        cost_estimate=pl.CostEstimate(flops=0, bytes_accessed=4 << 20, transcendentals=0),
    )(target, tile)
    arrived = [swapped(*waiting[0])]
    if len(waiting) > 1:
        arrived[0], following, middles = lax.optimization_barrier((arrived[0], waiting[1], middles))
        arrived.append(swapped(*following))
    phase = jnp.concatenate([propagator_phase[0::2], propagator_phase[1::2]], axis=0)
    prop = jnp.stack([jnp.cos(phase), jnp.sin(phase)])
    tables = jnp.asarray(fourier_tables(pixels))

    share = pixels // peers
    total = ()
    mid, back, groups, to_pair = [], [], [], []
    for index, (first, size) in enumerate(chunks):
        sums = jax.ShapeDtypeStruct((2 * modes + 1, pixels, pixels), F32)
        part = jax.ShapeDtypeStruct((peers // 2, 2 * modes + 1, share, pixels), F32)
        last = index == len(chunks) - 1
        message = units(size * planes)
        field = pltpu.VMEM((BATCH, planes, pixels, pixels), F32)
        kept = pltpu.VMEM((BATCH, modes, 2, pixels, pixels), F32)
        results = [part, part] if last else [sums]
        earlier = to_pair if last else []
        near_units = units(sum(CHUNKS) * planes) if last else message
        to_near, to_mid, to_cross, *total = pl.pallas_call(
            functools.partial(slot_kernel, first, size, len(earlier)),
            out_shape=[near_units, message, message] + results,
            in_specs=[in_smem()] * 2 + [in_vmem()] * (7 + len(total) + len(earlier)),
            out_specs=[in_vmem()] * (3 + len(results)),
            scratch_shapes=([pltpu.VMEM(sums.shape, F32)] if last else [])
            + [pltpu.VMEM((planes, 3 * tile_rows, pixels), F32), field, field, kept, kept],
            compiler_params=params,
            cost_estimate=pl.CostEstimate(
                flops=size * 6 * modes * 3 * 16 * pixels**3, bytes_accessed=8 << 20, transcendentals=0
            ),
        )(offsets, middle, middles[index], *arrived[index], target, probe_modes, prop, tables, *total, *earlier)
        to_pair.append(to_near)
        mid.append(to_mid)
        back.append(lax.ppermute(to_cross, ROW, other_pair))
        groups += [("mid", first, size, 0), ("cross", first, size, 0), ("near", first, size, first * planes)]

    def added(groups, strips):
        return pl.pallas_call(
            functools.partial(add_kernel, pixels, groups),
            out_shape=jax.ShapeDtypeStruct(tile.shape, F32),
            in_specs=[in_smem()] * 3 + [in_vmem()] * len(strips),
            out_specs=in_vmem(),
            compiler_params=params,
            cost_estimate=pl.CostEstimate(flops=0, bytes_accessed=5 << 20, transcendentals=0),
        )(offsets, middle, far, *strips)

    own, other = total
    own, other, back[:-1] = lax.optimization_barrier((own, other, back[:-1]))
    other, to_pair = lax.optimization_barrier((lax.ppermute(other, ROW, pair), to_pair[-1]))
    from_pair = lax.ppermute(to_pair, ROW, pair)
    both = own + other
    parts = lax.all_to_all(both, "chip", 0, 0)
    spread = pl.pallas_call(
        step_kernel,
        out_shape=jax.ShapeDtypeStruct((peers // 2, 2 * modes, share, pixels), F32),
        in_specs=[in_vmem()],
        out_specs=in_vmem(),
        compiler_params=params,
    )(parts)
    strips = [part for parts in zip(mid, back, [from_pair] * len(mid)) for part in parts]
    spread, strips = lax.optimization_barrier((spread, strips))
    gathered = lax.all_to_all(spread, "chip", 0, 0)
    object_grad = added(groups, strips)
    gathered, object_grad = lax.optimization_barrier((gathered, object_grad))
    object_grad = object_grad.reshape(object_slices.shape)

    probe_step = pl.pallas_call(
        functools.partial(order_kernel, tile_rows),
        out_shape=jax.ShapeDtypeStruct((2 * modes, pixels, pixels), F32),
        in_specs=[in_smem()] + [in_vmem()] * 2,
        out_specs=in_vmem(),
        compiler_params=params,
    )(offsets, gathered, lax.ppermute(gathered, ROW, pair)).reshape(probe_modes.shape)
    return (object_grad, probe_step)


def solution(mesh):
    groups, peers = mesh.shape["grp"], mesh.shape["row"]
    split = jax.sharding.Mesh(mesh.devices.reshape(groups, peers // 2, 2), ("grp",) + ROW)
    everywhere = ("grp",) + ROW
    in_specs = (
        P(None, None, everywhere, None),
        P("grp", None, None, None),
        P(),
        P(everywhere, None, None),
        P(everywhere, None),
        P(everywhere),
    )
    out_specs = (P(None, None, everywhere, None), P("grp", None, None, None))
    return jax.shard_map(local, mesh=split, in_specs=in_specs, out_specs=out_specs, check_vma=False)
```

```python
import functools

import jax
import jax.numpy as jnp
import numpy as np
from jax import lax
from jax.experimental import pallas as pl
from jax.experimental.pallas import tpu as pltpu
from jax.sharding import PartitionSpec as P

CHUNKS = (4, 4)
BATCH = 4
VMEM_LIMIT = 32 * 1024 * 1024
ROW = ("chip", "core")
F32 = jnp.float32
BF16 = jnp.bfloat16


def shifted(array, axis, by):
    peers = lax.axis_size(axis)
    return lax.ppermute(array, axis, [(i, (i + by) % peers) for i in range(peers)])


def real_form(matrix):
    return np.block([[matrix.real, -matrix.imag], [matrix.imag, matrix.real]]).astype(np.float32)


def two_pieces(matrix):
    high = matrix.astype(BF16)
    return high, (matrix - high.astype(np.float32)).astype(BF16)


def fourier_tables(pixels):
    half = pixels // 2
    kept, rows = np.arange(half)[:, None], np.arange(half)[None, :]
    lefts = []
    for odd in range(2):
        turns = (2 * kept + odd) * rows % pixels / pixels
        part = real_form(np.exp(-2j * np.pi * turns) / np.sqrt(pixels))
        for table in (part, part.T):
            high, low = two_pieces(table)
            lefts.append(np.block([[high, high], [low, np.zeros_like(low)]]))
    indices = np.arange(pixels)
    whole = np.exp(-2j * np.pi * (indices[:, None] * indices[None, :] % pixels) / pixels) / np.sqrt(pixels)
    rights = []
    for table in (real_form(whole).T, real_form(whole)):
        rights += two_pieces(table)
    return np.stack(lefts + rights)


def pieces(array):
    high = array.astype(BF16)
    return high, (array - high.astype(F32)).astype(BF16)


def from_left(tables, conj, waves):
    half = waves[0][0].shape[0] // 2
    pixels = 2 * half
    sides = []
    for odd in range(2):
        parts = []
        for wave in waves:
            if conj:
                parts.append(jnp.concatenate([part[odd * half : (odd + 1) * half] for part in wave], axis=0))
            elif odd:
                parts.append(jnp.concatenate([part[:half] - part[half:] for part in wave], axis=0))
            else:
                parts.append(jnp.concatenate([part[:half] + part[half:] for part in wave], axis=0))
        stacked = jnp.concatenate(pieces(jnp.concatenate(parts, axis=1)), axis=0)
        product = jnp.dot(tables[2 * odd + conj], stacked, preferred_element_type=F32)
        sides.append(product[:pixels] + product[pixels:])
    if conj:
        sides = [sides[0] + sides[1], sides[0] - sides[1]]
    turned = []
    for at in range(0, len(waves) * pixels, pixels):
        re = jnp.concatenate([side[:half, at : at + pixels] for side in sides], axis=0)
        im = jnp.concatenate([side[half:, at : at + pixels] for side in sides], axis=0)
        turned.append(jnp.concatenate([re, im], axis=1))
    return jnp.concatenate(turned, axis=0)


def transform(tables, conj, groups):
    right_high, right_low = tables[4 + 2 * conj], tables[5 + 2 * conj]
    right = jnp.concatenate([right_high, right_high, right_low], axis=0)
    halves = [pieces(from_left(tables, conj, waves)) for waves in groups]
    pixels = right.shape[1] // 2
    wholes = []
    for high, low in halves:
        whole = jnp.dot(jnp.concatenate([high, low, high], axis=1), right, preferred_element_type=F32)
        wholes.append(
            [
                (whole[at : at + pixels, :pixels], whole[at : at + pixels, pixels:])
                for at in range(0, whole.shape[0], pixels)
            ]
        )
    return wholes


def times(one, two):
    return one[0] * two[0] - one[1] * two[1], one[0] * two[1] + one[1] * two[0]


def conj_times(one, two):
    return one[0] * two[0] + one[1] * two[1], one[0] * two[1] - one[1] * two[0]


def place(column, columns, pixels):
    base = jnp.minimum(column // pixels * pixels, columns - 2 * pixels)
    return pl.multiple_of(base, pixels), column - base


def cut(tile, column, pixels):
    base, shift = place(column, tile.shape[-1], pixels)
    rows = tile.shape[1]
    wide = tile[:, :, pl.ds(base, 2 * pixels)].reshape(-1, 2 * pixels)
    turned = pltpu.roll(wide, 2 * pixels - shift, 1)
    return turned[:, :pixels].reshape(-1, rows, pixels)


def rows_of(index, share):
    return pl.ds(pl.multiple_of(index * share, share), share)


def is_even(offsets, rows):
    return lax.rem(offsets[0, 0] // rows, 2) == 0


def pack_kernel(offsets, counts, measured, out):
    slots, _, pixels = measured.shape
    half = pixels // 2
    for slot in range(slots):
        live = jnp.where(slot < counts[0], 1.0, 0.0).astype(F32)
        for odd in range(2):
            row = slot * pixels + odd * half
            out[row : row + half] = measured[slot, pl.ds(odd, half, stride=2)] * live
        for entry in range(2):
            line = jnp.full((1, pixels), offsets[slot, entry], jnp.int32).astype(F32)
            row = slots * pixels + 2 * slot + entry
            out[row : row + 1] = line


def middle_kernel(pixels, target, tile, *outs):
    *parts, offsets = outs
    planes = tile.shape[0]
    for slot in range(offsets.shape[0]):
        for entry in range(2):
            line = target.shape[0] - 2 * offsets.shape[0] + 2 * slot + entry
            value = target[line : line + 1]
            offsets[slot, entry] = jnp.max(value).astype(jnp.int32)
    slot = 0
    for part in parts:
        for at in range(part.shape[0] // planes):
            part[at * planes : (at + 1) * planes] = cut(tile, offsets[slot, 1], pixels)
            slot += 1


def cut_kernel(pixels, chunks, own, far, tile, *outs):
    planes, rows, _ = tile.shape
    even = is_even(own, rows)
    for (first, size), near, cross in zip(chunks, outs[::2], outs[1::2], strict=True):
        for at in range(size):
            slot = first + at
            strip = at * planes
            near[strip : strip + planes] = cut(tile, jnp.where(even, own[slot, 1], far[slot, 1]), pixels)
            cross[strip : strip + planes] = cut(tile, jnp.where(even, far[slot, 1], own[slot, 1]), pixels)


def add_kernel(pixels, groups, own, middle, far, *refs):
    *parts, out = refs
    planes, rows, _ = out.shape
    even = is_even(own, rows)
    out[...] = jnp.zeros_like(out)
    lane = lax.broadcasted_iota(jnp.int32, (1, 1, pixels), 2)
    for (kind, first, size, unit), strips in zip(groups, parts):

        turned = []
        for at in range(size):
            slot = first + at
            if kind == "mid":
                column = middle[slot, 1]
            elif kind == "near":
                column = jnp.where(even, own[slot, 1], far[slot, 1])
            else:
                column = jnp.where(even, far[slot, 1], own[slot, 1])
            base, shift = place(column, out.shape[-1], pixels)
            part = strips[unit + at * planes : unit + (at + 1) * planes].reshape(-1, pixels)
            part = pltpu.roll(part, lax.rem(shift, pixels), 1).reshape(planes, rows, pixels)
            turned.append((base, shift, part))
        for base, shift, part in turned:
            out[:, :, pl.ds(base, pixels)] += jnp.where(lane >= shift, part, 0.0)
            beside = pl.ds(pl.multiple_of(base + pixels, pixels), pixels)
            out[:, :, beside] += jnp.where(lane < shift, part, 0.0)


def slot_kernel(first, size, earlier, own_offsets, *refs):
    offsets, mid, near, cross, target, probe, prop, tables, *refs = refs
    so_far, refs = (refs[0], refs[1:]) if first else (None, refs)
    earlier, refs = refs[:earlier], refs[earlier:]
    out_near, out_mid, out_cross, *shares = refs[:-5]
    window, patch, grads, exit_wave, far = refs[-5:]
    total = shares.pop()
    modes, _, pixels, _ = probe.shape
    planes, rows = mid.shape[0] // size, mid.shape[1]
    behind = 0
    for strips in earlier:
        out_near[behind : behind + strips.shape[0]] = strips[...]
        behind += strips.shape[0]
    even = is_even(own_offsets, rows)
    total[...] = so_far[...] if first else jnp.zeros_like(total)
    held = range(BATCH)

    def is_live(at):
        return jnp.max(target[pl.ds((first + at) * pixels, 8)]) > 0.0

    def leave(slots):
        for at in slots:
            for out, unit in ((out_near, behind), (out_mid, 0), (out_cross, 0)):
                out[pl.ds(unit + at * planes, planes)] = jnp.zeros((planes, rows, pixels), F32)

    def visit(slots):
        starts = [lax.rem(offsets[first + at, 0], rows) for at in slots]
        live = [jnp.where(is_live(at), 1.0, 0.0).astype(F32) for at in slots]
        for s, at in enumerate(slots):
            strip = pl.ds(at * planes, planes)
            window[:, :rows] = jnp.where(even, cross[strip], near[strip])
            window[:, rows : 2 * rows] = mid[strip]
            window[:, 2 * rows :] = jnp.where(even, near[strip], cross[strip])
            patch[s] = window[:, pl.ds(starts[s], pixels), :]
            total[2 * modes] += live[s] * (patch[s, 0] * patch[s, 0] + patch[s, 1] * patch[s, 1])
        all_modes = range(modes)
        groups = [
            [times((probe[m, 0], probe[m, 1]), (patch[s, 0], patch[s, 1])) for m in all_modes] for s in held
        ]
        groups = transform(tables, False, groups)
        groups = [[times((prop[0], prop[1]), wave) for wave in waves] for waves in groups]
        groups = transform(tables, True, groups)
        for s in held:
            for m in all_modes:
                exit_wave[s, m, 0], exit_wave[s, m, 1] = groups[s][m]
            groups[s] = [times(wave, (patch[s, 2], patch[s, 3])) for wave in groups[s]]
        groups = transform(tables, False, groups)
        for s, at in enumerate(slots):
            intensity = jnp.zeros((pixels, pixels), F32)
            for m in all_modes:
                wave = groups[s][m]
                far[s, m, 0], far[s, m, 1] = wave
                intensity = intensity + wave[0] * wave[0] + wave[1] * wave[1]
            misfit = 2.0 * live[s] * (intensity - target[pl.ds((first + at) * pixels, pixels)])
            groups[s] = [(misfit * far[s, m, 0], misfit * far[s, m, 1]) for m in all_modes]
        groups = transform(tables, True, groups)
        for s in held:
            grad_re, grad_im = jnp.zeros((pixels, pixels), F32), jnp.zeros((pixels, pixels), F32)
            for m in all_modes:
                re, im = conj_times((exit_wave[s, m, 0], exit_wave[s, m, 1]), groups[s][m])
                grad_re, grad_im = grad_re + re, grad_im + im
            grads[s, 2], grads[s, 3] = grad_re, grad_im
            groups[s] = [conj_times((patch[s, 2], patch[s, 3]), wave) for wave in groups[s]]
        groups = transform(tables, False, groups)
        groups = [[conj_times((prop[0], prop[1]), wave) for wave in waves] for waves in groups]
        groups = transform(tables, True, groups)
        for s in held:
            grad_re, grad_im = jnp.zeros((pixels, pixels), F32), jnp.zeros((pixels, pixels), F32)
            for m in all_modes:
                re, im = conj_times((patch[s, 0], patch[s, 1]), groups[s][m])
                total[2 * m] += re
                total[2 * m + 1] += im
                re, im = conj_times((probe[m, 0], probe[m, 1]), groups[s][m])
                grad_re, grad_im = grad_re + re, grad_im + im
            grads[s, 0], grads[s, 1] = grad_re, grad_im
        for s, at in enumerate(slots):
            window[...] = jnp.zeros_like(window)
            window[:, pl.ds(starts[s], pixels), :] = grads[s]
            strip = pl.ds(at * planes, planes)
            out_near[pl.ds(behind + at * planes, planes)] = jnp.where(even, window[:, 2 * rows :], window[:, :rows])
            out_mid[pl.ds(at * planes, planes)] = window[:, rows : 2 * rows]
            out_cross[strip] = jnp.where(even, window[:, :rows], window[:, 2 * rows :])

    def step(index, carry):
        slots = [index * BATCH + s for s in range(BATCH)]
        some = is_live(slots[0])
        pl.when(some)(lambda: visit(slots))
        pl.when(jnp.logical_not(some))(lambda: leave(slots))
        return carry

    lax.fori_loop(0, size // BATCH, step, 0)

    if shares:
        own, other = shares
        chips, _, share, _ = own.shape
        core = jnp.where(even, 0, 1)
        for chip in range(chips):
            for plane in range(2 * modes + 1):
                own[chip, plane] = total[plane, rows_of(2 * chip + core, share)]
                other[chip, plane] = total[plane, rows_of(2 * chip + 1 - core, share)]


def step_kernel(parts, out):
    summed = parts[0]
    for at in range(1, parts.shape[0]):
        summed = summed + parts[at]
    step = summed[:-1] / (summed[-1:] + 1.0)
    for at in range(out.shape[0]):
        out[at] = step


def order_kernel(rows, offsets, own, other, out):
    chips, _, share, _ = own.shape
    core = jnp.where(is_even(offsets, rows), 0, 1)
    for chip in range(chips):
        out[:, rows_of(2 * chip + core, share)] = own[chip]
        out[:, rows_of(2 * chip + 1 - core, share)] = other[chip]


def in_smem():
    return pl.BlockSpec(memory_space=pltpu.SMEM)


def in_vmem():
    return pl.BlockSpec(memory_space=pltpu.VMEM)


def local(object_slices, probe_modes, propagator_phase, measured, offsets, counts):
    slices, _, tile_rows, columns = object_slices.shape
    modes, _, pixels, _ = probe_modes.shape
    planes = 2 * slices
    peers = lax.axis_size(ROW)
    params = pltpu.CompilerParams(vmem_limit_bytes=VMEM_LIMIT)
    tile = object_slices.reshape(planes, tile_rows, columns)
    starts = [sum(CHUNKS[:i]) for i in range(len(CHUNKS))]

    pair = [(i, i ^ 1) for i in range(peers)]
    other_pair = [(i, (i - 1) % peers if i % 2 == 0 else (i + 1) % peers) for i in range(peers)]
    far = shifted(offsets, ROW, 2)

    chunks = list(zip(starts, CHUNKS))
    target = pl.pallas_call(
        pack_kernel,
        out_shape=jax.ShapeDtypeStruct((measured.shape[0] * pixels + offsets.size, pixels), F32),
        in_specs=[in_smem()] * 2 + [in_vmem()],
        out_specs=in_vmem(),
        compiler_params=params,
        cost_estimate=pl.CostEstimate(flops=0, bytes_accessed=1 << 20, transcendentals=0),
    )(offsets, counts, measured)
    far, target = lax.optimization_barrier((far, target))
    target = shifted(target, ROW, 1)

    def units(count):
        return jax.ShapeDtypeStruct((count, tile_rows, pixels), F32)

    def strips(chunks, far):
        shapes = [units(size * planes) for _, size in chunks for _ in range(2)]
        outs = pl.pallas_call(
            functools.partial(cut_kernel, pixels, chunks),
            out_shape=shapes,
            in_specs=[in_smem()] * 2 + [in_vmem()],
            out_specs=[in_vmem()] * len(shapes),
            compiler_params=params,
            cost_estimate=pl.CostEstimate(flops=0, bytes_accessed=4 << 20, transcendentals=0),
        )(offsets, far, tile)
        return list(zip(outs[::2], outs[1::2]))

    def swapped(to_near, to_cross):
        return lax.ppermute(to_near, ROW, pair), lax.ppermute(to_cross, ROW, other_pair)

    far_later, target = lax.optimization_barrier((far, target))
    waiting = strips(chunks[:1], far) + strips(chunks[1:], far_later)
    *middles, middle = pl.pallas_call(
        functools.partial(middle_kernel, pixels),
        out_shape=[units(size * planes) for size in CHUNKS] + [jax.ShapeDtypeStruct(offsets.shape, jnp.int32)],
        in_specs=[in_vmem()] * 2,
        out_specs=[in_vmem()] * len(CHUNKS) + [in_smem()],
        compiler_params=params,
        cost_estimate=pl.CostEstimate(flops=0, bytes_accessed=4 << 20, transcendentals=0),
    )(target, tile)
    arrived = [swapped(*waiting[0])]
    if len(waiting) > 1:
        arrived[0], following, middles = lax.optimization_barrier((arrived[0], waiting[1], middles))
        arrived.append(swapped(*following))
    phase = jnp.concatenate([propagator_phase[0::2], propagator_phase[1::2]], axis=0)
    prop = jnp.stack([jnp.cos(phase), jnp.sin(phase)])
    tables = jnp.asarray(fourier_tables(pixels))

    share = pixels // peers
    total = ()
    mid, back, groups, to_pair = [], [], [], []
    for index, (first, size) in enumerate(chunks):
        sums = jax.ShapeDtypeStruct((2 * modes + 1, pixels, pixels), F32)
        part = jax.ShapeDtypeStruct((peers // 2, 2 * modes + 1, share, pixels), F32)
        last = index == len(chunks) - 1
        message = units(size * planes)
        field = pltpu.VMEM((BATCH, planes, pixels, pixels), F32)
        kept = pltpu.VMEM((BATCH, modes, 2, pixels, pixels), F32)
        results = [part, part] if last else [sums]
        earlier = to_pair if last else []
        near_units = units(sum(CHUNKS) * planes) if last else message
        to_near, to_mid, to_cross, *total = pl.pallas_call(
            functools.partial(slot_kernel, first, size, len(earlier)),
            out_shape=[near_units, message, message] + results,
            in_specs=[in_smem()] * 2 + [in_vmem()] * (7 + len(total) + len(earlier)),
            out_specs=[in_vmem()] * (3 + len(results)),
            scratch_shapes=([pltpu.VMEM(sums.shape, F32)] if last else [])
            + [pltpu.VMEM((planes, 3 * tile_rows, pixels), F32), field, field, kept, kept],
            compiler_params=params,
            cost_estimate=pl.CostEstimate(
                flops=size * 6 * modes * 3 * 16 * pixels**3, bytes_accessed=8 << 20, transcendentals=0
            ),
        )(offsets, middle, middles[index], *arrived[index], target, probe_modes, prop, tables, *total, *earlier)
        to_pair.append(to_near)
        mid.append(to_mid)
        back.append(lax.ppermute(to_cross, ROW, other_pair))
        groups += [("mid", first, size, 0), ("cross", first, size, 0), ("near", first, size, first * planes)]

    def added(groups, strips):
        return pl.pallas_call(
            functools.partial(add_kernel, pixels, groups),
            out_shape=jax.ShapeDtypeStruct(tile.shape, F32),
            in_specs=[in_smem()] * 3 + [in_vmem()] * len(strips),
            out_specs=in_vmem(),
            compiler_params=params,
            cost_estimate=pl.CostEstimate(flops=0, bytes_accessed=5 << 20, transcendentals=0),
        )(offsets, middle, far, *strips)

    own, other = total
    own, other, back[:-1] = lax.optimization_barrier((own, other, back[:-1]))
    other, to_pair = lax.optimization_barrier((lax.ppermute(other, ROW, pair), to_pair[-1]))
    from_pair = lax.ppermute(to_pair, ROW, pair)
    both = own + other
    parts = lax.all_to_all(both, "chip", 0, 0)
    spread = pl.pallas_call(
        step_kernel,
        out_shape=jax.ShapeDtypeStruct((peers // 2, 2 * modes, share, pixels), F32),
        in_specs=[in_vmem()],
        out_specs=in_vmem(),
        compiler_params=params,
    )(parts)
    strips = [part for parts in zip(mid, back, [from_pair] * len(mid)) for part in parts]
    spread, strips = lax.optimization_barrier((spread, strips))
    gathered = lax.all_to_all(spread, "chip", 0, 0)
    object_grad = added(groups, strips)
    gathered, object_grad = lax.optimization_barrier((gathered, object_grad))
    object_grad = object_grad.reshape(object_slices.shape)

    probe_step = pl.pallas_call(
        functools.partial(order_kernel, tile_rows),
        out_shape=jax.ShapeDtypeStruct((2 * modes, pixels, pixels), F32),
        in_specs=[in_smem()] + [in_vmem()] * 2,
        out_specs=in_vmem(),
        compiler_params=params,
    )(offsets, gathered, lax.ppermute(gathered, ROW, pair)).reshape(probe_modes.shape)
    return (object_grad, probe_step)


def solution(mesh):
    groups, peers = mesh.shape["grp"], mesh.shape["row"]
    split = jax.sharding.Mesh(mesh.devices.reshape(groups, peers // 2, 2), ("grp",) + ROW)
    everywhere = ("grp",) + ROW
    in_specs = (
        P(None, None, everywhere, None),
        P("grp", None, None, None),
        P(),
        P(everywhere, None, None),
        P(everywhere, None),
        P(everywhere),
    )
    out_specs = (P(None, None, everywhere, None), P("grp", None, None, None))
    return jax.shard_map(local, mesh=split, in_specs=in_specs, out_specs=out_specs, check_vma=False)
```

```python
import functools

import jax
import jax.numpy as jnp
import numpy as np
from jax import lax
from jax.experimental import pallas as pl
from jax.experimental.pallas import tpu as pltpu
from jax.sharding import PartitionSpec as P

CHUNKS = (4, 4)
BATCH = 4
VMEM_LIMIT = 32 * 1024 * 1024
ROW = ("chip", "core")
F32 = jnp.float32
BF16 = jnp.bfloat16


def shifted(array, axis, by):
    peers = lax.axis_size(axis)
    return lax.ppermute(array, axis, [(i, (i + by) % peers) for i in range(peers)])


def real_form(matrix):
    return np.block([[matrix.real, -matrix.imag], [matrix.imag, matrix.real]]).astype(np.float32)


def two_pieces(matrix):
    high = matrix.astype(BF16)
    return high, (matrix - high.astype(np.float32)).astype(BF16)


def fourier_tables(pixels):
    half = pixels // 2
    kept, rows = np.arange(half)[:, None], np.arange(half)[None, :]
    lefts = []
    for odd in range(2):
        turns = (2 * kept + odd) * rows % pixels / pixels
        part = real_form(np.exp(-2j * np.pi * turns) / np.sqrt(pixels))
        for table in (part, part.T):
            high, low = two_pieces(table)
            lefts.append(np.block([[high, high], [low, np.zeros_like(low)]]))
    indices = np.arange(pixels)
    whole = np.exp(-2j * np.pi * (indices[:, None] * indices[None, :] % pixels) / pixels) / np.sqrt(pixels)
    rights = []
    for table in (real_form(whole).T, real_form(whole)):
        rights += two_pieces(table)
    return np.stack(lefts + rights)


def pieces(array):
    high = array.astype(BF16)
    return high, (array - high.astype(F32)).astype(BF16)


def from_left(tables, conj, waves):
    half = waves[0][0].shape[0] // 2
    pixels = 2 * half
    sides = []
    for odd in range(2):
        parts = []
        for wave in waves:
            if conj:
                parts.append(jnp.concatenate([part[odd * half : (odd + 1) * half] for part in wave], axis=0))
            elif odd:
                parts.append(jnp.concatenate([part[:half] - part[half:] for part in wave], axis=0))
            else:
                parts.append(jnp.concatenate([part[:half] + part[half:] for part in wave], axis=0))
        stacked = jnp.concatenate(pieces(jnp.concatenate(parts, axis=1)), axis=0)
        product = jnp.dot(tables[2 * odd + conj], stacked, preferred_element_type=F32)
        sides.append(product[:pixels] + product[pixels:])
    if conj:
        sides = [sides[0] + sides[1], sides[0] - sides[1]]
    turned = []
    for at in range(0, len(waves) * pixels, pixels):
        re = jnp.concatenate([side[:half, at : at + pixels] for side in sides], axis=0)
        im = jnp.concatenate([side[half:, at : at + pixels] for side in sides], axis=0)
        turned.append(jnp.concatenate([re, im], axis=1))
    return jnp.concatenate(turned, axis=0)


def transform(tables, conj, groups):
    right_high, right_low = tables[4 + 2 * conj], tables[5 + 2 * conj]
    right = jnp.concatenate([right_high, right_high, right_low], axis=0)
    halves = [pieces(from_left(tables, conj, waves)) for waves in groups]
    pixels = right.shape[1] // 2
    wholes = []
    for high, low in halves:
        whole = jnp.dot(jnp.concatenate([high, low, high], axis=1), right, preferred_element_type=F32)
        wholes.append(
            [
                (whole[at : at + pixels, :pixels], whole[at : at + pixels, pixels:])
                for at in range(0, whole.shape[0], pixels)
            ]
        )
    return wholes


def times(one, two):
    return one[0] * two[0] - one[1] * two[1], one[0] * two[1] + one[1] * two[0]


def conj_times(one, two):
    return one[0] * two[0] + one[1] * two[1], one[0] * two[1] - one[1] * two[0]


def place(column, columns, pixels):
    base = jnp.minimum(column // pixels * pixels, columns - 2 * pixels)
    return pl.multiple_of(base, pixels), column - base


def cut(tile, column, pixels):
    base, shift = place(column, tile.shape[-1], pixels)
    rows = tile.shape[1]
    wide = tile[:, :, pl.ds(base, 2 * pixels)].reshape(-1, 2 * pixels)
    turned = pltpu.roll(wide, 2 * pixels - shift, 1)
    return turned[:, :pixels].reshape(-1, rows, pixels)


def rows_of(index, share):
    return pl.ds(pl.multiple_of(index * share, share), share)


def is_even(offsets, rows):
    return lax.rem(offsets[0, 0] // rows, 2) == 0


def pack_kernel(offsets, counts, measured, out):
    slots, _, pixels = measured.shape
    half = pixels // 2
    for slot in range(slots):
        live = jnp.where(slot < counts[0], 1.0, 0.0).astype(F32)
        for odd in range(2):
            row = slot * pixels + odd * half
            out[row : row + half] = measured[slot, pl.ds(odd, half, stride=2)] * live
        for entry in range(2):
            line = jnp.full((1, pixels), offsets[slot, entry], jnp.int32).astype(F32)
            row = slots * pixels + 2 * slot + entry
            out[row : row + 1] = line


def middle_kernel(pixels, target, tile, *outs):
    *parts, offsets = outs
    planes = tile.shape[0]
    for slot in range(offsets.shape[0]):
        for entry in range(2):
            line = target.shape[0] - 2 * offsets.shape[0] + 2 * slot + entry
            value = target[line : line + 1]
            offsets[slot, entry] = jnp.max(value).astype(jnp.int32)
    slot = 0
    for part in parts:
        for at in range(part.shape[0] // planes):
            part[at * planes : (at + 1) * planes] = cut(tile, offsets[slot, 1], pixels)
            slot += 1


def cut_kernel(pixels, chunks, own, far, tile, *outs):
    planes, rows, _ = tile.shape
    even = is_even(own, rows)
    for (first, size), near, cross in zip(chunks, outs[::2], outs[1::2], strict=True):
        for at in range(size):
            slot = first + at
            strip = at * planes
            near[strip : strip + planes] = cut(tile, jnp.where(even, own[slot, 1], far[slot, 1]), pixels)
            cross[strip : strip + planes] = cut(tile, jnp.where(even, far[slot, 1], own[slot, 1]), pixels)


def add_kernel(pixels, groups, own, middle, far, *refs):
    *parts, out = refs
    planes, rows, _ = out.shape
    even = is_even(own, rows)
    out[...] = jnp.zeros_like(out)
    lane = lax.broadcasted_iota(jnp.int32, (1, 1, pixels), 2)
    for (kind, first, size, unit), strips in zip(groups, parts):

        turned = []
        for at in range(size):
            slot = first + at
            if kind == "mid":
                column = middle[slot, 1]
            elif kind == "near":
                column = jnp.where(even, own[slot, 1], far[slot, 1])
            else:
                column = jnp.where(even, far[slot, 1], own[slot, 1])
            base, shift = place(column, out.shape[-1], pixels)
            part = strips[unit + at * planes : unit + (at + 1) * planes].reshape(-1, pixels)
            part = pltpu.roll(part, lax.rem(shift, pixels), 1).reshape(planes, rows, pixels)
            turned.append((base, shift, part))
        for base, shift, part in turned:
            out[:, :, pl.ds(base, pixels)] += jnp.where(lane >= shift, part, 0.0)
            beside = pl.ds(pl.multiple_of(base + pixels, pixels), pixels)
            out[:, :, beside] += jnp.where(lane < shift, part, 0.0)


def slot_kernel(first, size, earlier, own_offsets, *refs):
    offsets, mid, near, cross, target, probe, prop, tables, *refs = refs
    so_far, refs = (refs[0], refs[1:]) if first else (None, refs)
    earlier, refs = refs[:earlier], refs[earlier:]
    out_near, out_mid, out_cross, *shares = refs[:-5]
    window, patch, grads, exit_wave, far = refs[-5:]
    total = shares.pop()
    modes, _, pixels, _ = probe.shape
    planes, rows = mid.shape[0] // size, mid.shape[1]
    behind = 0
    for strips in earlier:
        out_near[behind : behind + strips.shape[0]] = strips[...]
        behind += strips.shape[0]
    even = is_even(own_offsets, rows)
    total[...] = so_far[...] if first else jnp.zeros_like(total)
    held = range(BATCH)

    def is_live(at):
        return jnp.max(target[pl.ds((first + at) * pixels, 8)]) > 0.0

    def leave(slots):
        for at in slots:
            for out, unit in ((out_near, behind), (out_mid, 0), (out_cross, 0)):
                out[pl.ds(unit + at * planes, planes)] = jnp.zeros((planes, rows, pixels), F32)

    def visit(slots):
        starts = [lax.rem(offsets[first + at, 0], rows) for at in slots]
        live = [jnp.where(is_live(at), 1.0, 0.0).astype(F32) for at in slots]
        for s, at in enumerate(slots):
            strip = pl.ds(at * planes, planes)
            window[:, :rows] = jnp.where(even, cross[strip], near[strip])
            window[:, rows : 2 * rows] = mid[strip]
            window[:, 2 * rows :] = jnp.where(even, near[strip], cross[strip])
            patch[s] = window[:, pl.ds(starts[s], pixels), :]
            total[2 * modes] += live[s] * (patch[s, 0] * patch[s, 0] + patch[s, 1] * patch[s, 1])
        all_modes = range(modes)
        groups = [
            [times((probe[m, 0], probe[m, 1]), (patch[s, 0], patch[s, 1])) for m in all_modes] for s in held
        ]
        groups = transform(tables, False, groups)
        groups = [[times((prop[0], prop[1]), wave) for wave in waves] for waves in groups]
        groups = transform(tables, True, groups)
        for s in held:
            for m in all_modes:
                exit_wave[s, m, 0], exit_wave[s, m, 1] = groups[s][m]
            groups[s] = [times(wave, (patch[s, 2], patch[s, 3])) for wave in groups[s]]
        groups = transform(tables, False, groups)
        for s, at in enumerate(slots):
            intensity = jnp.zeros((pixels, pixels), F32)
            for m in all_modes:
                wave = groups[s][m]
                far[s, m, 0], far[s, m, 1] = wave
                intensity = intensity + wave[0] * wave[0] + wave[1] * wave[1]
            misfit = 2.0 * live[s] * (intensity - target[pl.ds((first + at) * pixels, pixels)])
            groups[s] = [(misfit * far[s, m, 0], misfit * far[s, m, 1]) for m in all_modes]
        groups = transform(tables, True, groups)
        for s in held:
            grad_re, grad_im = jnp.zeros((pixels, pixels), F32), jnp.zeros((pixels, pixels), F32)
            for m in all_modes:
                re, im = conj_times((exit_wave[s, m, 0], exit_wave[s, m, 1]), groups[s][m])
                grad_re, grad_im = grad_re + re, grad_im + im
            grads[s, 2], grads[s, 3] = grad_re, grad_im
            groups[s] = [conj_times((patch[s, 2], patch[s, 3]), wave) for wave in groups[s]]
        groups = transform(tables, False, groups)
        groups = [[conj_times((prop[0], prop[1]), wave) for wave in waves] for waves in groups]
        groups = transform(tables, True, groups)
        for s in held:
            grad_re, grad_im = jnp.zeros((pixels, pixels), F32), jnp.zeros((pixels, pixels), F32)
            for m in all_modes:
                re, im = conj_times((patch[s, 0], patch[s, 1]), groups[s][m])
                total[2 * m] += re
                total[2 * m + 1] += im
                re, im = conj_times((probe[m, 0], probe[m, 1]), groups[s][m])
                grad_re, grad_im = grad_re + re, grad_im + im
            grads[s, 0], grads[s, 1] = grad_re, grad_im
        for s, at in enumerate(slots):
            window[...] = jnp.zeros_like(window)
            window[:, pl.ds(starts[s], pixels), :] = grads[s]
            strip = pl.ds(at * planes, planes)
            out_near[pl.ds(behind + at * planes, planes)] = jnp.where(even, window[:, 2 * rows :], window[:, :rows])
            out_mid[pl.ds(at * planes, planes)] = window[:, rows : 2 * rows]
            out_cross[strip] = jnp.where(even, window[:, :rows], window[:, 2 * rows :])

    def step(index, carry):
        slots = [index * BATCH + s for s in range(BATCH)]
        some = is_live(slots[0])
        pl.when(some)(lambda: visit(slots))
        pl.when(jnp.logical_not(some))(lambda: leave(slots))
        return carry

    lax.fori_loop(0, size // BATCH, step, 0)

    if shares:
        own, other = shares
        chips, _, share, _ = own.shape
        core = jnp.where(even, 0, 1)
        for chip in range(chips):
            for plane in range(2 * modes + 1):
                own[chip, plane] = total[plane, rows_of(2 * chip + core, share)]
                other[chip, plane] = total[plane, rows_of(2 * chip + 1 - core, share)]


def step_kernel(parts, out):
    summed = parts[0]
    for at in range(1, parts.shape[0]):
        summed = summed + parts[at]
    step = summed[:-1] / (summed[-1:] + 1.0)
    for at in range(out.shape[0]):
        out[at] = step


def order_kernel(rows, offsets, own, other, out):
    chips, _, share, _ = own.shape
    core = jnp.where(is_even(offsets, rows), 0, 1)
    for chip in range(chips):
        out[:, rows_of(2 * chip + core, share)] = own[chip]
        out[:, rows_of(2 * chip + 1 - core, share)] = other[chip]


def in_smem():
    return pl.BlockSpec(memory_space=pltpu.SMEM)


def in_vmem():
    return pl.BlockSpec(memory_space=pltpu.VMEM)


def local(object_slices, probe_modes, propagator_phase, measured, offsets, counts):
    slices, _, tile_rows, columns = object_slices.shape
    modes, _, pixels, _ = probe_modes.shape
    planes = 2 * slices
    peers = lax.axis_size(ROW)
    params = pltpu.CompilerParams(vmem_limit_bytes=VMEM_LIMIT)
    tile = object_slices.reshape(planes, tile_rows, columns)
    starts = [sum(CHUNKS[:i]) for i in range(len(CHUNKS))]

    pair = [(i, i ^ 1) for i in range(peers)]
    other_pair = [(i, (i - 1) % peers if i % 2 == 0 else (i + 1) % peers) for i in range(peers)]
    far = shifted(offsets, ROW, 2)

    chunks = list(zip(starts, CHUNKS))
    target = pl.pallas_call(
        pack_kernel,
        out_shape=jax.ShapeDtypeStruct((measured.shape[0] * pixels + offsets.size, pixels), F32),
        in_specs=[in_smem()] * 2 + [in_vmem()],
        out_specs=in_vmem(),
        compiler_params=params,
        cost_estimate=pl.CostEstimate(flops=0, bytes_accessed=1 << 20, transcendentals=0),
    )(offsets, counts, measured)
    far, target = lax.optimization_barrier((far, target))
    target = shifted(target, ROW, 1)

    def units(count):
        return jax.ShapeDtypeStruct((count, tile_rows, pixels), F32)

    def strips(chunks, far):
        shapes = [units(size * planes) for _, size in chunks for _ in range(2)]
        outs = pl.pallas_call(
            functools.partial(cut_kernel, pixels, chunks),
            out_shape=shapes,
            in_specs=[in_smem()] * 2 + [in_vmem()],
            out_specs=[in_vmem()] * len(shapes),
            compiler_params=params,
            cost_estimate=pl.CostEstimate(flops=0, bytes_accessed=4 << 20, transcendentals=0),
        )(offsets, far, tile)
        return list(zip(outs[::2], outs[1::2]))

    def swapped(to_near, to_cross):
        return lax.ppermute(to_near, ROW, pair), lax.ppermute(to_cross, ROW, other_pair)

    far_later, target = lax.optimization_barrier((far, target))
    waiting = strips(chunks[:1], far) + strips(chunks[1:], far_later)
    *middles, middle = pl.pallas_call(
        functools.partial(middle_kernel, pixels),
        out_shape=[units(size * planes) for size in CHUNKS] + [jax.ShapeDtypeStruct(offsets.shape, jnp.int32)],
        in_specs=[in_vmem()] * 2,
        out_specs=[in_vmem()] * len(CHUNKS) + [in_smem()],
        compiler_params=params,
        cost_estimate=pl.CostEstimate(flops=0, bytes_accessed=4 << 20, transcendentals=0),
    )(target, tile)
    arrived = [swapped(*waiting[0])]
    if len(waiting) > 1:
        arrived[0], following, middles = lax.optimization_barrier((arrived[0], waiting[1], middles))
        arrived.append(swapped(*following))
    phase = jnp.concatenate([propagator_phase[0::2], propagator_phase[1::2]], axis=0)
    prop = jnp.stack([jnp.cos(phase), jnp.sin(phase)])
    tables = jnp.asarray(fourier_tables(pixels))

    share = pixels // peers
    total = ()
    mid, back, groups, to_pair = [], [], [], []
    for index, (first, size) in enumerate(chunks):
        sums = jax.ShapeDtypeStruct((2 * modes + 1, pixels, pixels), F32)
        part = jax.ShapeDtypeStruct((peers // 2, 2 * modes + 1, share, pixels), F32)
        last = index == len(chunks) - 1
        message = units(size * planes)
        field = pltpu.VMEM((BATCH, planes, pixels, pixels), F32)
        kept = pltpu.VMEM((BATCH, modes, 2, pixels, pixels), F32)
        results = [part, part] if last else [sums]
        earlier = to_pair if last else []
        near_units = units(sum(CHUNKS) * planes) if last else message
        to_near, to_mid, to_cross, *total = pl.pallas_call(
            functools.partial(slot_kernel, first, size, len(earlier)),
            out_shape=[near_units, message, message] + results,
            in_specs=[in_smem()] * 2 + [in_vmem()] * (7 + len(total) + len(earlier)),
            out_specs=[in_vmem()] * (3 + len(results)),
            scratch_shapes=([pltpu.VMEM(sums.shape, F32)] if last else [])
            + [pltpu.VMEM((planes, 3 * tile_rows, pixels), F32), field, field, kept, kept],
            compiler_params=params,
            cost_estimate=pl.CostEstimate(
                flops=size * 6 * modes * 3 * 16 * pixels**3, bytes_accessed=8 << 20, transcendentals=0
            ),
        )(offsets, middle, middles[index], *arrived[index], target, probe_modes, prop, tables, *total, *earlier)
        to_pair.append(to_near)
        mid.append(to_mid)
        back.append(lax.ppermute(to_cross, ROW, other_pair))
        groups += [("mid", first, size, 0), ("cross", first, size, 0), ("near", first, size, first * planes)]

    def added(groups, strips):
        return pl.pallas_call(
            functools.partial(add_kernel, pixels, groups),
            out_shape=jax.ShapeDtypeStruct(tile.shape, F32),
            in_specs=[in_smem()] * 3 + [in_vmem()] * len(strips),
            out_specs=in_vmem(),
            compiler_params=params,
            cost_estimate=pl.CostEstimate(flops=0, bytes_accessed=5 << 20, transcendentals=0),
        )(offsets, middle, far, *strips)

    own, other = total
    own, other, back[:-1] = lax.optimization_barrier((own, other, back[:-1]))
    other, to_pair = lax.optimization_barrier((lax.ppermute(other, ROW, pair), to_pair[-1]))
    from_pair = lax.ppermute(to_pair, ROW, pair)
    both = own + other
    parts = lax.all_to_all(both, "chip", 0, 0)
    spread = pl.pallas_call(
        step_kernel,
        out_shape=jax.ShapeDtypeStruct((peers // 2, 2 * modes, share, pixels), F32),
        in_specs=[in_vmem()],
        out_specs=in_vmem(),
        compiler_params=params,
    )(parts)
    spread, back = lax.optimization_barrier((spread, back))
    strips = [part for parts in zip(mid, back, [from_pair] * len(mid)) for part in parts]
    gathered = lax.all_to_all(spread, "chip", 0, 0)
    object_grad = added(groups, strips)
    gathered, object_grad = lax.optimization_barrier((gathered, object_grad))
    object_grad = object_grad.reshape(object_slices.shape)

    probe_step = pl.pallas_call(
        functools.partial(order_kernel, tile_rows),
        out_shape=jax.ShapeDtypeStruct((2 * modes, pixels, pixels), F32),
        in_specs=[in_smem()] + [in_vmem()] * 2,
        out_specs=in_vmem(),
        compiler_params=params,
    )(offsets, gathered, lax.ppermute(gathered, ROW, pair)).reshape(probe_modes.shape)
    return (object_grad, probe_step)


def solution(mesh):
    groups, peers = mesh.shape["grp"], mesh.shape["row"]
    split = jax.sharding.Mesh(mesh.devices.reshape(groups, peers // 2, 2), ("grp",) + ROW)
    everywhere = ("grp",) + ROW
    in_specs = (
        P(None, None, everywhere, None),
        P("grp", None, None, None),
        P(),
        P(everywhere, None, None),
        P(everywhere, None),
        P(everywhere),
    )
    out_specs = (P(None, None, everywhere, None), P("grp", None, None, None))
    return jax.shard_map(local, mesh=split, in_specs=in_specs, out_specs=out_specs, check_vma=False)
```
